32 devices in a mesh: rows: 8 (over z, y), cols: 4 (over x, core).
Axes of the slice: x: 2, y: 2, z: 4, core: 2. Of those that a mesh axis runs over, the one named last changes fastest.
Arguments:
- pin_features: bfloat16 [8192, 1024], P('rows', 'cols'), may hold values from -6 to 6
- board_features: bfloat16 [8192, 512], P('rows', 'cols'), may hold values from -6 to 6
- is_board: int32 [8192], P('rows'), may hold values 0 or 1
- neighbours: int32 [8192, 50], P('rows'), may hold values from 0 to 8191
- present: int32 [8192, 50], P('rows'), may hold values from 0 to 1, as said below
- importance: float32 [8192, 50], P('rows')
- proj_weight: bfloat16 [512, 1024], P(None, 'cols'), may hold values from -0.25 to 0.25
- proj_bias: float32 [1024], P('cols'), may hold values from -3 to 3
- q_weight: bfloat16 [1024, 1024], P(None, 'cols'), may hold values from -0.1875 to 0.1875
- q_bias: float32 [1024], P('cols'), may hold values from -3 to 3
- w_weight: bfloat16 [2048, 1024], P(None, 'cols'), may hold values from -0.125 to 0.125
- w_bias: float32 [1024], P('cols'), may hold values from -3 to 3
- cotangent: bfloat16 [8192, 1024], P('rows', 'cols'), may hold values from -6 to 6
Outputs:
- embeddings: bfloat16 [8192, 1024], P('rows', 'cols')
- grad_pin: float32 [8192, 1024], P('rows', 'cols')
- grad_board: float32 [8192, 512], P('rows', 'cols')
- grad_proj: float32 [512, 1024], P('rows', 'cols')
- grad_proj_bias: float32 [1024], P('cols')
- grad_q: float32 [1024, 1024], P('rows', 'cols')
- grad_q_bias: float32 [1024], P('cols')
- grad_w: float32 [2048, 1024], P('rows', 'cols')
- grad_w_bias: float32 [1024], P('cols')
- mean_count: float32 [], replicated
- mean_weight: float32 [], replicated
The draws below stay inside these ranges and needn't reach their ends.
Inputs may be any that keep to these rules, and one draw needn't show every extreme that they name: `present`: each node has 5 to 50 filled slots, some node exactly 5 and some exactly 50.
All inputs are finite; a program needn't handle non-finite values. No bound on the sum of `is_board` on one device may be relied on, other than what follows from the above.
Results may differ from the reference program's by a relative error of at most 0.018.
Values may be sent and summed in bfloat16 or wider, within the bound.
A program may use at most 128 MiB of HBM per device.

```python
import math
import jax
import jax.numpy as jnp
from jax import lax

D = 1024
DB = 512
SLOTS = 50
NODES_DEV = 1024
NODES = 8192


def draw_present(key, part):
    first, second = jax.random.split(jax.random.fold_in(key, 11))
    nodes = jnp.arange(NODES, dtype=jnp.int32)
    blocks_all = NODES // NODES_DEV
    span = 1 + 45 * (nodes // NODES_DEV + 1) // blocks_all
    count = 5 + jax.random.randint(first, (NODES,), 0, 1048576) % span
    count = jnp.where(nodes == NODES - 1, 50, jnp.where(nodes == 0, 5, count))
    scores = jax.random.randint(second, (NODES, SLOTS), 0, 1048576)
    order = jnp.argsort(scores, axis=1, stable=True)
    ranks = jnp.argsort(order, axis=1, stable=True)
    return (ranks < count[:, None]).astype(jnp.int32)


def draw_importance(key, part):
    first = jax.random.fold_in(key, 23)
    nodes = jnp.arange(NODES)
    blocks_all = NODES // NODES_DEV
    factor = 1.0 + 2.0 * (nodes // NODES_DEV).astype(jnp.float32) / max(blocks_all - 1, 1)
    base = jnp.exp(jax.random.uniform(first, (NODES, SLOTS), jnp.float32, -1.386, 1.386))
    return base * factor[:, None]


def place_ends(drawn, own_key, smallest, top_value):
    place = [jax.random.randint(jax.random.fold_in(own_key, axis), (), 0, length) for axis, length in enumerate(drawn.shape)]
    main_axis = drawn.shape.index(max(drawn.shape))
    next_to = place[:main_axis] + [(place[main_axis] + 1) % drawn.shape[main_axis]] + place[main_axis + 1:]
    return drawn.at[tuple(place)].set(smallest).at[tuple(next_to)].set(top_value)


def levels(stream_key, extent, cuts, least, largest):
    def one(axis_at, blocks):
        heights = jax.random.uniform(jax.random.fold_in(jax.random.fold_in(stream_key, 6), axis_at), (blocks,), jnp.float32, least / len(cuts), largest / len(cuts))
        return jnp.repeat(jnp.exp(heights), extent[axis_at] // blocks).reshape((-1,) + (1,) * (len(extent) - axis_at - 1))

    factor_of = one(*cuts[0])
    for cut in cuts[1:]:
        factor_of = factor_of * one(*cut)
    return factor_of


def normal_values(rng, dims, deviation, reach, pieces=(), kind=jnp.bfloat16):
    entries = deviation * jax.random.normal(rng, dims, jnp.float32)
    if pieces:
        entries = entries * levels(rng, dims, pieces, -0.22, 0.18)
    return jnp.clip(entries, -reach, reach).astype(kind)


def setup_inputs(seed: int = 0) -> dict:
    streams_of = jax.random.split(jax.random.key(seed), 14)
    pin_features = normal_values(streams_of[0], (NODES, D), 1.0, 6.0, ((0, 8), (1, 4)))
    board_features = normal_values(streams_of[1], (NODES, DB), 1.0, 6.0, ((0, 8), (1, 4)))
    is_board = place_ends((jax.random.randint(streams_of[2], (NODES,), 0, 2) < 1).astype(jnp.int32), jax.random.fold_in(streams_of[2], 1), 0, 1)
    neighbours = place_ends(jax.random.randint(streams_of[3], (NODES, SLOTS), 0, NODES), jax.random.fold_in(streams_of[3], 1), 0, NODES - 1).astype(jnp.int32)
    present = draw_present(jax.random.fold_in(streams_of[13], 71), 0)
    importance = draw_importance(jax.random.fold_in(streams_of[13], 71), 0)
    proj_weight = normal_values(streams_of[6], (DB, D), DB ** -0.5, 0.25, ((1, 4),))
    proj_bias = normal_values(streams_of[7], (D,), 0.5, 3.0, ((0, 4),), jnp.float32)
    q_weight = normal_values(streams_of[8], (D, D), D ** -0.5, 0.1875, ((1, 4),))
    q_bias = normal_values(streams_of[9], (D,), 0.5, 3.0, ((0, 4),), jnp.float32)
    w_weight = normal_values(streams_of[10], (2 * D, D), (2 * D) ** -0.5, 0.125, ((1, 4),))
    w_bias = normal_values(streams_of[11], (D,), 0.5, 3.0, ((0, 4),), jnp.float32)
    cotangent = normal_values(streams_of[12], (NODES, D), 1.0, 6.0, ((0, 8), (1, 4)))
    return dict(pin_features=pin_features, board_features=board_features, is_board=is_board, neighbours=neighbours, present=present, importance=importance, proj_weight=proj_weight, proj_bias=proj_bias, q_weight=q_weight, q_bias=q_bias, w_weight=w_weight, w_bias=w_bias, cotangent=cotangent)


@jax.custom_vjp
def low(v):
    return lax.optimization_barrier(v.astype(jnp.bfloat16)).astype(jnp.float32)

@jax.custom_vjp
def low_back(v):
    return v

def low_keep(v):
    return (low(v), None)

def low_pass(kept, grad):
    return (grad,)

def back_keep(v):
    return (v, None)

def back_low(kept, grad):
    return (low(grad),)
low.defvjp(low_keep, low_pass)
low_back.defvjp(back_keep, back_low)
HI = lax.Precision.HIGHEST

def mat(a, b):
    return jnp.dot(a, b, precision=HI, preferred_element_type=jnp.float32)

def reference(pin_features, board_features, is_board, neighbours, present, importance, proj_weight, proj_bias, q_weight, q_bias, w_weight, w_bias, cotangent):
    filled = present.astype(jnp.float32) * importance
    alpha = filled / lax.optimization_barrier(jnp.sum(filled, axis=1, keepdims=True))
    board_mask = (is_board == 1)[:, None]
    block_rows = math.gcd(NODES, 256)
    blocks = NODES // block_rows
    idx_blocks = neighbours.reshape(blocks, block_rows, SLOTS)
    alpha_blocks = alpha.reshape(blocks, block_rows, SLOTS)

    def forward(pin, board, pw, pb, qw, qb, ww, wb):
        board_proj = mat(board, pw) + pb
        h = low(jnp.where(board_mask, low_back(board_proj), pin))
        v = low_back(mat(h, qw) + qb)
        message = low(jax.nn.silu(v))

        def one_block(pair):
            return lax.optimization_barrier(jnp.sum(pair[1][:, :, None] * message[pair[0]], axis=1))
        agg = lax.map(jax.checkpoint(one_block), (idx_blocks, alpha_blocks)).reshape(NODES, D)
        agg = low(low_back(agg))
        u = low_back(mat(jnp.concatenate([h, agg], axis=1), ww) + wb)
        z = jax.nn.silu(u)
        s = lax.optimization_barrier(jnp.sum(z * z, axis=1, keepdims=True))
        return z * lax.rsqrt(s + 1e-06)
    inputs = (pin_features.astype(jnp.float32), board_features.astype(jnp.float32), proj_weight.astype(jnp.float32), proj_bias, q_weight.astype(jnp.float32), q_bias, w_weight.astype(jnp.float32), w_bias)
    emb, pullback = jax.vjp(forward, *inputs)
    grads = pullback(cotangent.astype(jnp.float32))
    mean_count = jnp.sum(present.astype(jnp.float32)) / NODES
    mean_weight = jnp.sum(filled) / (NODES * SLOTS)
    return (emb.astype(jnp.bfloat16), grads[0], grads[1], grads[2], grads[3], grads[4], grads[5], grads[6], grads[7], mean_count, mean_weight)
```

```python
import functools
import math

import jax
import jax.numpy as jnp
from jax import lax
from jax.experimental import pallas as pl
from jax.experimental.pallas import tpu as pltpu
from jax.sharding import PartitionSpec as P

SLOTS = 50
MESH = pl.DeviceIdType.MESH
BF = jnp.bfloat16
F32 = jnp.float32
NQ = 4
LO = 128
PIECE = 64
NT = (((1,), (1,)), ((), ()))
TN = (((0,), (0,)), ((), ()))


def dot(a, b):
    return jnp.dot(a, b, preferred_element_type=F32)


def dot_nt(a, b):
    return lax.dot_general(a, b, NT, preferred_element_type=F32)


def dot_tn(a, b):
    return lax.dot_general(a, b, TN, preferred_element_type=F32)


def loop(n, body, unroll=1):
    def step(i, carry):
        body(i)
        return carry

    lax.fori_loop(0, n, step, 0, unroll=unroll)


def row_sums(x):
    y = x[:, :128] + x[:, 128:]
    return jnp.concatenate(
        [jnp.sum(y[i * 128 : (i + 1) * 128].T, axis=0, keepdims=True) for i in range(2)], axis=0
    )


def down(row):
    return jnp.broadcast_to(row, (128, 128)).T


def down_pair(rows):
    col = jnp.concatenate([down(rows[0:1]), down(rows[1:2])], axis=0)
    return jnp.concatenate([col, col], axis=1)


def fused_kernel(*refs, names):
    s = dict(zip(names, refs))
    r = lax.axis_index("rows")
    c = lax.axis_index("cols")
    z, y = r // 2, r % 2
    x, k = c // 2, c % 2
    rows, width = s["pin"].shape
    bwidth = s["board"].shape[1]
    chunk = rows // NQ
    zn = 4
    core = (r, x * 2 + 1 - k)
    xp = (r, (1 - x) * 2 + k)
    xk = (r, (1 - x) * 2 + 1 - k)
    yp = (z * 2 + 1 - y, c)

    def at(q):
        return pl.ds(pl.multiple_of(q * chunk, chunk), chunk)

    def rdma(src, dst, send, recv, dev):
        return pltpu.make_async_remote_copy(
            src_ref=src, dst_ref=dst, send_sem=send, recv_sem=recv, device_id=dev, device_id_type=MESH
        )

    def arrived(ref, sem):
        rdma(ref, ref, sem, sem, core).wait_recv()

    def sent(ref, sem):
        rdma(ref, ref, sem, sem, core).wait_send()

    class Gather:
        def __init__(self, buf, base, ss, rs):
            self.buf, self.base, self.ss, self.rs = buf, base, ss, rs

        def ref(self, col, q):
            return self.buf.at[self.base + col, at(q)]

        def start(self, q):
            own = self.ref(c, q)
            rdma(own, own, self.ss.at[1, q], self.rs.at[1, q], xp).start()
            rdma(own, own, self.ss.at[0, q], self.rs.at[0, q], core).start()

        def forward(self, q):
            got = self.ref((1 - x) * 2 + k, q)
            arrived(got, self.rs.at[1, q])
            rdma(got, got, self.ss.at[2, q], self.rs.at[2, q], core).start()

        def finish(self, q):
            arrived(self.ref(x * 2 + 1 - k, q), self.rs.at[0, q])
            arrived(self.ref((1 - x) * 2 + 1 - k, q), self.rs.at[2, q])

        def drain(self, q):
            for i in range(3):
                sent(self.ref(c, q), self.ss.at[i, q])

    class Scatter:
        def __init__(self, part, name):
            self.part = part
            self.send1, self.recv1 = s[name + "_send1"], s[name + "_recv1"]
            self.sendx, self.recvx = s[name + "_sendx"], s[name + "_recvx"]
            self.ss, self.rs = s[name + "_ss"], s[name + "_rs"]

        def first(self, q):
            for i, xs in ((0, 1 - x), (1, x)):
                self.send1[i, q] = self.part(xs * 2 + 1 - k, q).astype(BF)
                rdma(
                    self.send1.at[i, q], self.recv1.at[i, q], self.ss.at[i, q], self.rs.at[i, q], core
                ).start()

        def second(self, q):
            own = self.part((1 - x) * 2 + k, q)
            arrived(self.recv1.at[0, q], self.rs.at[0, q])
            self.sendx[q] = (own + self.recv1[0, q].astype(F32)).astype(BF)
            rdma(self.sendx.at[q], self.recvx.at[q], self.ss.at[2, q], self.rs.at[2, q], xp).start()

        def third(self, q):
            own = self.part(c, q)
            arrived(self.recv1.at[1, q], self.rs.at[1, q])
            own = own + self.recv1[1, q].astype(F32)
            arrived(self.recvx.at[q], self.rs.at[2, q])
            return own + self.recvx[q].astype(F32)

        def drain(self, q):
            for i in range(2):
                sent(self.send1.at[i, q], self.ss.at[i, q])
            sent(self.sendx.at[q], self.ss.at[2, q])

    class WeightSum:
        def __init__(self, part, name, out):
            self.part, self.out = part, out
            self.ysend, self.yrecv = s[name + "_ysend"], s[name + "_yrecv"]
            self.zsend, self.zrecv = s[name + "_zsend"], s[name + "_zrecv"]
            self.ss, self.rs = s[name + "_ss"], s[name + "_rs"]

        def first(self):
            def step(d):
                self.ysend[d] = self.part(d, 1 - y).astype(BF)
                rdma(self.ysend.at[d], self.yrecv.at[d], self.ss.at[0, d], self.rs.at[0, d], yp).start()

            loop(zn, step)

        def second(self):
            def step(d):
                own = self.part(d, y)
                arrived(self.yrecv.at[d], self.rs.at[0, d])
                own = own + self.yrecv[d].astype(F32)

                @pl.when(d == z)
                def _():
                    self.out[...] = own

                @pl.when(d != z)
                def _():
                    self.zsend[d] = own.astype(BF)
                    rdma(
                        self.zsend.at[d],
                        self.zrecv.at[z],
                        self.ss.at[1, d],
                        self.rs.at[1, z],
                        (d * 2 + y, c),
                    ).start()

            loop(zn, step)

        def third(self):
            def step(d):
                @pl.when(d != z)
                def _():
                    arrived(self.zrecv.at[d], self.rs.at[1, d])
                    self.out[...] += self.zrecv[d].astype(F32)

            loop(zn, step)

        def drain(self):
            def step(d):
                sent(self.ysend.at[d], self.ss.at[0, d])

                @pl.when(d != z)
                def _():
                    sent(self.zsend.at[d], self.ss.at[1, d])

            loop(zn, step)

    barrier = pltpu.get_barrier_semaphore()
    greeted = [(r, (c + d) % 4) for d in range(1, 4)] + [((r + d) % 8, c) for d in range(1, 8)]
    for dev in greeted:
        pl.semaphore_signal(barrier, inc=1, device_id=dev, device_id_type=MESH)

    boards, own_h = s["boards"], s["ha"]
    boards[c] = s["board"][...]

    filled = s["present"][...].astype(F32) * s["importance"][...]
    alpha = filled / jnp.sum(filled, axis=1, keepdims=True)
    half = rows // 2
    gap = 64 - SLOTS

    def pairs(a):
        pad = jnp.zeros((half, gap), a.dtype)
        return jnp.concatenate([a[:half], pad, a[half:], pad], axis=1)

    small = s["small"]
    small[...] = jnp.zeros_like(small)
    sums = jnp.concatenate(
        [
            jnp.broadcast_to(jnp.sum(s["present"][...].astype(F32)).reshape(1, 1), (1, 128)),
            jnp.broadcast_to(jnp.sum(filled).reshape(1, 1), (1, 128)),
        ],
        axis=1,
    )
    small[r, 3:4] = sums
    numbers = pairs(s["neighbours"][...])
    s["high"][...] = (numbers // LO).astype(F32)
    s["low"][...] = (numbers % LO).astype(F32)
    s["weight"][...] = pairs(alpha)
    mask = s["mask"]
    flags = s["is_board"][...].astype(F32)
    for i in range(rows // 128):
        mask[i * 128 : (i + 1) * 128] = down(flags[i : i + 1])

    pl.semaphore_wait(barrier, len(greeted))

    def mask_of(q):
        m = mask[at(q)] > 0.5
        return jnp.concatenate([m, m], axis=1)

    table, stage = s["table"], s["stage"]
    pitch = stage.shape[0] // 64
    pairs_piece = PIECE // 2

    def piece(i):
        iota = lax.broadcasted_iota(jnp.int32, (128, 128), 0).astype(F32).astype(BF)
        front = lax.broadcasted_iota(jnp.int32, (16, 128), 1) < 64
        zero, one = jnp.zeros((), BF), jnp.ones((), BF)

        def tiles(v, n):
            return jnp.concatenate([v] * n, axis=0)

        def pair(j):
            p = i * pairs_piece + j

            def row(ref):
                return jnp.broadcast_to(ref[pl.ds(p, 1), :], (16, 128))

            hi, lo, al = row(s["high"]).astype(BF), row(s["low"]).astype(BF), row(s["weight"])
            al_a = jnp.where(front, al, 0.0).astype(BF)
            al_b = jnp.where(front, 0.0, al).astype(BF)
            places = jnp.where(tiles(lo, 8) == iota, one, zero)
            same = tiles(hi, 4) == iota[:64]
            weights = jnp.concatenate(
                [jnp.where(same, tiles(al_a, 4), zero), jnp.where(same, tiles(al_b, 4), zero)], axis=0
            )
            out = dot_nt(weights, places)
            stage[pl.ds(j, 64, stride=pitch), :] = out[:64]
            stage[pl.ds(j + pairs_piece, 64, stride=pitch), :] = out[64:]

        loop(pairs_piece, pair, unroll=8)

        def convert(h):
            for f in range(2):
                base = (2 * h + f) * pitch
                for g in range(2):
                    table[
                        h,
                        pl.ds(pl.multiple_of(i * pairs_piece + g * half, 16), pairs_piece),
                        f * 128 : (f + 1) * 128,
                    ] = stage[
                        pl.ds(pl.multiple_of(base + g * pairs_piece, 8), pairs_piece), :
                    ].astype(BF)

        loop(table.shape[0], convert, unroll=4)

    n_pieces = rows // PIECE

    gather_b = Gather(boards, 0, s["gb_ss"], s["gb_rs"])
    gather_h = Gather(own_h, 0, s["gh_ss"], s["gh_rs"])
    gather_a = Gather(own_h, 4, s["ga_ss"], s["ga_rs"])
    message, v_pre, u_pre = s["message"], s["v_pre"], s["u_pre"]

    def make_h(q):
        lines = at(q)
        b01 = jnp.concatenate([boards[0, lines], boards[1, lines]], axis=1)
        b23 = jnp.concatenate([boards[2, lines], boards[3, lines]], axis=1)
        proj = dot(b01, s["proj_w"][: 2 * bwidth]) + dot(b23, s["proj_w"][2 * bwidth :]) + s["proj_b"][...]
        own_h[c, lines] = jnp.where(mask_of(q), proj, s["pin"][lines].astype(F32)).astype(BF)

    def block(zb, yb, q):
        return message.at[zb * 2 + yb, q]

    def send_up(zb, q):
        ref = block(zb, y, q)
        rdma(ref, ref, s["up_ss"].at[zb, q], s["msg_rs"].at[zb * 2 + y, q], ((z + 1) * 2 + y, c)).start()

    def send_down(zb, q):
        ref = block(zb, y, q)
        rdma(ref, ref, s["down_ss"].at[zb, q], s["msg_rs"].at[zb * 2 + y, q], ((z - 1) * 2 + y, c)).start()

    def send_y(zb, q):
        ref = block(zb, y, q)
        rdma(ref, ref, s["y_ss"].at[zb, q], s["msg_rs"].at[zb * 2 + y, q], yp).start()

    def make_message(q):
        lines = at(q)
        acc = dot(own_h[0, lines], s["q_w"][:width])
        for i in range(1, 4):
            acc = acc + dot(own_h[i, lines], s["q_w"][i * width : (i + 1) * width])
        v = acc + s["q_b"][...]
        v_pre[lines] = v
        message[r, q] = (v * jax.nn.sigmoid(v)).astype(BF)

        @pl.when(z < 3)
        def _():
            send_up(z, q)

        @pl.when(z > 0)
        def _():
            send_down(z, q)

        send_y(z, q)

    loop(NQ, gather_b.start)

    def first_phase(t):
        @pl.when(t < NQ)
        def _():
            gather_b.forward(t)

        @pl.when((t >= 1) & (t < NQ + 1))
        def _():
            gather_b.finish(t - 1)
            make_h(t - 1)
            gather_h.start(t - 1)

        @pl.when((t >= 2) & (t < NQ + 2))
        def _():
            gather_h.forward(t - 2)

        @pl.when(t >= 3)
        def _():
            gather_h.finish(t - 3)
            make_message(t - 3)

        piece(t)

    loop(NQ + 3, first_phase)

    def u_from_h(q):
        lines = at(q)
        acc = dot(own_h[0, lines], s["w_w"][:width])
        for i in range(1, 4):
            acc = acc + dot(own_h[i, lines], s["w_w"][i * width : (i + 1) * width])
        u_pre[lines] = acc + s["w_b"][...]

    def second_phase(i):
        t, q = 1 + i // NQ, i % NQ

        @pl.when(z - t >= 0)
        def _():
            arrived(block(z - t, y, q), s["msg_rs"].at[(z - t) * 2 + y, q])

            @pl.when(z < 3)
            def _():
                send_up(z - t, q)

            send_y(z - t, q)

        @pl.when(z + t <= 3)
        def _():
            arrived(block(z + t, y, q), s["msg_rs"].at[(z + t) * 2 + y, q])

            @pl.when(z > 0)
            def _():
                send_down(z + t, q)

            send_y(z + t, q)

        @pl.when(i + NQ + 3 < n_pieces)
        def _():
            piece(i + NQ + 3)

        @pl.when(i < NQ)
        def _():
            u_from_h(i)

    loop(3 * NQ, second_phase)

    agg = s["agg"]
    agg[...] = jnp.zeros_like(agg)

    def add_block(b):
        def part(i):
            lines = at(i)
            acc = agg[lines]
            for q in range(NQ):
                acc = acc + dot(table[b * NQ + q, lines], message[b, q])
            agg[lines] = acc

        loop(rows // chunk, part)

    loop(zn, lambda zb: add_block(zb * 2 + y))

    order = [0, 1, 1, 2, 2, 3, 3]
    signs = [1, 1, -1, 1, -1, 1, -1]
    for t, sign in zip(order, signs):
        zb = z + sign * t

        @pl.when((zb >= 0) & (zb <= 3))
        def _():
            b = zb * 2 + 1 - y
            loop(NQ, lambda q: arrived(message.at[b, q], s["msg_rs"].at[b, q]))
            add_block(b)

    own_h[4 + c] = agg[...].astype(BF)

    gu, gv, gb = s["gu"], s["gv"], s["gb"]
    stat, stat_ss, stat_rs = s["stat"], s["stat_ss"], s["stat_rs"]
    peers = (core, xp, xk)

    loop(NQ, gather_a.start)

    def make_u(q):
        lines = at(q)
        u = u_pre[lines]
        for i in range(4):
            u = u + dot(own_h[4 + i, lines], s["w_w"][(4 + i) * width : (5 + i) * width])
        u_pre[lines] = u
        zz = u * jax.nn.sigmoid(u)
        g = s["cotangent"][lines].astype(F32)
        pad = jnp.zeros((4, 128), F32)
        stat[0, q] = jnp.concatenate([row_sums(zz * zz), row_sums(g * zz), pad], axis=0)
        for i, dev in enumerate(peers):
            rdma(
                stat.at[0, q], stat.at[1 + i, q], stat_ss.at[i, q], stat_rs.at[i, q], dev
            ).start()

    def make_gu(q):
        lines = at(q)
        for i in range(3):
            arrived(stat.at[1 + i, q], stat_rs.at[i, q])
        total = (stat[0, q] + stat[1, q]) + (stat[2, q] + stat[3, q])
        rr = lax.rsqrt(total[0:2] + 1e-6)
        scale = down_pair(rr)
        pull = down_pair(rr * rr * rr * total[2:4])
        u = u_pre[lines]
        sig = jax.nn.sigmoid(u)
        zz = u * sig
        g = s["cotangent"][lines].astype(F32)
        s["embeddings"][lines] = (zz * scale).astype(BF)
        gu[lines] = ((g * scale - zz * pull) * (sig * (1.0 + u * (1.0 - sig)))).astype(BF)

    def agg_part(col, q):
        wr = s["w_w"][pl.ds(pl.multiple_of((4 + col) * width, width), width), :]
        return dot_nt(gu[at(q)], wr)

    scatter_a = Scatter(agg_part, "sa")
    grad_agg = s["grad_agg"]

    sum_w = WeightSum(lambda d, yy: dot_tn(own_h[d * 2 + yy], gu[...]), "ww", s["grad_w"])

    def third_phase(t):
        @pl.when(t < NQ)
        def _():
            gather_a.forward(t)

        @pl.when((t >= 1) & (t < NQ + 1))
        def _():
            gather_a.finish(t - 1)
            make_u(t - 1)

        @pl.when((t >= 2) & (t < NQ + 2))
        def _():
            make_gu(t - 2)
            scatter_a.first(t - 2)

        @pl.when((t >= 3) & (t < NQ + 3))
        def _():
            scatter_a.second(t - 3)

        @pl.when(t == NQ + 1)
        def _():
            sum_w.first()

        @pl.when(t >= 4)
        def _():
            grad_agg[t - 4] = scatter_a.third(t - 4).T.astype(BF)

    loop(NQ + 4, third_phase)

    def sent_messages(q):
        @pl.when(z < 3)
        def _():
            sent(block(z, y, q), s["up_ss"].at[z, q])

        @pl.when(z > 0)
        def _():
            sent(block(z, y, q), s["down_ss"].at[z, q])

        for t in range(1, 4):
            @pl.when((z - t >= 0) & (z < 3))
            def _():
                sent(block(z, y, q), s["up_ss"].at[z - t, q])

            @pl.when((z + t <= 3) & (z > 0))
            def _():
                sent(block(z, y, q), s["down_ss"].at[z + t, q])

        for zb in range(4):
            sent(block(z, y, q), s["y_ss"].at[zb, q])

    loop(NQ, sent_messages)

    ysend = lambda d, q: message.at[d, q]
    zsend = lambda d, q: message.at[4 + d, q]
    yrecv, zrecv = s["yrecv"], s["zrecv"]
    m_ys, m_yr, m_zs, m_zr = s["m_ys"], s["m_yr"], s["m_zs"], s["m_zr"]
    upper = z // 2
    inner = z + upper * (3 - 2 * z) - 2 * upper * (z - z)
    inner = (z % 2) + upper * (1 - 2 * (z % 2))
    adjust = (0, 0, -1, 1)

    def dest(j):
        base = 3 - j + inner * adjust[j]
        return base + upper * (3 - 2 * base)

    def spread(d, yy, q):
        b = (d * 2 + yy) * NQ + q
        acc = dot(grad_agg[0], table[b, at(0)])
        for i in range(1, NQ):
            acc = acc + dot(grad_agg[i], table[b, at(i)])
        return acc

    for j in range(4):
        def over_y(q, j=j):
            d = dest(j)
            message[d, q] = spread(d, 1 - y, q).astype(BF)
            rdma(ysend(d, q), yrecv.at[d, q], m_ys.at[d, q], m_yr.at[d, q], yp).start()

        loop(NQ, over_y)

    sum_w.second()

    for j in range(3):
        d = dest(j)
        step = 1 - 2 * upper
        if j == 2:
            step = step * (1 - 2 * inner)
        is_dest = (0, inner, 1)[j]
        slot = d + is_dest * ((1 - step) // 2) * (4 - d)

        def along_z(q, d=d, step=step, slot=slot):
            own = spread(d, y, q)
            arrived(yrecv.at[d, q], m_yr.at[d, q])
            message[4 + d, q] = (own + yrecv[d, q].astype(F32)).astype(BF)

            @pl.when(inner == 1)
            def _():
                own2 = own + yrecv[d, q].astype(F32)
                arrived(zrecv.at[d, q], m_zr.at[d, q])
                message[4 + d, q] = (own2 + zrecv[d, q].astype(F32)).astype(BF)

            rdma(
                zsend(d, q), zrecv.at[slot, q], m_zs.at[d, q], m_zr.at[slot, q], ((z + step) * 2 + y, c)
            ).start()

        loop(NQ, along_z)

    total_t = s["total_t"]

    def make_gv(q):
        own = spread(z, y, q)
        arrived(yrecv.at[z, q], m_yr.at[z, q])
        total_t[...] = own + yrecv[z, q].astype(F32)

        @pl.when(z > 0)
        def _():
            arrived(zrecv.at[z, q], m_zr.at[z, q])
            total_t[...] += zrecv[z, q].astype(F32)

        @pl.when(z < 3)
        def _():
            arrived(zrecv.at[4, q], m_zr.at[4, q])
            total_t[...] += zrecv[4, q].astype(F32)

        v = v_pre[at(q)]
        sig = jax.nn.sigmoid(v)
        gv[at(q)] = (total_t[...].T * (sig * (1.0 + v * (1.0 - sig)))).astype(BF)

    def h_part(col, q):
        lines = pl.ds(pl.multiple_of(col * width, width), width)
        return dot_nt(gu[at(q)], s["w_w"][lines, :]) + dot_nt(gv[at(q)], s["q_w"][lines, :])

    def b_part(col, q):
        lines = pl.ds(pl.multiple_of(col * bwidth, bwidth), bwidth)
        return dot_nt(gb[at(q)], s["proj_w"][lines, :])

    scatter_h, scatter_b = Scatter(h_part, "sh"), Scatter(b_part, "sb")

    def q_part(d, yy):
        return dot_tn(own_h[d, :, pl.ds(pl.multiple_of(yy * 128, 128), 128)], gv[...])

    prod = s["prod"]

    def p_part(d, yy):
        prod[...] = dot_tn(boards[d], gb[...])
        n = prod.shape[0] // 2
        return prod[pl.ds(pl.multiple_of(yy * n, n), n), :]

    sum_q = WeightSum(q_part, "wq", s["grad_q"])
    sum_p = WeightSum(p_part, "wp", s["grad_p"])
    small_ss, small_rs = s["small_ss"], s["small_rs"]

    def send_small():
        for i, ref in enumerate((gb, gv, gu)):
            small[r, i : i + 1] = jnp.sum(ref[...].astype(F32), axis=0, keepdims=True)
        for d in range(1, 8):
            rdma(
                small.at[r], small.at[r], small_ss.at[d - 1], small_rs.at[r], ((r + d) % 8, c)
            ).start()

    def fourth_phase(t):
        @pl.when(t < NQ)
        def _():
            make_gv(t)
            scatter_h.first(t)

        @pl.when((t >= 1) & (t < NQ + 1))
        def _():
            scatter_h.second(t - 1)

        @pl.when(t == NQ)
        def _():
            sum_q.first()

        @pl.when((t >= 2) & (t < NQ + 2))
        def _():
            q = t - 2
            g = scatter_h.third(q)
            m = mask_of(q)
            s["grad_pin"][at(q)] = jnp.where(m, 0.0, g)
            gb[at(q)] = jnp.where(m, g, 0.0).astype(BF)
            scatter_b.first(q)

        @pl.when((t >= 3) & (t < NQ + 3))
        def _():
            scatter_b.second(t - 3)

        @pl.when(t == NQ + 1)
        def _():
            sum_p.first()
            send_small()
            sum_q.second()

        @pl.when(t >= 4)
        def _():
            s["grad_board"][at(t - 4)] = scatter_b.third(t - 4)

    loop(NQ + 4, fourth_phase)
    sum_p.second()
    sum_w.third()
    sum_q.third()
    for d in range(1, 8):
        other = (r + d) % 8
        arrived(small.at[other], small_rs.at[other])
    total = small[0]
    for i in range(1, 8):
        total = total + small[i]
    nodes = rows * 8
    per = jnp.concatenate(
        [jnp.full((1, 128), 1.0 / nodes, F32), jnp.full((1, 128), 1.0 / (nodes * SLOTS), F32)], axis=1
    )
    s["sums"][...] = total
    s["sums"][3:4] = total[3:4] * per
    sum_p.third()

    def drain(q):
        gather_b.drain(q)
        gather_h.drain(q)
        gather_a.drain(q)
        scatter_a.drain(q)
        scatter_h.drain(q)
        scatter_b.drain(q)
        for i in range(3):
            sent(stat.at[0, q], stat_ss.at[i, q])
        for d in range(4):
            sent(ysend(d, q), m_ys.at[d, q])

            @pl.when(d != z)
            def _():
                sent(zsend(d, q), m_zs.at[d, q])

    loop(NQ, drain)
    sum_w.drain()
    sum_q.drain()
    sum_p.drain()
    for d in range(7):
        sent(small.at[r], small_ss.at[d])


def fused_device(
    pin, board, is_board, neighbours, present, importance, proj_w, proj_b, q_w, q_b, w_w, w_b, cotangent
):
    rows, width = pin.shape
    bwidth = board.shape[1]
    chunk = rows // NQ
    nodes = rows * 8
    inputs = dict(
        pin=pin,
        board=board,
        is_board=is_board.reshape(rows // 128, 128),
        neighbours=neighbours,
        present=present,
        importance=importance,
        proj_w=proj_w,
        proj_b=proj_b.reshape(1, width),
        q_w=q_w,
        q_b=q_b.reshape(1, width),
        w_w=w_w,
        w_b=w_b.reshape(1, width),
        cotangent=cotangent,
    )
    shape = jax.ShapeDtypeStruct
    outs = dict(
        embeddings=shape((rows, width), BF),
        grad_pin=shape((rows, width), F32),
        grad_board=shape((rows, bwidth), F32),
        grad_p=shape((bwidth * 4 // 8, width), F32),
        grad_q=shape((width * 4 // 8, width), F32),
        grad_w=shape((2 * width * 4 // 8, width), F32),
        sums=shape((8, width), F32),
    )
    vmem, dma = pltpu.VMEM, pltpu.SemaphoreType.DMA
    scratch = dict(
        table=vmem((nodes // chunk, rows, chunk), BF),
        stage=vmem((64 * (PIECE + 8), 128), F32),
        high=vmem((rows // 2, 128), F32),
        low=vmem((rows // 2, 128), F32),
        weight=vmem((rows // 2, 128), F32),
        mask=vmem((rows, 128), F32),
        boards=vmem((4, rows, bwidth), BF),
        ha=vmem((8, rows, width), BF),
        message=vmem((8, NQ, chunk, width), BF),
        v_pre=vmem((rows, width), F32),
        u_pre=vmem((rows, width), F32),
        agg=vmem((rows, width), F32),
        gu=vmem((rows, width), BF),
        gv=vmem((rows, width), BF),
        gb=vmem((rows, width), BF),
        grad_agg=vmem((NQ, width, chunk), BF),
        stat=vmem((4, NQ, 8, 128), F32),
        small=vmem((8, 8, width), F32),
        yrecv=vmem((4, NQ, width, chunk), BF),
        zrecv=vmem((5, NQ, width, chunk), BF),
        total_t=vmem((width, chunk), F32),
        prod=vmem((bwidth, width), F32),
        stat_ss=dma((3, NQ)),
        stat_rs=dma((3, NQ)),
        msg_rs=dma((8, NQ)),
        up_ss=dma((4, NQ)),
        down_ss=dma((4, NQ)),
        y_ss=dma((4, NQ)),
        m_ys=dma((4, NQ)),
        m_yr=dma((4, NQ)),
        m_zs=dma((4, NQ)),
        m_zr=dma((5, NQ)),
        small_ss=dma((7,)),
        small_rs=dma((8,)),
    )
    for name in ("gb", "gh", "ga"):
        scratch[name + "_ss"] = dma((3, NQ))
        scratch[name + "_rs"] = dma((3, NQ))
    for name, w in (("sa", width), ("sh", width), ("sb", bwidth)):
        scratch[name + "_send1"] = vmem((2, NQ, chunk, w), BF)
        scratch[name + "_recv1"] = vmem((2, NQ, chunk, w), BF)
        scratch[name + "_sendx"] = vmem((NQ, chunk, w), BF)
        scratch[name + "_recvx"] = vmem((NQ, chunk, w), BF)
        scratch[name + "_ss"] = dma((3, NQ))
        scratch[name + "_rs"] = dma((3, NQ))
    for name, n in (("ww", width), ("wq", width // 2), ("wp", bwidth // 2)):
        for part in ("_ysend", "_yrecv", "_zsend", "_zrecv"):
            scratch[name + part] = vmem((4, n, width), BF)
        scratch[name + "_ss"] = dma((2, 4))
        scratch[name + "_rs"] = dma((2, 4))
    whole = pl.BlockSpec(memory_space=pltpu.VMEM)
    got = pl.pallas_call(
        functools.partial(fused_kernel, names=tuple(inputs) + tuple(outs) + tuple(scratch)),
        out_shape=list(outs.values()),
        in_specs=[whole] * len(inputs),
        out_specs=[whole] * len(outs),
        scratch_shapes=list(scratch.values()),
        compiler_params=pltpu.CompilerParams(
            collective_id=1, has_side_effects=True, vmem_limit_bytes=62 << 20
        ),
        cost_estimate=pl.CostEstimate(flops=14 << 30, bytes_accessed=8 << 20, transcendentals=0),
    )(*inputs.values())
    emb, g_pin, g_board, g_proj, g_q, g_w, sums = got
    return (
        emb,
        g_pin,
        g_board,
        g_proj,
        sums[0],
        g_q,
        sums[1],
        g_w,
        sums[2],
        sums[3, 0],
        sums[3, 128],
    )


def silu_slope(value):
    sig = jax.nn.sigmoid(value)
    return sig * (1.0 + value * (1.0 - sig))


def slot_table(nbr_block, alpha_block, start, width):
    offsets = nbr_block - start
    places = lax.broadcasted_iota(jnp.int32, (1, 1, width), 2)
    return jnp.sum(jnp.where(offsets[:, :, None] == places, alpha_block[:, :, None], 0.0), axis=1)


def split_pair(table):
    upper = table.astype(jnp.bfloat16)
    lower = (table - upper.astype(jnp.float32)).astype(jnp.bfloat16)
    return (upper, lower)


def collect_rows(nbrs, alphas, table_all):
    total, columns = table_all.shape
    col_tile = math.gcd(total, 2048)
    count_tiles = total // col_tile
    tiles = table_all.reshape(count_tiles, col_tile, columns)
    rows = nbrs.shape[0]
    row_block = math.gcd(rows, 512)
    count_rows = rows // row_block

    def one_rows(pair):
        nbr_block, alpha_block = pair

        def step(acc, index):
            upper, lower = split_pair(
                slot_table(nbr_block, alpha_block, index * col_tile, col_tile)
            )
            piece = tiles[index]
            acc = acc + jnp.dot(upper, piece, preferred_element_type=jnp.float32)
            return (acc + jnp.dot(lower, piece, preferred_element_type=jnp.float32), None)

        acc, unused = lax.scan(
            step, jnp.zeros((row_block, columns), jnp.float32), jnp.arange(count_tiles)
        )
        return acc

    out = lax.map(
        one_rows,
        (nbrs.reshape(count_rows, row_block, -1), alphas.reshape(count_rows, row_block, -1)),
    )
    return out.reshape(rows, columns)


def spread_rows(grads, nbrs, alphas, base, width):
    rows, columns = grads.shape
    row_block = math.gcd(rows, 512)
    count_rows = rows // row_block
    col_tile = math.gcd(width, 2048)
    count_tiles = width // col_tile
    stacked = (
        grads.reshape(count_rows, row_block, columns),
        nbrs.reshape(count_rows, row_block, -1),
        alphas.reshape(count_rows, row_block, -1),
    )
    tdot = (((0,), (0,)), ((), ()))

    def one_tile(index):

        def step(acc, triple):
            grad_block, nbr_block, alpha_block = triple
            upper, lower = split_pair(
                slot_table(nbr_block, alpha_block, base + index * col_tile, col_tile)
            )
            acc = acc + lax.dot_general(upper, grad_block, tdot, preferred_element_type=jnp.float32)
            return (
                acc + lax.dot_general(lower, grad_block, tdot, preferred_element_type=jnp.float32),
                None,
            )

        acc, unused = lax.scan(step, jnp.zeros((col_tile, columns), jnp.float32), stacked)
        return acc

    out = lax.map(one_tile, jnp.arange(count_tiles))
    return out.reshape(width, columns)


def per_device(
    pin_features,
    board_features,
    is_board,
    neighbours,
    present,
    importance,
    proj_weight,
    proj_bias,
    q_weight,
    q_bias,
    w_weight,
    w_bias,
    cotangent,
):
    local_rows = pin_features.shape[0]
    width = q_weight.shape[0]
    filled = present.astype(jnp.float32) * importance
    alpha = filled / jnp.sum(filled, axis=1, keepdims=True)
    board_mask = (is_board == 1)[:, None]
    stat_terms = (jnp.sum(present.astype(jnp.float32)), jnp.sum(filled))
    stat_totals = lax.psum((stat_terms[0], stat_terms[1]), "rows")
    board_full = lax.all_gather(board_features, "cols", axis=1, tiled=True)
    board_proj = jnp.dot(board_full, proj_weight, preferred_element_type=jnp.float32) + proj_bias
    h_local = jnp.where(board_mask, board_proj, pin_features.astype(jnp.float32)).astype(
        jnp.bfloat16
    )
    h_full = lax.all_gather(h_local, "cols", axis=1, tiled=True)
    v_pre = jnp.dot(h_full, q_weight, preferred_element_type=jnp.float32) + q_bias
    message = jax.nn.silu(v_pre).astype(jnp.bfloat16)
    message_all = lax.all_gather(message, "rows", axis=0, tiled=True)
    agg_local = collect_rows(neighbours, alpha, message_all).astype(jnp.bfloat16)
    agg_full = lax.all_gather(agg_local, "cols", axis=1, tiled=True)
    w_self = w_weight[:width]
    w_agg = w_weight[width:]
    u_pre = (
        jnp.dot(h_full, w_self, preferred_element_type=jnp.float32)
        + jnp.dot(agg_full, w_agg, preferred_element_type=jnp.float32)
        + w_bias
    )
    z_act = jax.nn.silu(u_pre)
    squares = lax.psum(jnp.sum(z_act * z_act, axis=1), "cols")
    scale = lax.rsqrt(squares + 1e-06)[:, None]
    embeddings = (z_act * scale).astype(jnp.bfloat16)
    grad_out = cotangent.astype(jnp.float32)
    inner = lax.psum(jnp.sum(grad_out * z_act, axis=1), "cols")[:, None]
    grad_z = grad_out * scale - z_act * scale * scale * scale * inner
    grad_u = (grad_z * silu_slope(u_pre)).astype(jnp.bfloat16)
    agg_part = lax.dot_general(
        grad_u, w_agg, (((1,), (1,)), ((), ())), preferred_element_type=jnp.float32
    )
    grad_agg = lax.psum_scatter(agg_part, "cols", scatter_dimension=1, tiled=True).astype(
        jnp.bfloat16
    )
    table = spread_rows(grad_agg, neighbours, alpha, 0, message_all.shape[0])
    grad_message = lax.psum_scatter(
        table.astype(jnp.bfloat16), "rows", scatter_dimension=0, tiled=True
    ).astype(jnp.float32)
    grad_v = (grad_message * silu_slope(v_pre)).astype(jnp.bfloat16)
    h_part = lax.dot_general(
        grad_u, w_self, (((1,), (1,)), ((), ())), preferred_element_type=jnp.float32
    )
    h_part = h_part + lax.dot_general(
        grad_v, q_weight, (((1,), (1,)), ((), ())), preferred_element_type=jnp.float32
    )
    grad_h = lax.psum_scatter(
        h_part.astype(jnp.bfloat16), "cols", scatter_dimension=1, tiled=True
    ).astype(jnp.float32)
    grad_pin = jnp.where(board_mask, 0.0, grad_h)
    grad_hb = jnp.where(board_mask, grad_h, 0.0).astype(jnp.bfloat16)
    board_part = lax.dot_general(
        grad_hb, proj_weight, (((1,), (1,)), ((), ())), preferred_element_type=jnp.float32
    )
    grad_board = lax.psum_scatter(
        board_part.astype(jnp.bfloat16), "cols", scatter_dimension=1, tiled=True
    ).astype(jnp.float32)
    tdot = (((0,), (0,)), ((), ()))
    grad_w_local = jnp.concatenate(
        [
            lax.dot_general(h_full, grad_u, tdot, preferred_element_type=jnp.float32),
            lax.dot_general(agg_full, grad_u, tdot, preferred_element_type=jnp.float32),
        ],
        axis=0,
    )
    grad_q_local = lax.dot_general(h_full, grad_v, tdot, preferred_element_type=jnp.float32)
    grad_p_local = lax.dot_general(board_full, grad_hb, tdot, preferred_element_type=jnp.float32)
    grad_w, grad_q, grad_proj = (
        lax.psum_scatter(
            grad_w_local.astype(jnp.bfloat16), "rows", scatter_dimension=0, tiled=True
        ).astype(jnp.float32),
        lax.psum_scatter(
            grad_q_local.astype(jnp.bfloat16), "rows", scatter_dimension=0, tiled=True
        ).astype(jnp.float32),
        lax.psum_scatter(
            grad_p_local.astype(jnp.bfloat16), "rows", scatter_dimension=0, tiled=True
        ).astype(jnp.float32),
    )
    bias_terms = (
        jnp.sum(grad_hb.astype(jnp.float32), axis=0),
        jnp.sum(grad_v.astype(jnp.float32), axis=0),
        jnp.sum(grad_u.astype(jnp.float32), axis=0),
    )
    grad_pb, grad_qb, grad_wb = lax.psum((bias_terms[0], bias_terms[1], bias_terms[2]), "rows")
    all_nodes = local_rows * lax.axis_size("rows")
    mean_count = stat_totals[0] / all_nodes
    mean_weight = stat_totals[1] / (all_nodes * SLOTS)
    return (
        embeddings,
        grad_pin,
        grad_board,
        grad_proj,
        grad_pb,
        grad_q,
        grad_qb,
        grad_w,
        grad_wb,
        mean_count,
        mean_weight,
    )


def solution(mesh):
    in_specs = (
        P("rows", "cols"),
        P("rows", "cols"),
        P("rows"),
        P("rows", None),
        P("rows", None),
        P("rows", None),
        P(None, "cols"),
        P("cols"),
        P(None, "cols"),
        P("cols"),
        P(None, "cols"),
        P("cols"),
        P("rows", "cols"),
    )
    out_specs = (
        P("rows", "cols"),
        P("rows", "cols"),
        P("rows", "cols"),
        P("rows", "cols"),
        P("cols"),
        P("rows", "cols"),
        P("cols"),
        P("rows", "cols"),
        P("cols"),
        P(),
        P(),
    )
    fused = mesh.shape["rows"] == 8 and mesh.shape["cols"] == 4
    return jax.shard_map(
        fused_device if fused else per_device, mesh=mesh, in_specs=in_specs, out_specs=out_specs, check_vma=False
    )
```

```python
import functools
import math
import types

import jax
import jax.numpy as jnp
from jax import lax
from jax.experimental import pallas as pl
from jax.experimental.pallas import tpu as pltpu
from jax.sharding import PartitionSpec as P

SLOTS = 50
MESH = pl.DeviceIdType.MESH
BF = jnp.bfloat16
F32 = jnp.float32
NQ = 4
NP = 2
LO_BITS = 7
LO = 1 << LO_BITS
PIECE = 64
NT = (((1,), (1,)), ((), ()))
TN = (((0,), (0,)), ((), ()))


def dot(a, b):
    return jnp.dot(a, b, preferred_element_type=F32)


def dot_nt(a, b):
    return lax.dot_general(a, b, NT, preferred_element_type=F32)


def dot_tn(a, b):
    return lax.dot_general(a, b, TN, preferred_element_type=F32)


def loop(n, body, unroll=1):
    def step(i, carry):
        body(i)
        return carry

    lax.fori_loop(0, n, step, 0, unroll=unroll)


def row_sums(x):
    y = x[:, :128] + x[:, 128:]
    sums = [
        jnp.sum(y[i * 128 : (i + 1) * 128].T, axis=0, keepdims=True) for i in range(x.shape[0] // 128)
    ]
    return sums[0] if len(sums) == 1 else jnp.concatenate(sums, axis=0)


def down(row):
    return jnp.broadcast_to(row, (128, 128)).T


def down_rows(rows):
    cols = [down(rows[i : i + 1]) for i in range(rows.shape[0])]
    col = cols[0] if len(cols) == 1 else jnp.concatenate(cols, axis=0)
    return jnp.concatenate([col, col], axis=1)


def fused_kernel(*refs, names):
    s = types.SimpleNamespace(**dict(zip(names, refs)))
    r = lax.axis_index("rows")
    c = lax.axis_index("cols")
    z, y = r // 2, r % 2
    x, k = c // 2, c % 2
    rows, width = s.pin.shape
    bwidth = s.boards.shape[2]
    chunk = rows // NQ
    zn = 4
    per_block = rows // LO
    core = (r, x * 2 + 1 - k)
    xp = (r, (1 - x) * 2 + k)
    xk = (r, (1 - x) * 2 + 1 - k)
    yp = (z * 2 + 1 - y, c)
    upper = z // 2
    inner = (z % 2) + upper * (1 - 2 * (z % 2))
    zx = z + 1 - 2 * (z % 2)
    zxp = (zx * 2 + y, c)

    def at(q):
        return pl.ds(pl.multiple_of(q * chunk, chunk), chunk)

    def rdma(src, dst, send, recv, dev):
        return pltpu.make_async_remote_copy(
            src_ref=src, dst_ref=dst, send_sem=send, recv_sem=recv, device_id=dev, device_id_type=MESH
        )

    def arrived(ref, sem):
        rdma(ref, ref, sem, sem, core).wait_recv()

    def sent(ref, sem):
        rdma(ref, ref, sem, sem, core).wait_send()

    class Gather:
        def __init__(self, buf, base, ss, rs):
            self.buf, self.base, self.ss, self.rs = buf, base, ss, rs

        def ref(self, col, q):
            return self.buf.at[self.base + col, at(q)]

        def start(self, q):
            own = self.ref(c, q)
            rdma(own, own, self.ss.at[1, q], self.rs.at[1, q], xp).start()
            rdma(own, own, self.ss.at[0, q], self.rs.at[0, q], core).start()

        def forward(self, q):
            got = self.ref((1 - x) * 2 + k, q)
            arrived(got, self.rs.at[1, q])
            rdma(got, got, self.ss.at[2, q], self.rs.at[2, q], core).start()

        def finish(self, q):
            arrived(self.ref(x * 2 + 1 - k, q), self.rs.at[0, q])
            arrived(self.ref((1 - x) * 2 + 1 - k, q), self.rs.at[2, q])

        def drain(self, q):
            for i in range(3):
                sent(self.ref(c, q), self.ss.at[i, q])

    class Scatter:
        def __init__(self, part, name):
            self.part = part
            self.send1, self.recv1 = getattr(s, name + "_send1"), getattr(s, name + "_recv1")
            self.sendx, self.recvx = getattr(s, name + "_sendx"), getattr(s, name + "_recvx")
            self.ss, self.rs = getattr(s, name + "_ss"), getattr(s, name + "_rs")

        def first(self, q):
            for i, xs in ((0, 1 - x), (1, x)):
                self.send1[i, q] = self.part(xs * 2 + 1 - k, q).astype(BF)
                rdma(
                    self.send1.at[i, q], self.recv1.at[i, q], self.ss.at[i, q], self.rs.at[i, q], core
                ).start()

        def second(self, q):
            own = self.part((1 - x) * 2 + k, q)
            arrived(self.recv1.at[0, q], self.rs.at[0, q])
            self.sendx[q] = (own + self.recv1[0, q].astype(F32)).astype(BF)
            rdma(self.sendx.at[q], self.recvx.at[q], self.ss.at[2, q], self.rs.at[2, q], xp).start()

        def third(self, q):
            own = self.part(c, q)
            arrived(self.recv1.at[1, q], self.rs.at[1, q])
            own = own + self.recv1[1, q].astype(F32)
            arrived(self.recvx.at[q], self.rs.at[2, q])
            return own + self.recvx[q].astype(F32)

        def drain(self, q):
            for i in range(2):
                sent(self.send1.at[i, q], self.ss.at[i, q])
            sent(self.sendx.at[q], self.ss.at[2, q])

    class WeightSum:
        def __init__(self, part, name, out, ysend, zsend):
            self.part, self.out = part, out
            self.ysend, self.zsend = ysend, zsend
            self.yrecv, self.zrecv = getattr(s, name + "_yrecv"), getattr(s, name + "_zrecv")
            self.ss, self.rs = getattr(s, name + "_ss"), getattr(s, name + "_rs")

        def first(self):
            def step(d):
                ref = self.ysend(d)
                ref[...] = self.part(d, 1 - y).astype(BF)
                rdma(ref, self.yrecv.at[d], self.ss.at[0, d], self.rs.at[0, d], yp).start()

            loop(zn, step)

        def second(self):
            def step(d):
                own = self.part(d, y)
                arrived(self.yrecv.at[d], self.rs.at[0, d])
                own = own + self.yrecv[d].astype(F32)

                @pl.when(d == z)
                def _():
                    self.out[...] = own

                @pl.when(d != z)
                def _():
                    ref = self.zsend(d)
                    ref[...] = own.astype(BF)
                    rdma(
                        ref, self.zrecv.at[z], self.ss.at[1, d], self.rs.at[1, z], (d * 2 + y, c)
                    ).start()

            loop(zn, step)

        def third(self):
            def step(d):
                @pl.when(d != z)
                def _():
                    arrived(self.zrecv.at[d], self.rs.at[1, d])
                    self.out[...] += self.zrecv[d].astype(F32)

            loop(zn, step)

        def drain(self):
            def step(d):
                sent(self.ysend(d), self.ss.at[0, d])

                @pl.when(d != z)
                def _():
                    sent(self.zsend(d), self.ss.at[1, d])

            loop(zn, step)

    class DirectSum:
        def __init__(self, out):
            self.out, self.send, self.recv = out, s.wp_send, s.wp_recv
            self.ss, self.rs = s.wp_ss, s.wp_rs

        def first(self, part):
            n = self.out.shape[0]

            def step(d):
                both = part(d)
                for yy in range(2):
                    block = both[yy * n : (yy + 1) * n]
                    row = d * 2 + yy

                    @pl.when(row == r)
                    def _():
                        self.out[...] = block

                    @pl.when(row != r)
                    def _():
                        ref = self.send.at[row]
                        ref[...] = block.astype(BF)
                        rdma(ref, self.recv.at[r], self.ss.at[row], self.rs.at[r], (row, c)).start()

            loop(zn, step)

        def second(self):
            def step(row):
                @pl.when(row != r)
                def _():
                    arrived(self.recv.at[row], self.rs.at[row])
                    self.out[...] += self.recv[row].astype(F32)

            loop(2 * zn, step)

        def drain(self):
            def step(row):
                @pl.when(row != r)
                def _():
                    sent(self.send.at[row], self.ss.at[row])

            loop(2 * zn, step)

    barrier = pltpu.get_barrier_semaphore()
    greeted = [(r, (c + d) % 4) for d in range(1, 4)] + [((r + d) % 8, c) for d in range(1, 8)]
    for dev in greeted:
        pl.semaphore_signal(barrier, inc=1, device_id=dev, device_id_type=MESH)

    boards, own_h = s.boards, s.ha
    in_sem = s.in_sem
    loads = {}
    order = (
        ("board", boards.at[c]),
        ("is_board", s.flags),
        ("proj_w", s.proj_w),
        ("proj_b", s.proj_b),
        ("pin", s.pin),
        ("neighbours", s.numbers),
        ("present", s.present),
        ("importance", s.importance),
        ("q_w", s.q_w),
        ("q_b", s.q_b),
        ("w_w", s.w_w),
        ("w_b", s.w_b),
        ("cotangent", s.cotangent),
    )
    for i, (name, ref) in enumerate(order):
        loads[name] = pltpu.make_async_copy(getattr(s, name + "_in"), ref, in_sem.at[i])
        loads[name].start()

    out_sem = s.out_sem

    def store(i, q, src, dst):
        return pltpu.make_async_copy(src, dst, out_sem.at[i, q])

    gather_b = Gather(boards, 0, s.gb_ss, s.gb_rs)
    gather_h = Gather(own_h, 0, s.gh_ss, s.gh_rs)
    loads["board"].wait()
    pl.semaphore_wait(barrier, len(greeted))
    loop(NQ, gather_b.start)

    mask = s.mask
    loads["is_board"].wait()
    flags = s.flags[...].astype(F32)
    for i in range(rows // 128):
        mask[i * 128 : (i + 1) * 128] = down(flags[i : i + 1])

    half = rows // 2
    padded = s.padded
    list_ss, list_rs = s.list_ss, s.list_rs

    quarter = rows // 4

    def lay(ref):
        for t in range(2):
            for i in range(quarter // 128):
                a, b = 2 * t * quarter + i * 128, (2 * t + 1) * quarter + i * 128
                ref[t, i * 128 : (i + 1) * 128] = jnp.concatenate(
                    [padded[:, a : a + 128], padded[:, b : b + 128]], axis=0
                ).T

    def lend_list(i):
        src, dst = ((s.numbers, s.numbers2), (s.alpha, s.alpha2))[i]
        return rdma(src, dst, list_ss.at[i], list_rs.at[i], yp)

    def prepare():
        for name in ("neighbours", "present", "importance"):
            loads[name].wait()
        lend_list(0).start()
        present = s.present[...].astype(F32)
        filled = present * s.importance[...]
        padded[SLOTS:] = jnp.zeros((padded.shape[0] - SLOTS, rows), F32)
        padded[:SLOTS] = filled / jnp.sum(filled, axis=0, keepdims=True)
        s.alpha[...] = padded[...].astype(BF)
        lend_list(1).start()
        lay(s.weight)
        small = s.small
        small[r] = jnp.zeros(small.shape[1:], F32)
        small[r, 3:4] = jnp.concatenate(
            [
                jnp.broadcast_to(jnp.sum(present).reshape(1, 1), (1, 128)),
                jnp.broadcast_to(jnp.sum(filled).reshape(1, 1), (1, 128)),
            ],
            axis=1,
        )
        numbers = s.numbers[...]
        padded[:SLOTS] = (numbers >> LO_BITS).astype(F32)
        lay(s.high)
        padded[:SLOTS] = (numbers & (LO - 1)).astype(F32)
        lay(s.low)

    def prepare2():
        for i in range(2):
            lend_list(i).wait_recv()
        numbers = s.numbers2[...]
        high = numbers >> LO_BITS
        place = (high // (2 * per_block)) * per_block + high % per_block
        padded[:SLOTS] = jnp.where((high // per_block) % 2 == y, place, -1).astype(F32)
        lay(s.high2)
        padded[:SLOTS] = (numbers & (LO - 1)).astype(F32)
        lay(s.low2)
        padded[...] = s.alpha2[...].astype(F32)
        lay(s.weight2)

    def mask_of(q):
        m = mask[at(q)] > 0.5
        return jnp.concatenate([m, m], axis=1)

    table, stage = s.table, s.stage
    pitch = stage.shape[0] // 64
    piece_rows = PIECE // 4

    def build(i, lists, table):
        n_high = 2 * table.shape[0]
        iota = lax.broadcasted_iota(jnp.int32, (128, 128), 0).astype(F32).astype(BF)
        front = lax.broadcasted_iota(jnp.int32, (16, 128), 1) < 64
        zero, one = jnp.zeros((), BF), jnp.ones((), BF)

        def tiles(v, n):
            return jnp.concatenate([v] * n, axis=0)

        zeros = jnp.zeros((n_high, 128), BF)
        n = n_high // 16

        def four(j):
            p = i * piece_rows + j
            weights, places = [], []
            for t in range(2):

                def row(ref):
                    return jnp.broadcast_to(ref[t, pl.ds(p, 1), :], (16, 128))

                hi, lo, al = row(lists[0]).astype(BF), row(lists[1]).astype(BF), row(lists[2])
                places.append(jnp.where(tiles(lo, 8) == iota, one, zero))
                same = tiles(hi, n) == iota[:n_high]
                for a in (jnp.where(front, al, 0.0), jnp.where(front, 0.0, al)):
                    w = jnp.where(same, tiles(a.astype(BF), n), zero)
                    weights.append(jnp.concatenate([w, zeros] if t == 0 else [zeros, w], axis=1))
            out = dot_nt(jnp.concatenate(weights, axis=0), jnp.concatenate(places, axis=1))
            for g in range(4):
                stage[pl.ds(j + g * piece_rows, n_high, stride=pitch), :] = out[
                    g * n_high : (g + 1) * n_high
                ]

        loop(piece_rows, four, unroll=16)

        def convert(h):
            for f in range(2):
                base = (2 * h + f) * pitch
                for g in range(4):
                    table[
                        h,
                        pl.ds(pl.multiple_of(i * piece_rows + g * quarter, 16), piece_rows),
                        f * 128 : (f + 1) * 128,
                    ] = stage[
                        pl.ds(pl.multiple_of(base + g * piece_rows, 8), piece_rows), :
                    ].astype(BF)

        loop(table.shape[0], convert, unroll=4)

    lists1 = (s.high, s.low, s.weight)
    lists2 = (s.high2, s.low2, s.weight2)
    table2 = s.table2

    def piece(i):
        build(i, lists1, table)

    def piece2(i):
        build(i, lists2, table2)

    n_pieces = rows // PIECE

    message, v_pre = s.message, s.v_pre

    def make_h(q):
        lines = at(q)
        b01 = jnp.concatenate([boards[0, lines], boards[1, lines]], axis=1)
        b23 = jnp.concatenate([boards[2, lines], boards[3, lines]], axis=1)
        proj = dot(b01, s.proj_w[: 2 * bwidth]) + dot(b23, s.proj_w[2 * bwidth :]) + s.proj_b[...]
        own_h[c, lines] = jnp.where(mask_of(q), proj, s.pin[lines].astype(F32)).astype(BF)

    def block(zb, yb, q):
        return message.at[zb * 2 + yb, q]

    def send_up(zb, q):
        ref = block(zb, y, q)
        rdma(ref, ref, s.up_ss.at[zb, q], s.msg_rs.at[zb * 2 + y, q], ((z + 1) * 2 + y, c)).start()

    def send_down(zb, q):
        ref = block(zb, y, q)
        rdma(ref, ref, s.down_ss.at[zb, q], s.msg_rs.at[zb * 2 + y, q], ((z - 1) * 2 + y, c)).start()

    def send_y(zb, q):
        ref = block(zb, y, q)
        rdma(ref, ref, s.y_ss.at[zb, q], s.msg_rs.at[zb * 2 + y, q], yp).start()

    def make_message(q):
        lines = at(q)
        acc = dot(own_h[0, lines], s.q_w[:width])
        for i in range(1, 4):
            acc = acc + dot(own_h[i, lines], s.q_w[i * width : (i + 1) * width])
        v = acc + s.q_b[...]
        v_pre[lines] = v
        message[r, q] = (v * jax.nn.sigmoid(v)).astype(BF)

        @pl.when(z < 3)
        def _():
            send_up(z, q)

        @pl.when(z > 0)
        def _():
            send_down(z, q)

        send_y(z, q)

    prepare()
    for name in ("proj_w", "proj_b", "pin"):
        loads[name].wait()

    def board_phase(q):
        gather_b.forward(q)
        gather_b.finish(q)
        make_h(q)
        gather_h.start(q)

    piece(0)
    loop(NQ, board_phase)
    early = 3
    loop(early - 1, lambda i: piece(1 + i))

    half = rows // 2
    sub = half // NP
    own_half = pl.ds(pl.multiple_of(x * half, half), half)
    their_half = pl.ds(pl.multiple_of((1 - x) * half, half), half)
    lend_ss, lend_rs = s.lend_ss, s.lend_rs
    wide = 4 * width

    def lends():
        return (
            (s.w_w.at[:wide], s.w2.at[:wide]),
            (s.w_b, s.w_b2),
            (s.w_w.at[wide:], s.w2.at[wide:]),
            (s.cotangent.at[their_half], s.cotangent2),
        )

    def lend(i):
        src, dst = lends()[i]
        return rdma(src, dst, lend_ss.at[i], lend_rs.at[i], xp)

    for name in ("w_w", "w_b", "cotangent"):
        loads[name].wait()
    for i in range(4):
        lend(i).start()
    loads["q_w"].wait()
    loads["q_b"].wait()

    def message_phase(q):
        gather_h.forward(q)
        gather_h.finish(q)
        make_message(q)
        piece(early + q)

        @pl.when(q % 2 == 0)
        def _():
            piece(early + NQ + q // 2)

    loop(NQ, message_phase)
    built = early + NQ + NQ // 2

    u_pre = s.u_pre

    def part_of(i):
        return pl.ds(pl.multiple_of(i * sub, sub), sub)

    def mine(i):
        return pl.ds(pl.multiple_of(x * half + i * sub, sub), sub)

    def theirs(i):
        return pl.ds(pl.multiple_of((1 - x) * half + i * sub, sub), sub)

    def u_from_h(i):
        for n, w, b in ((0, s.w_w, s.w_b), (1, s.w2, s.w_b2)):
            acc = dot(own_h[0, mine(i)], w[:width])
            for m in range(1, 4):
                acc = acc + dot(own_h[m, mine(i)], w[m * width : (m + 1) * width])
            u_pre[n, part_of(i)] = acc + b[...]

    agg = s.grad_pin
    parts = rows // chunk

    def add(b, first, n):
        for i in range(parts):
            lines = slice(i * chunk, (i + 1) * chunk)
            acc = agg[lines]
            for q in range(first, first + n):
                acc = acc + dot(table[b * NQ + q, lines], message[b, q])
            agg[lines] = acc

    def over_y(zb, q):
        @pl.when((zb != zx) | ((inner == 0) & (q < NQ // 2)))
        def _():
            send_y(zb, q)

    def send_zx(q):
        ref = block(z, 1 - y, q)
        rdma(ref, ref, s.zx_ss.at[q], s.msg_rs.at[z * 2 + 1 - y, q], zxp).start()

    def at_z(zb):
        return (zb >= 0) & (zb <= 3)

    n_second = 3 * NQ
    n_second2 = n_pieces // 2
    steps = n_pieces - built

    def second_phase(i):
        t, q = 1 + i // NQ, i % NQ

        @pl.when(z - t >= 0)
        def _():
            arrived(block(z - t, y, q), s.msg_rs.at[(z - t) * 2 + y, q])

            @pl.when(z < 3)
            def _():
                send_up(z - t, q)

            over_y(z - t, q)

        @pl.when(z + t <= 3)
        def _():
            arrived(block(z + t, y, q), s.msg_rs.at[(z + t) * 2 + y, q])

            @pl.when(z > 0)
            def _():
                send_down(z + t, q)

            over_y(z + t, q)

        @pl.when(t == 1)
        def _():
            arrived(block(z, 1 - y, q), s.msg_rs.at[z * 2 + 1 - y, q])

            @pl.when(inner == 0)
            def _():
                send_zx(q)

        @pl.when((t == 3) & (inner == 1) & (q >= NQ // 2))
        def _():
            send_zx(q)

        @pl.when(i < steps)
        def _():
            piece(built + i)

        @pl.when(i == 0)
        def _():
            prepare2()

        @pl.when((i > 0) & (i < 1 + n_second2))
        def _():
            loop(2, lambda n: piece2(2 * (i - 1) + n))

        @pl.when(i == steps)
        def _():
            agg[...] = jnp.zeros_like(agg)
            lend(0).wait_recv()
            lend(1).wait_recv()

        @pl.when(i >= n_second - NP)
        def _():
            u_from_h(i - (n_second - NP))

        @pl.when((i >= n_second - 5) & (i < n_second))
        def _():
            n = i - (n_second - 5)
            zb = z + jnp.where(n == 0, 0, jnp.where(n == 1, -1, jnp.where(n == 2, 1, jnp.where(n == 3, -2, 2))))

            @pl.when(at_z(zb))
            def _():
                add(zb * 2 + y, 0, NQ)

    loop(n_second, second_phase)

    add(z * 2 + 1 - y, 0, NQ)
    for zb in (z - 3, z + 3):
        @pl.when(at_z(zb))
        def _():
            add(zb * 2 + y, 0, NQ)

    def add_arriving(zb, first, n):
        b = zb * 2 + 1 - y
        loop(n, lambda q: arrived(message.at[b, first + q], s.msg_rs.at[b, first + q]))
        add(b, first, n)

    add_arriving(zx, 0, NQ // 2)
    for t in (1, 2, 3):
        for zb in (z - t, z + t):
            @pl.when(at_z(zb) & (zb != zx))
            def _():
                add_arriving(zb, 0, NQ)

    add_arriving(zx, NQ // 2, NQ // 2)
    own_h[4 + c] = agg[...].astype(BF)

    gu, gv, gb, gu2 = s.gu, s.gv, s.gb, s.gu2
    stat, stat_ss, stat_rs = s.stat, s.stat_ss, s.stat_rs
    ga_ss, ga_rs = s.ga_ss, s.ga_rs
    other_x = (1 - x) * 2 + k

    def agg_ref(col, lines):
        return own_h.at[4 + col, lines]

    def agg_start(i):
        a, b = agg_ref(c, theirs(i)), agg_ref(c, mine(i))
        rdma(a, a, ga_ss.at[1, i], ga_rs.at[1, i], xp).start()
        rdma(b, b, ga_ss.at[0, i], ga_rs.at[0, i], core).start()

    def agg_forward(i):
        got = agg_ref(other_x, mine(i))
        arrived(got, ga_rs.at[1, i])
        rdma(got, got, ga_ss.at[2, i], ga_rs.at[2, i], core).start()

    def agg_finish(i):
        arrived(agg_ref(x * 2 + 1 - k, mine(i)), ga_rs.at[0, i])
        arrived(agg_ref((1 - x) * 2 + 1 - k, mine(i)), ga_rs.at[2, i])

    def rest_start():
        a, b = agg_ref(c, own_half), agg_ref(c, their_half)
        rdma(a, a, ga_ss.at[1, NP], ga_rs.at[1, NP], xp).start()
        rdma(b, b, ga_ss.at[0, NP], ga_rs.at[0, NP], core).start()

    def rest_forward():
        got = agg_ref(other_x, their_half)
        arrived(got, ga_rs.at[1, NP])
        rdma(got, got, ga_ss.at[2, NP], ga_rs.at[2, NP], core).start()

    def rest_finish():
        arrived(agg_ref(x * 2 + 1 - k, their_half), ga_rs.at[0, NP])
        arrived(agg_ref((1 - x) * 2 + 1 - k, their_half), ga_rs.at[2, NP])

    loop(NP, agg_start)
    lend(2).wait_recv()
    lend(3).wait_recv()

    def gradients(i):
        return s.cotangent[mine(i)].astype(F32), s.cotangent2[part_of(i)].astype(F32)

    def make_u(i):
        us = [u_pre[n, part_of(i)] for n in range(2)]
        for m in range(4):
            a = own_h[4 + m, mine(i)]
            us = [u + dot(a, w[(4 + m) * width : (5 + m) * width]) for u, w in zip(us, (s.w_w, s.w2))]
        squares, inners = 0.0, 0.0
        for n, (u, g) in enumerate(zip(us, gradients(i))):
            u_pre[n, part_of(i)] = u
            zz = u * jax.nn.sigmoid(u)
            squares = squares + zz * zz
            inners = inners + g * zz
        pad = jnp.zeros((8 - 2 * sub // 128, 128), F32)
        stat[0, i] = jnp.concatenate([row_sums(squares), row_sums(inners), pad], axis=0)
        rdma(stat.at[0, i], stat.at[1, i], stat_ss.at[i], stat_rs.at[i], core).start()

    def make_gu(i):
        arrived(stat.at[1, i], stat_rs.at[i])
        total = stat[0, i] + stat[1, i]
        n_rows = sub // 128
        rr = lax.rsqrt(total[:n_rows] + 1e-6)
        scale = down_rows(rr)
        pull = down_rows(rr * rr * rr * total[n_rows : 2 * n_rows])
        for n, (g, emb, grad) in enumerate(
            zip(gradients(i), (s.embeddings, s.emb2), (gu, gu2))
        ):
            u = u_pre[n, part_of(i)]
            sig = jax.nn.sigmoid(u)
            zz = u * sig
            lines = mine(i) if n == 0 else part_of(i)
            emb[lines] = (zz * scale).astype(BF)
            grad[lines] = ((g * scale - zz * pull) * (sig * (1.0 + u * (1.0 - sig)))).astype(BF)

    def agg_part(col, i):
        lines = pl.ds(pl.multiple_of((4 + col) * width, width), width)
        return dot_nt(gu[mine(i)], s.w_w[lines, :]) + dot_nt(gu2[part_of(i)], s.w2[lines, :])

    grad_agg, grad_agg2 = s.grad_agg, s.grad_agg2
    sa_send, sa_recv, sa_x, sa_ss, sa_rs = s.sa_send, s.sa_recv, s.sa_x, s.sa_ss, s.sa_rs

    def agg_first(i):
        for n, xs in ((0, 1 - x), (1, x)):
            sa_send[n, i] = agg_part(xs * 2 + 1 - k, i).astype(BF)
            rdma(sa_send.at[n, i], sa_recv.at[n, i], sa_ss.at[n, i], sa_rs.at[n, i], core).start()

    def agg_second(i):
        own = agg_part(other_x, i)
        arrived(sa_recv.at[0, i], sa_rs.at[0, i])
        sa_x[i] = (own + sa_recv[0, i].astype(F32)).T.astype(BF)
        rdma(sa_x.at[i], grad_agg.at[x * NP + i], sa_ss.at[2, i], sa_rs.at[2, i], xp).start()

    def agg_third(i):
        own = agg_part(c, i)
        arrived(sa_recv.at[1, i], sa_rs.at[1, i])
        grad_agg[x * NP + i] = (own + sa_recv[1, i].astype(F32)).T.astype(BF)
        agg_over_y(x * NP + i)

    def agg_over_y(i):
        rdma(grad_agg.at[i], grad_agg2.at[i], s.gy_ss.at[i], s.gy_rs.at[i], yp).start()

    def room(at_block, n):
        return [lambda d, b=b, n=n: message.at[b, d, pl.ds(0, n)] for b in (at_block, at_block + 1)]

    def room_narrow(at_block, n):
        return [lambda d, i=i: message.at[at_block, d, pl.ds(i * n, n)] for i in range(2)]

    sum_w = WeightSum(lambda d, yy: dot_tn(own_h[d * 2 + yy], gu[...]), "ww", s.grad_w, *room(4, width))

    def third_phase(t):
        @pl.when(t < NP)
        def _():
            agg_forward(t)
            agg_finish(t)
            make_u(t)

        @pl.when((t >= 2) & (t < NP + 2))
        def _():
            agg_second(t - 2)
            agg_third(t - 2)

        @pl.when((t >= 1) & (t < NP + 1))
        def _():
            make_gu(t - 1)
            agg_first(t - 1)

    loop(NP + 2, third_phase)

    def give(n):
        src, dst = ((gu2, gu.at[own_half]), (s.emb2, s.embeddings.at[own_half]))[n]
        return rdma(src, dst, s.give_ss.at[n], s.give_rs.at[n], xp)

    def give_back(n):
        ref = (gu, s.embeddings)[n].at[their_half]
        return rdma(ref, ref, s.give_ss.at[n], s.give_rs.at[n], xp)

    give(0).start()
    rest_start()
    give(1).start()
    def pass_on(i):
        arrived(grad_agg.at[(1 - x) * NP + i], sa_rs.at[2, i])
        agg_over_y((1 - x) * NP + i)

    loop(NP, pass_on)
    loop(2 * NP, lambda i: arrived(grad_agg2.at[i], s.gy_rs.at[i]))

    def sent_messages(q):
        @pl.when(z < 3)
        def _():
            sent(block(z, y, q), s.up_ss.at[z, q])

        @pl.when(z > 0)
        def _():
            sent(block(z, y, q), s.down_ss.at[z, q])

        for t in range(1, 4):
            @pl.when((z - t >= 0) & (z < 3))
            def _():
                sent(block(z, y, q), s.up_ss.at[z - t, q])

            @pl.when((z + t <= 3) & (z > 0))
            def _():
                sent(block(z, y, q), s.down_ss.at[z + t, q])

        for zb in range(4):
            @pl.when((zb != zx) | ((inner == 0) & (q < NQ // 2)))
            def _():
                sent(block(z, y, q), s.y_ss.at[zb, q])

        @pl.when((inner == 0) | (q >= NQ // 2))
        def _():
            sent(block(z, y, q), s.zx_ss.at[q])

    loop(NQ, sent_messages)

    zsend, zrecv = message, s.zrecv
    m_zs, m_zr = s.m_zs, s.m_zr
    adjust = (0, 0, -1, 1)

    def dest(j):
        base = 3 - j + inner * adjust[j]
        return base + upper * (3 - 2 * base)

    each = 2 * NP // NQ

    def sum_of(terms):
        total = None
        for term in terms:
            total = term if total is None else total + term
        return total

    def spread(d, q):
        own, other = (d * 2 + y) * NQ + q, d * NQ + q

        def grads(ref, i):
            return jnp.concatenate([ref[m] for m in range(i * each, (i + 1) * each)], axis=1)

        return sum_of(
            dot(grads(ref, i), tab[b, at(i)])
            for ref, tab, b in ((grad_agg, table, own), (grad_agg2, table2, other))
            for i in range(NQ)
        )

    def along(j):
        d = dest(j)
        step = 1 - 2 * upper
        if j == 2:
            step = step * (1 - 2 * inner)
        is_dest = (0, inner, 1)[j]
        slot = d + is_dest * ((1 - step) // 2) * (4 - d)

        def along_z(q):
            own = spread(d, q)

            @pl.when(inner == 0)
            def _():
                zsend[d, q] = own.astype(BF)

            @pl.when(inner == 1)
            def _():
                arrived(zrecv.at[d, q], m_zr.at[d, q])
                zsend[d, q] = (own + zrecv[d, q].astype(F32)).astype(BF)

            rdma(
                zsend.at[d, q], zrecv.at[slot, q], m_zs.at[d, q], m_zr.at[slot, q], ((z + step) * 2 + y, c)
            ).start()

        loop(NQ, along_z)

    along(0)

    @pl.when(inner == 0)
    def _():
        along(1)
        along(2)

    for n in range(2):
        give_back(n).wait_recv()
    store(0, 0, s.embeddings, s.embeddings_out).start()
    rest_forward()
    rest_finish()
    sum_w.first()

    @pl.when(inner == 1)
    def _():
        along(1)
        along(2)

    sum_w.second()

    total_t = s.total_t

    def make_gv(q):
        total_t[...] = spread(z, q)

        @pl.when(z > 0)
        def _():
            arrived(zrecv.at[z, q], m_zr.at[z, q])
            total_t[...] += zrecv[z, q].astype(F32)

        @pl.when(z < 3)
        def _():
            arrived(zrecv.at[4, q], m_zr.at[4, q])
            total_t[...] += zrecv[4, q].astype(F32)

        v = v_pre[at(q)]
        sig = jax.nn.sigmoid(v)
        gv[at(q)] = (total_t[...].T * (sig * (1.0 + v * (1.0 - sig)))).astype(BF)

    def h_part(col, q):
        lines = pl.ds(pl.multiple_of(col * width, width), width)
        return dot_nt(gu[at(q)], s.w_w[lines, :]) + dot_nt(gv[at(q)], s.q_w[lines, :])

    def b_part(col, q):
        lines = pl.ds(pl.multiple_of(col * bwidth, bwidth), bwidth)
        return dot_nt(gb[at(q)], s.proj_w[lines, :])

    scatter_h, scatter_b = Scatter(h_part, "sh"), Scatter(b_part, "sb")

    def q_part(d, yy):
        return dot_tn(own_h[d, :, pl.ds(pl.multiple_of(yy * 128, 128), 128)], gv[...])

    sum_q = WeightSum(q_part, "wq", s.grad_q, *room_narrow(6, width // 2))
    sum_p = DirectSum(s.grad_p)
    small, small_ss, small_rs = s.small, s.small_ss, s.small_rs

    def send_small():
        for i, ref in enumerate((gb, gv, gu)):
            small[r, i : i + 1] = jnp.sum(ref[...].astype(F32), axis=0, keepdims=True)
        for d in range(1, 8):
            rdma(
                small.at[r], small.at[r], small_ss.at[d - 1], small_rs.at[r], ((r + d) % 8, c)
            ).start()

    def finish_board(q):
        s.grad_board[at(q)] = scatter_b.third(q)
        store(2, q, s.grad_board.at[at(q)], s.grad_board_out.at[at(q)]).start()

    def fourth_phase(t):
        @pl.when(t < NQ)
        def _():
            make_gv(t)
            scatter_h.first(t)

        @pl.when((t >= 2) & (t < NQ + 2))
        def _():
            q = t - 2
            g = scatter_h.third(q)
            m = mask_of(q)
            gb[at(q)] = jnp.where(m, g, 0.0).astype(BF)
            s.grad_pin[at(q)] = jnp.where(m, 0.0, g)

            @pl.when(t == NQ + 1)
            def _():
                sum_p.first(lambda d: dot_tn(boards[d], gb[...]))

            scatter_b.first(q)
            store(1, q, s.grad_pin.at[at(q)], s.grad_pin_out.at[at(q)]).start()

        @pl.when(t < NQ)
        def _():
            scatter_h.second(t)

        @pl.when(t == NQ - 1)
        def _():
            sum_q.first()

        @pl.when(t == NQ + 1)
        def _():
            send_small()

        @pl.when((t >= 2) & (t < NQ + 2))
        def _():
            scatter_b.second(t - 2)

        @pl.when(t == NQ + 1)
        def _():
            sum_q.second()

        @pl.when(t >= NQ)
        def _():
            finish_board(t - NQ)

    loop(NQ + 2, fourth_phase)
    sum_w.third()
    store(0, 1, s.grad_w, s.grad_w_out).start()
    loop(NQ - 2, lambda t: finish_board(t + 2))
    sum_q.third()
    store(0, 2, s.grad_q, s.grad_q_out).start()
    for d in range(1, 8):
        other = (r + d) % 8
        arrived(small.at[other], small_rs.at[other])
    total = small[0]
    for i in range(1, 8):
        total = total + small[i]
    nodes = rows * 8
    per = jnp.concatenate(
        [jnp.full((1, 128), 1.0 / nodes, F32), jnp.full((1, 128), 1.0 / (nodes * SLOTS), F32)], axis=1
    )
    s.sums[...] = total
    s.sums[3:4] = total[3:4] * per
    store(0, 3, s.sums, s.sums_out).start()
    sum_p.second()
    store(3, 0, s.grad_p, s.grad_p_out).start()

    def drain(q):
        gather_b.drain(q)
        gather_h.drain(q)
        scatter_h.drain(q)
        scatter_b.drain(q)
        store(1, q, s.grad_pin.at[at(q)], s.grad_pin_out.at[at(q)]).wait()
        store(2, q, s.grad_board.at[at(q)], s.grad_board_out.at[at(q)]).wait()
        for d in range(4):
            @pl.when(d != z)
            def _():
                sent(zsend.at[d, q], m_zs.at[d, q])

    loop(NQ, drain)

    def drain_half(i):
        for n in range(3):
            sent(agg_ref(c, mine(i)), ga_ss.at[n, i])
        for n in range(2):
            sent(sa_send.at[n, i], sa_ss.at[n, i])
        sent(sa_x.at[i], sa_ss.at[2, i])
        sent(stat.at[0, i], stat_ss.at[i])

    loop(NP, drain_half)
    for n in range(3):
        sent(agg_ref(c, own_half), ga_ss.at[n, NP])
    for n in range(4):
        lend(n).wait_send()
    for n in range(2):
        lend_list(n).wait_send()
    loop(2 * NP, lambda i: sent(grad_agg.at[i], s.gy_ss.at[i]))
    for n in range(2):
        give(n).wait_send()
    sum_w.drain()
    sum_q.drain()
    sum_p.drain()
    for d in range(7):
        sent(small.at[r], small_ss.at[d])
    for i, (n, name) in enumerate(
        ((0, "embeddings"), (0, "grad_w"), (0, "grad_q"), (0, "sums"), (3, "grad_p"))
    ):
        store(n, i % 4, getattr(s, name), getattr(s, name + "_out")).wait()


def finish_kernel(*refs):
    ins, sums, outs, small, held, sem = refs[:6], refs[6], refs[7:13], refs[13:18], refs[18:24], refs[24]
    first = [pltpu.make_async_copy(a, b, sem.at[0, i]) for i, (a, b) in enumerate(zip(ins, held))]
    second = [pltpu.make_async_copy(a, b, sem.at[1, i]) for i, (a, b) in enumerate(zip(held, outs))]
    for copy in first:
        copy.start()
    for i in range(3):
        small[i][...] = sums[i : i + 1]
    small[3][...] = sums[3:4, 0:1]
    small[4][...] = sums[3:4, 128:129]
    for a, b in zip(first, second):
        a.wait()
        b.start()
    for copy in second:
        copy.wait()


def fused_device(
    pin, board, is_board, neighbours, present, importance, proj_w, proj_b, q_w, q_b, w_w, w_b, cotangent
):
    rows, width = pin.shape
    bwidth = board.shape[1]
    chunk = rows // NQ
    nodes = rows * 8
    inputs = dict(
        board=board,
        is_board=is_board.reshape(rows // 128, 128),
        proj_w=proj_w,
        proj_b=proj_b.reshape(1, width),
        pin=pin,
        neighbours=neighbours.T,
        present=present.T,
        importance=importance.T,
        q_w=q_w,
        q_b=q_b.reshape(1, width),
        w_w=w_w,
        w_b=w_b.reshape(1, width),
        cotangent=cotangent,
    )
    shape = jax.ShapeDtypeStruct
    outs = dict(
        embeddings=shape((rows, width), BF),
        grad_pin=shape((rows, width), F32),
        grad_board=shape((rows, bwidth), F32),
        grad_p=shape((bwidth * 4 // 8, width), F32),
        grad_q=shape((width * 4 // 8, width), F32),
        grad_w=shape((2 * width * 4 // 8, width), F32),
        sums=shape((8, width), F32),
    )
    vmem, dma = pltpu.VMEM, pltpu.SemaphoreType.DMA
    scratch = dict(
        in_sem=dma((len(inputs),)),
        out_sem=dma((4, NQ)),
        flags=vmem((rows // 128, 128), jnp.int32),
        numbers=vmem((SLOTS, rows), jnp.int32),
        numbers2=vmem((SLOTS, rows), jnp.int32),
        alpha=vmem((64, rows), BF),
        alpha2=vmem((64, rows), BF),
        padded=vmem((64, rows), F32),
        table2=vmem((nodes // 2 // chunk, rows, chunk), BF),
        high2=vmem((2, rows // 4, 128), F32),
        low2=vmem((2, rows // 4, 128), F32),
        weight2=vmem((2, rows // 4, 128), F32),
        grad_agg2=vmem((2 * NP, width, rows // 2 // NP), BF),
        table=vmem((nodes // chunk, rows, chunk), BF),
        stage=vmem((64 * (PIECE + 8), 128), F32),
        high=vmem((2, rows // 4, 128), F32),
        low=vmem((2, rows // 4, 128), F32),
        weight=vmem((2, rows // 4, 128), F32),
        mask=vmem((rows, 128), F32),
        boards=vmem((4, rows, bwidth), BF),
        ha=vmem((8, rows, width), BF),
        message=vmem((8, NQ, chunk, width), BF),
        v_pre=vmem((rows, width), F32),
        u_pre=vmem((2, rows // 2, width), F32),
        w2=vmem(w_w.shape, BF),
        w_b2=vmem((1, width), F32),
        cotangent2=vmem((rows // 2, width), BF),
        gu2=vmem((rows // 2, width), BF),
        emb2=vmem((rows // 2, width), BF),
        sa_send=vmem((2, NP, rows // 2 // NP, width), BF),
        sa_recv=vmem((2, NP, rows // 2 // NP, width), BF),
        sa_x=vmem((NP, width, rows // 2 // NP), BF),
        sa_ss=dma((3, NP)),
        sa_rs=dma((3, NP)),
        ga_ss=dma((3, NP + 1)),
        ga_rs=dma((3, NP + 1)),
        lend_ss=dma((4,)),
        lend_rs=dma((4,)),
        give_ss=dma((2,)),
        give_rs=dma((2,)),
        gu=vmem((rows, width), BF),
        gv=vmem((rows, width), BF),
        gb=vmem((rows, width), BF),
        grad_agg=vmem((2 * NP, width, rows // 2 // NP), BF),
        stat=vmem((2, NP, 8, 128), F32),
        small=vmem((8, 8, width), F32),
        zrecv=vmem((5, NQ, width, chunk), BF),
        total_t=vmem((width, chunk), F32),
        stat_ss=dma((NP,)),
        stat_rs=dma((NP,)),
        msg_rs=dma((8, NQ)),
        up_ss=dma((4, NQ)),
        down_ss=dma((4, NQ)),
        y_ss=dma((4, NQ)),
        zx_ss=dma((NQ,)),
        m_zs=dma((4, NQ)),
        m_zr=dma((5, NQ)),
        list_ss=dma((2,)),
        list_rs=dma((2,)),
        gy_ss=dma((2 * NP,)),
        gy_rs=dma((2 * NP,)),
        small_ss=dma((7,)),
        small_rs=dma((8,)),
    )
    for name in ("present", "importance", "proj_w", "proj_b", "pin", "q_w", "q_b", "w_w", "w_b", "cotangent"):
        scratch[name] = vmem(inputs[name].shape, inputs[name].dtype)
    for name, out in outs.items():
        scratch[name] = vmem(out.shape, out.dtype)
    for name in ("gb", "gh"):
        scratch[name + "_ss"] = dma((3, NQ))
        scratch[name + "_rs"] = dma((3, NQ))
    for name, w in (("sh", width), ("sb", bwidth)):
        scratch[name + "_send1"] = vmem((2, NQ, chunk, w), BF)
        scratch[name + "_recv1"] = vmem((2, NQ, chunk, w), BF)
        scratch[name + "_sendx"] = vmem((NQ, chunk, w), BF)
        scratch[name + "_recvx"] = vmem((NQ, chunk, w), BF)
        scratch[name + "_ss"] = dma((3, NQ))
        scratch[name + "_rs"] = dma((3, NQ))
    for name, n in (("ww", width), ("wq", width // 2)):
        for part in ("_yrecv", "_zrecv"):
            scratch[name + part] = vmem((4, n, width), BF)
        scratch[name + "_ss"] = dma((2, 4))
        scratch[name + "_rs"] = dma((2, 4))
    for name in ("wp_send", "wp_recv"):
        scratch[name] = vmem((8, bwidth // 2, width), BF)
    for name in ("wp_ss", "wp_rs"):
        scratch[name] = dma((8,))
    place = pl.BlockSpec(memory_space=pl.ANY)
    whole = pl.BlockSpec(memory_space=pltpu.VMEM)
    names = [n + "_in" for n in inputs] + [n + "_out" for n in outs] + list(scratch)
    got = pl.pallas_call(
        functools.partial(fused_kernel, names=tuple(names)),
        out_shape=list(outs.values()),
        in_specs=[place] * len(inputs),
        out_specs=[place] * len(outs),
        scratch_shapes=list(scratch.values()),
        compiler_params=pltpu.CompilerParams(
            collective_id=1, has_side_effects=True, vmem_limit_bytes=63 << 20
        ),
        cost_estimate=pl.CostEstimate(flops=14 << 30, bytes_accessed=8 << 20, transcendentals=0),
    )(*inputs.values())
    row, one = shape((1, width), F32), shape((1, 1), F32)
    emb, g_pin, g_board, g_proj, g_q, g_w, p_b, q_bias, w_bias, count, weight = pl.pallas_call(
        finish_kernel,
        out_shape=list(outs.values())[:6] + [row, row, row, one, one],
        in_specs=[place] * 6 + [whole],
        out_specs=[place] * 6 + [whole] * 5,
        scratch_shapes=[vmem(out.shape, out.dtype) for out in list(outs.values())[:6]] + [dma((2, 6))],
        cost_estimate=pl.CostEstimate(flops=0, bytes_accessed=5 << 20, transcendentals=0),
    )(*got)
    return (
        emb,
        g_pin,
        g_board,
        g_proj,
        p_b.reshape(width),
        g_q,
        q_bias.reshape(width),
        g_w,
        w_bias.reshape(width),
        count.reshape(()),
        weight.reshape(()),
    )


def silu_slope(value):
    sig = jax.nn.sigmoid(value)
    return sig * (1.0 + value * (1.0 - sig))


def slot_table(nbr_block, alpha_block, start, width):
    offsets = nbr_block - start
    places = lax.broadcasted_iota(jnp.int32, (1, 1, width), 2)
    return jnp.sum(jnp.where(offsets[:, :, None] == places, alpha_block[:, :, None], 0.0), axis=1)


def split_pair(table):
    upper = table.astype(jnp.bfloat16)
    lower = (table - upper.astype(jnp.float32)).astype(jnp.bfloat16)
    return (upper, lower)


def collect_rows(nbrs, alphas, table_all):
    total, columns = table_all.shape
    col_tile = math.gcd(total, 2048)
    count_tiles = total // col_tile
    tiles = table_all.reshape(count_tiles, col_tile, columns)
    rows = nbrs.shape[0]
    row_block = math.gcd(rows, 512)
    count_rows = rows // row_block

    def one_rows(pair):
        nbr_block, alpha_block = pair

        def step(acc, index):
            upper, lower = split_pair(
                slot_table(nbr_block, alpha_block, index * col_tile, col_tile)
            )
            piece = tiles[index]
            acc = acc + jnp.dot(upper, piece, preferred_element_type=jnp.float32)
            return (acc + jnp.dot(lower, piece, preferred_element_type=jnp.float32), None)

        acc, unused = lax.scan(
            step, jnp.zeros((row_block, columns), jnp.float32), jnp.arange(count_tiles)
        )
        return acc

    out = lax.map(
        one_rows,
        (nbrs.reshape(count_rows, row_block, -1), alphas.reshape(count_rows, row_block, -1)),
    )
    return out.reshape(rows, columns)


def spread_rows(grads, nbrs, alphas, base, width):
    rows, columns = grads.shape
    row_block = math.gcd(rows, 512)
    count_rows = rows // row_block
    col_tile = math.gcd(width, 2048)
    count_tiles = width // col_tile
    stacked = (
        grads.reshape(count_rows, row_block, columns),
        nbrs.reshape(count_rows, row_block, -1),
        alphas.reshape(count_rows, row_block, -1),
    )
    tdot = (((0,), (0,)), ((), ()))

    def one_tile(index):

        def step(acc, triple):
            grad_block, nbr_block, alpha_block = triple
            upper, lower = split_pair(
                slot_table(nbr_block, alpha_block, base + index * col_tile, col_tile)
            )
            acc = acc + lax.dot_general(upper, grad_block, tdot, preferred_element_type=jnp.float32)
            return (
                acc + lax.dot_general(lower, grad_block, tdot, preferred_element_type=jnp.float32),
                None,
            )

        acc, unused = lax.scan(step, jnp.zeros((col_tile, columns), jnp.float32), stacked)
        return acc

    out = lax.map(one_tile, jnp.arange(count_tiles))
    return out.reshape(width, columns)


def per_device(
    pin_features,
    board_features,
    is_board,
    neighbours,
    present,
    importance,
    proj_weight,
    proj_bias,
    q_weight,
    q_bias,
    w_weight,
    w_bias,
    cotangent,
):
    local_rows = pin_features.shape[0]
    width = q_weight.shape[0]
    filled = present.astype(jnp.float32) * importance
    alpha = filled / jnp.sum(filled, axis=1, keepdims=True)
    board_mask = (is_board == 1)[:, None]
    stat_terms = (jnp.sum(present.astype(jnp.float32)), jnp.sum(filled))
    stat_totals = lax.psum((stat_terms[0], stat_terms[1]), "rows")
    board_full = lax.all_gather(board_features, "cols", axis=1, tiled=True)
    board_proj = jnp.dot(board_full, proj_weight, preferred_element_type=jnp.float32) + proj_bias
    h_local = jnp.where(board_mask, board_proj, pin_features.astype(jnp.float32)).astype(
        jnp.bfloat16
    )
    h_full = lax.all_gather(h_local, "cols", axis=1, tiled=True)
    v_pre = jnp.dot(h_full, q_weight, preferred_element_type=jnp.float32) + q_bias
    message = jax.nn.silu(v_pre).astype(jnp.bfloat16)
    message_all = lax.all_gather(message, "rows", axis=0, tiled=True)
    agg_local = collect_rows(neighbours, alpha, message_all).astype(jnp.bfloat16)
    agg_full = lax.all_gather(agg_local, "cols", axis=1, tiled=True)
    w_self = w_weight[:width]
    w_agg = w_weight[width:]
    u_pre = (
        jnp.dot(h_full, w_self, preferred_element_type=jnp.float32)
        + jnp.dot(agg_full, w_agg, preferred_element_type=jnp.float32)
        + w_bias
    )
    z_act = jax.nn.silu(u_pre)
    squares = lax.psum(jnp.sum(z_act * z_act, axis=1), "cols")
    scale = lax.rsqrt(squares + 1e-06)[:, None]
    embeddings = (z_act * scale).astype(jnp.bfloat16)
    grad_out = cotangent.astype(jnp.float32)
    inner = lax.psum(jnp.sum(grad_out * z_act, axis=1), "cols")[:, None]
    grad_z = grad_out * scale - z_act * scale * scale * scale * inner
    grad_u = (grad_z * silu_slope(u_pre)).astype(jnp.bfloat16)
    agg_part = lax.dot_general(
        grad_u, w_agg, (((1,), (1,)), ((), ())), preferred_element_type=jnp.float32
    )
    grad_agg = lax.psum_scatter(agg_part, "cols", scatter_dimension=1, tiled=True).astype(
        jnp.bfloat16
    )
    table = spread_rows(grad_agg, neighbours, alpha, 0, message_all.shape[0])
    grad_message = lax.psum_scatter(
        table.astype(jnp.bfloat16), "rows", scatter_dimension=0, tiled=True
    ).astype(jnp.float32)
    grad_v = (grad_message * silu_slope(v_pre)).astype(jnp.bfloat16)
    h_part = lax.dot_general(
        grad_u, w_self, (((1,), (1,)), ((), ())), preferred_element_type=jnp.float32
    )
    h_part = h_part + lax.dot_general(
        grad_v, q_weight, (((1,), (1,)), ((), ())), preferred_element_type=jnp.float32
    )
    grad_h = lax.psum_scatter(
        h_part.astype(jnp.bfloat16), "cols", scatter_dimension=1, tiled=True
    ).astype(jnp.float32)
    grad_pin = jnp.where(board_mask, 0.0, grad_h)
    grad_hb = jnp.where(board_mask, grad_h, 0.0).astype(jnp.bfloat16)
    board_part = lax.dot_general(
        grad_hb, proj_weight, (((1,), (1,)), ((), ())), preferred_element_type=jnp.float32
    )
    grad_board = lax.psum_scatter(
        board_part.astype(jnp.bfloat16), "cols", scatter_dimension=1, tiled=True
    ).astype(jnp.float32)
    tdot = (((0,), (0,)), ((), ()))
    grad_w_local = jnp.concatenate(
        [
            lax.dot_general(h_full, grad_u, tdot, preferred_element_type=jnp.float32),
            lax.dot_general(agg_full, grad_u, tdot, preferred_element_type=jnp.float32),
        ],
        axis=0,
    )
    grad_q_local = lax.dot_general(h_full, grad_v, tdot, preferred_element_type=jnp.float32)
    grad_p_local = lax.dot_general(board_full, grad_hb, tdot, preferred_element_type=jnp.float32)
    grad_w, grad_q, grad_proj = (
        lax.psum_scatter(
            grad_w_local.astype(jnp.bfloat16), "rows", scatter_dimension=0, tiled=True
        ).astype(jnp.float32),
        lax.psum_scatter(
            grad_q_local.astype(jnp.bfloat16), "rows", scatter_dimension=0, tiled=True
        ).astype(jnp.float32),
        lax.psum_scatter(
            grad_p_local.astype(jnp.bfloat16), "rows", scatter_dimension=0, tiled=True
        ).astype(jnp.float32),
    )
    bias_terms = (
        jnp.sum(grad_hb.astype(jnp.float32), axis=0),
        jnp.sum(grad_v.astype(jnp.float32), axis=0),
        jnp.sum(grad_u.astype(jnp.float32), axis=0),
    )
    grad_pb, grad_qb, grad_wb = lax.psum((bias_terms[0], bias_terms[1], bias_terms[2]), "rows")
    all_nodes = local_rows * lax.axis_size("rows")
    mean_count = stat_totals[0] / all_nodes
    mean_weight = stat_totals[1] / (all_nodes * SLOTS)
    return (
        embeddings,
        grad_pin,
        grad_board,
        grad_proj,
        grad_pb,
        grad_q,
        grad_qb,
        grad_w,
        grad_wb,
        mean_count,
        mean_weight,
    )


def solution(mesh):
    in_specs = (
        P("rows", "cols"),
        P("rows", "cols"),
        P("rows"),
        P("rows", None),
        P("rows", None),
        P("rows", None),
        P(None, "cols"),
        P("cols"),
        P(None, "cols"),
        P("cols"),
        P(None, "cols"),
        P("cols"),
        P("rows", "cols"),
    )
    out_specs = (
        P("rows", "cols"),
        P("rows", "cols"),
        P("rows", "cols"),
        P("rows", "cols"),
        P("cols"),
        P("rows", "cols"),
        P("cols"),
        P("rows", "cols"),
        P("cols"),
        P(),
        P(),
    )
    fused = mesh.shape["rows"] == 8 and mesh.shape["cols"] == 4
    return jax.shard_map(
        fused_device if fused else per_device, mesh=mesh, in_specs=in_specs, out_specs=out_specs, check_vma=False
    )
```

```python
import functools
import math
import types

import jax
import jax.numpy as jnp
from jax import lax
from jax.experimental import pallas as pl
from jax.experimental.pallas import tpu as pltpu
from jax.sharding import PartitionSpec as P

SLOTS = 50
MESH = pl.DeviceIdType.MESH
BF = jnp.bfloat16
F32 = jnp.float32
NQ = 4
NP = 2
LO_BITS = 7
LO = 1 << LO_BITS
PIECE = 64
NT = (((1,), (1,)), ((), ()))
TN = (((0,), (0,)), ((), ()))


def dot(a, b):
    return jnp.dot(a, b, preferred_element_type=F32)


def dot_nt(a, b):
    return lax.dot_general(a, b, NT, preferred_element_type=F32)


def dot_tn(a, b):
    return lax.dot_general(a, b, TN, preferred_element_type=F32)


def loop(n, body, unroll=1):
    def step(i, carry):
        body(i)
        return carry

    lax.fori_loop(0, n, step, 0, unroll=unroll)


def row_sums(x):
    y = x[:, :128] + x[:, 128:]
    sums = [
        jnp.sum(y[i * 128 : (i + 1) * 128].T, axis=0, keepdims=True) for i in range(x.shape[0] // 128)
    ]
    return sums[0] if len(sums) == 1 else jnp.concatenate(sums, axis=0)


def down(row):
    return jnp.broadcast_to(row, (128, 128)).T


def down_rows(rows):
    cols = [down(rows[i : i + 1]) for i in range(rows.shape[0])]
    col = cols[0] if len(cols) == 1 else jnp.concatenate(cols, axis=0)
    return jnp.concatenate([col, col], axis=1)


def fused_kernel(*refs, names):
    s = types.SimpleNamespace(**dict(zip(names, refs)))
    r = lax.axis_index("rows")
    c = lax.axis_index("cols")
    z, y = r // 2, r % 2
    x, k = c // 2, c % 2
    rows, width = s.pin.shape
    bwidth = s.boards.shape[2]
    chunk = rows // NQ
    zn = 4
    per_block = rows // LO
    core = (r, x * 2 + 1 - k)
    xp = (r, (1 - x) * 2 + k)
    diagonal = (z * 2 + 1 - y, (1 - x) * 2 + k)
    yp = (z * 2 + 1 - y, c)
    upper = z // 2
    inner = (z % 2) + upper * (1 - 2 * (z % 2))
    zx = z + 1 - 2 * (z % 2)
    zxp = (zx * 2 + y, c)

    def at(q):
        return pl.ds(pl.multiple_of(q * chunk, chunk), chunk)

    def rdma(src, dst, send, recv, dev):
        return pltpu.make_async_remote_copy(
            src_ref=src, dst_ref=dst, send_sem=send, recv_sem=recv, device_id=dev, device_id_type=MESH
        )

    def arrived(ref, sem):
        rdma(ref, ref, sem, sem, core).wait_recv()

    def sent(ref, sem):
        rdma(ref, ref, sem, sem, core).wait_send()

    class Gather:
        def __init__(self, buf, base, ss, rs):
            self.buf, self.base, self.ss, self.rs = buf, base, ss, rs

        def ref(self, col, q):
            return self.buf.at[self.base + col, at(q)]

        def start(self, q):
            own = self.ref(c, q)
            rdma(own, own, self.ss.at[1, q], self.rs.at[1, q], xp).start()
            rdma(own, own, self.ss.at[0, q], self.rs.at[0, q], core).start()

        def forward(self, q):
            got = self.ref((1 - x) * 2 + k, q)
            arrived(got, self.rs.at[1, q])
            rdma(got, got, self.ss.at[2, q], self.rs.at[2, q], core).start()

        def finish(self, q):
            arrived(self.ref(x * 2 + 1 - k, q), self.rs.at[0, q])
            arrived(self.ref((1 - x) * 2 + 1 - k, q), self.rs.at[2, q])

        def drain(self, q):
            for i in range(3):
                sent(self.ref(c, q), self.ss.at[i, q])

    class Scatter:
        def __init__(self, part, name):
            self.part = part
            self.send1, self.recv1 = getattr(s, name + "_send1"), getattr(s, name + "_recv1")
            self.sendx, self.recvx = getattr(s, name + "_sendx"), getattr(s, name + "_recvx")
            self.ss, self.rs = getattr(s, name + "_ss"), getattr(s, name + "_rs")

        def first(self, q):
            for i, xs in ((0, 1 - x), (1, x)):
                self.send1[i, q] = self.part(xs * 2 + 1 - k, q).astype(BF)
                rdma(
                    self.send1.at[i, q], self.recv1.at[i, q], self.ss.at[i, q], self.rs.at[i, q], core
                ).start()

        def second(self, q):
            own = self.part((1 - x) * 2 + k, q)
            arrived(self.recv1.at[0, q], self.rs.at[0, q])
            self.sendx[q] = (own + self.recv1[0, q].astype(F32)).astype(BF)
            rdma(self.sendx.at[q], self.recvx.at[q], self.ss.at[2, q], self.rs.at[2, q], xp).start()

        def third(self, q):
            own = self.part(c, q)
            arrived(self.recv1.at[1, q], self.rs.at[1, q])
            own = own + self.recv1[1, q].astype(F32)
            arrived(self.recvx.at[q], self.rs.at[2, q])
            return own + self.recvx[q].astype(F32)

        def drain(self, q):
            for i in range(2):
                sent(self.send1.at[i, q], self.ss.at[i, q])
            sent(self.sendx.at[q], self.ss.at[2, q])

    class WeightSum:
        def __init__(self, part, name, out, ysend, zsend):
            self.part, self.out = part, out
            self.ysend, self.zsend = ysend, zsend
            self.yrecv, self.zrecv = getattr(s, name + "_yrecv"), getattr(s, name + "_zrecv")
            self.ss, self.rs = getattr(s, name + "_ss"), getattr(s, name + "_rs")

        def first(self):
            def step(d):
                ref = self.ysend(d)
                ref[...] = self.part(d, 1 - y, True).astype(BF)
                rdma(ref, self.yrecv.at[d], self.ss.at[0, d], self.rs.at[0, d], yp).start()

            loop(zn, step, unroll=zn)

        def second(self, at0=0, n=4):
            def step(i):
                d = at0 + i
                own = self.part(d, y)
                arrived(self.yrecv.at[d], self.rs.at[0, d])
                own = own + self.yrecv[d].astype(F32)

                @pl.when(d == z)
                def _():
                    self.out[...] = own

                @pl.when(d != z)
                def _():
                    ref = self.zsend(d)
                    ref[...] = own.astype(BF)
                    rdma(
                        ref, self.zrecv.at[z], self.ss.at[1, d], self.rs.at[1, z], (d * 2 + y, c)
                    ).start()

            loop(n, step)

        def third(self):
            def step(d):
                @pl.when(d != z)
                def _():
                    arrived(self.zrecv.at[d], self.rs.at[1, d])
                    self.out[...] += self.zrecv[d].astype(F32)

            loop(zn, step)

        def drain(self):
            def step(d):
                sent(self.ysend(d), self.ss.at[0, d])

                @pl.when(d != z)
                def _():
                    sent(self.zsend(d), self.ss.at[1, d])

            loop(zn, step)

    class DirectSum:
        def __init__(self, out):
            self.out, self.send, self.recv = out, s.wp_send, s.wp_recv
            self.ss, self.rs = s.wp_ss, s.wp_rs

        def first(self, part):
            n = self.out.shape[0]

            def step(d):
                both = part(d)
                for yy in range(2):
                    block = both[yy * n : (yy + 1) * n]
                    row = d * 2 + yy

                    @pl.when(row == r)
                    def _():
                        self.out[...] = block

                    @pl.when(row != r)
                    def _():
                        ref = self.send.at[row]
                        ref[...] = block.astype(BF)
                        rdma(ref, self.recv.at[r], self.ss.at[row], self.rs.at[r], (row, c)).start()

            loop(zn, step)

        def second(self):
            def step(row):
                @pl.when(row != r)
                def _():
                    arrived(self.recv.at[row], self.rs.at[row])
                    self.out[...] += self.recv[row].astype(F32)

            loop(2 * zn, step)

        def drain(self):
            def step(row):
                @pl.when(row != r)
                def _():
                    sent(self.send.at[row], self.ss.at[row])

            loop(2 * zn, step)

    barrier = pltpu.get_barrier_semaphore()

    def greet(dev):
        pl.semaphore_signal(barrier, inc=1, device_id=dev, device_id_type=MESH)

    near_by = (xp, yp, diagonal, core)
    for dev in near_by:
        greet(dev)

    @pl.when(z < 3)
    def _():
        greet(((z + 1) * 2 + y, c))

    @pl.when(z > 0)
    def _():
        greet(((z - 1) * 2 + y, c))

    boards, own_h = s.boards, s.ha
    in_sem = s.in_sem
    loads = {}
    order = (
        ("board", boards.at[c]),
        ("is_board", s.flags),
        ("proj_w", s.proj_w),
        ("proj_b", s.proj_b),
        ("pin", s.pin),
        ("neighbours", s.numbers),
        ("present", s.present),
        ("importance", s.importance),
        ("q_w", s.q_w),
        ("q_b", s.q_b),
        ("w_w", s.w_w),
        ("w_b", s.w_b),
        ("cotangent", s.cotangent),
    )
    for i, (name, ref) in enumerate(order):
        loads[name] = pltpu.make_async_copy(getattr(s, name + "_in"), ref, in_sem.at[i])
        loads[name].start()

    out_sem = s.out_sem

    def store(i, q, src, dst):
        return pltpu.make_async_copy(src, dst, out_sem.at[i, q])

    gather_b = Gather(boards, 0, s.gb_ss, s.gb_rs)
    gather_h = Gather(own_h, 0, s.gh_ss, s.gh_rs)
    loads["board"].wait()
    pl.semaphore_wait(barrier, len(near_by) + 1 + inner)
    loop(NQ, gather_b.start)

    mask = s.mask
    loads["is_board"].wait()
    flags = s.flags[...].astype(F32)
    for i in range(rows // 128):
        mask[i * 128 : (i + 1) * 128] = down(flags[i : i + 1])

    half = rows // 2
    padded = s.padded
    list_ss, list_rs = s.list_ss, s.list_rs

    quarter = rows // 4

    def lay(ref):
        for t in range(2):
            for i in range(quarter // 128):
                a, b = 2 * t * quarter + i * 128, (2 * t + 1) * quarter + i * 128
                ref[t, i * 128 : (i + 1) * 128] = jnp.concatenate(
                    [padded[:, a : a + 128], padded[:, b : b + 128]], axis=0
                ).T

    def lend_list(i):
        src, dst = ((s.numbers, s.numbers2), (s.alpha, s.alpha2))[i]
        return rdma(src, dst, list_ss.at[i], list_rs.at[i], yp)

    def prepare():
        for name in ("neighbours", "present", "importance"):
            loads[name].wait()
        lend_list(0).start()
        present = s.present[...].astype(F32)
        filled = present * s.importance[...]
        padded[SLOTS:] = jnp.zeros((padded.shape[0] - SLOTS, rows), F32)
        padded[:SLOTS] = filled / jnp.sum(filled, axis=0, keepdims=True)
        s.alpha[...] = padded[...].astype(BF)
        lend_list(1).start()
        lay(s.weight)
        small = s.small
        small[r] = jnp.zeros(small.shape[1:], F32)
        small[r, 3:4] = jnp.concatenate(
            [
                jnp.broadcast_to(jnp.sum(present).reshape(1, 1), (1, 128)),
                jnp.broadcast_to(jnp.sum(filled).reshape(1, 1), (1, 128)),
            ],
            axis=1,
        )
        numbers = s.numbers[...]
        padded[:SLOTS] = (numbers >> LO_BITS).astype(F32)
        lay(s.high)
        padded[:SLOTS] = (numbers & (LO - 1)).astype(F32)
        lay(s.low)

    def prepare2():
        for i in range(2):
            lend_list(i).wait_recv()
        numbers = s.numbers2[...]
        high = numbers >> LO_BITS
        place = (high // (2 * per_block)) * per_block + high % per_block
        padded[:SLOTS] = jnp.where((high // per_block) % 2 == y, place, -1).astype(F32)
        lay(s.high2)
        padded[:SLOTS] = (numbers & (LO - 1)).astype(F32)
        lay(s.low2)
        padded[...] = s.alpha2[...].astype(F32)
        lay(s.weight2)

    def mask_of(q):
        m = mask[at(q)] > 0.5
        return jnp.concatenate([m, m], axis=1)

    table, stage = s.table, s.stage
    pitch = stage.shape[0] // 64
    piece_rows = PIECE // 4

    def build(i, lists, table):
        n_high = 2 * table.shape[0]
        iota = lax.broadcasted_iota(jnp.int32, (128, 128), 0).astype(F32).astype(BF)
        front = lax.broadcasted_iota(jnp.int32, (16, 128), 1) < 64
        zero, one = jnp.zeros((), BF), jnp.ones((), BF)

        def tiles(v, n):
            return jnp.concatenate([v] * n, axis=0)

        zeros = jnp.zeros((n_high, 128), BF)
        n = n_high // 16

        def four(j):
            p = i * piece_rows + j
            weights, places = [], []
            for t in range(2):

                def row(ref):
                    return jnp.broadcast_to(ref[t, pl.ds(p, 1), :], (16, 128))

                hi, lo, al = row(lists[0]).astype(BF), row(lists[1]).astype(BF), row(lists[2])
                places.append(jnp.where(tiles(lo, 8) == iota, one, zero))
                same = tiles(hi, n) == iota[:n_high]
                for a in (jnp.where(front, al, 0.0), jnp.where(front, 0.0, al)):
                    w = jnp.where(same, tiles(a.astype(BF), n), zero)
                    weights.append(jnp.concatenate([w, zeros] if t == 0 else [zeros, w], axis=1))
            out = dot_nt(jnp.concatenate(weights, axis=0), jnp.concatenate(places, axis=1))
            for g in range(4):
                stage[pl.ds(j + g * piece_rows, n_high, stride=pitch), :] = out[
                    g * n_high : (g + 1) * n_high
                ]

        loop(piece_rows, four, unroll=16)

        def convert(h):
            for f in range(2):
                base = (2 * h + f) * pitch
                for g in range(4):
                    table[
                        h,
                        pl.ds(pl.multiple_of(i * piece_rows + g * quarter, 16), piece_rows),
                        f * 128 : (f + 1) * 128,
                    ] = stage[
                        pl.ds(pl.multiple_of(base + g * piece_rows, 8), piece_rows), :
                    ].astype(BF)

        loop(table.shape[0], convert, unroll=4)

    lists1 = (s.high, s.low, s.weight)
    lists2 = (s.high2, s.low2, s.weight2)
    table2 = s.table2

    def piece(i):
        build(i, lists1, table)

    def piece2(i):
        build(i, lists2, table2)

    n_pieces = rows // PIECE

    message, v_pre = s.message, s.v_pre

    def make_h(q):
        lines = at(q)
        b01 = jnp.concatenate([boards[0, lines], boards[1, lines]], axis=1)
        b23 = jnp.concatenate([boards[2, lines], boards[3, lines]], axis=1)
        proj = dot(b01, s.proj_w[: 2 * bwidth]) + dot(b23, s.proj_w[2 * bwidth :]) + s.proj_b[...]
        own_h[c, lines] = jnp.where(mask_of(q), proj, s.pin[lines].astype(F32)).astype(BF)

    def block(zb, yb, q):
        return message.at[zb * 2 + yb, q]

    def send_up(zb, q):
        ref = block(zb, y, q)
        rdma(ref, ref, s.up_ss.at[zb, q], s.msg_rs.at[zb * 2 + y, q], ((z + 1) * 2 + y, c)).start()

    def send_down(zb, q):
        ref = block(zb, y, q)
        rdma(ref, ref, s.down_ss.at[zb, q], s.msg_rs.at[zb * 2 + y, q], ((z - 1) * 2 + y, c)).start()

    def send_y(zb, q):
        ref = block(zb, y, q)
        rdma(ref, ref, s.y_ss.at[zb, q], s.msg_rs.at[zb * 2 + y, q], yp).start()

    def make_message(q):
        lines = at(q)
        acc = dot(own_h[0, lines], s.q_w[:width])
        for i in range(1, 4):
            acc = acc + dot(own_h[i, lines], s.q_w[i * width : (i + 1) * width])
        v = acc + s.q_b[...]
        v_pre[lines] = v
        message[r, q] = (v * jax.nn.sigmoid(v)).astype(BF)

        @pl.when(z < 3)
        def _():
            send_up(z, q)

        @pl.when(z > 0)
        def _():
            send_down(z, q)

        send_y(z, q)

    prepare()
    for name in ("proj_w", "proj_b", "pin"):
        loads[name].wait()

    def board_phase(q):
        gather_b.forward(q)
        gather_b.finish(q)
        make_h(q)
        gather_h.start(q)

    piece(0)
    loop(NQ, board_phase)
    early = 3
    loop(early - 1, lambda i: piece(1 + i))

    half = rows // 2
    sub = half // NP
    own_half = pl.ds(pl.multiple_of(x * half, half), half)
    their_half = pl.ds(pl.multiple_of((1 - x) * half, half), half)
    lend_ss, lend_rs = s.lend_ss, s.lend_rs
    wide = 4 * width

    def lends():
        return (
            (s.w_w.at[:wide], s.w2.at[:wide]),
            (s.w_b, s.w_b2),
            (s.w_w.at[wide:], s.w2.at[wide:]),
            (s.cotangent.at[their_half], s.cotangent2),
        )

    def lend(i):
        src, dst = lends()[i]
        return rdma(src, dst, lend_ss.at[i], lend_rs.at[i], xp)

    for name in ("w_w", "w_b", "cotangent"):
        loads[name].wait()
    for i in range(4):
        lend(i).start()
    loads["q_w"].wait()
    loads["q_b"].wait()

    def message_phase(q):
        gather_h.forward(q)
        gather_h.finish(q)
        make_message(q)
        piece(early + q)

        @pl.when(q % 2 == 0)
        def _():
            piece(early + NQ + q // 2)

    loop(NQ, message_phase)
    built = early + NQ + NQ // 2

    u_pre = s.u_pre

    def part_of(i):
        return pl.ds(pl.multiple_of(i * sub, sub), sub)

    def mine(i):
        return pl.ds(pl.multiple_of(x * half + i * sub, sub), sub)

    def theirs(i):
        return pl.ds(pl.multiple_of((1 - x) * half + i * sub, sub), sub)

    def u_from_h(i):
        for n, w, b in ((0, s.w_w, s.w_b), (1, s.w2, s.w_b2)):
            acc = dot(own_h[0, mine(i)], w[:width])
            for m in range(1, 4):
                acc = acc + dot(own_h[m, mine(i)], w[m * width : (m + 1) * width])
            u_pre[n, part_of(i)] = acc + b[...]

    agg = s.grad_pin
    parts = rows // chunk

    def add(b, first, n):
        for i in range(parts):
            lines = slice(i * chunk, (i + 1) * chunk)
            acc = agg[lines]
            for q in range(first, first + n):
                acc = acc + dot(table[b * NQ + q, lines], message[b, q])
            agg[lines] = acc

    def over_y(zb, q):
        @pl.when((zb != zx) | ((inner == 0) & (q < NQ // 2)))
        def _():
            send_y(zb, q)

    def send_zx(q):
        ref = block(z, 1 - y, q)
        rdma(ref, ref, s.zx_ss.at[q], s.msg_rs.at[z * 2 + 1 - y, q], zxp).start()

    def at_z(zb):
        return (zb >= 0) & (zb <= 3)

    n_second = 3 * NQ
    n_second2 = n_pieces // 2
    steps = n_pieces - built

    def second_phase(i):
        t, q = 1 + i // NQ, i % NQ

        @pl.when(z - t >= 0)
        def _():
            arrived(block(z - t, y, q), s.msg_rs.at[(z - t) * 2 + y, q])

            @pl.when(z < 3)
            def _():
                send_up(z - t, q)

            over_y(z - t, q)

        @pl.when(z + t <= 3)
        def _():
            arrived(block(z + t, y, q), s.msg_rs.at[(z + t) * 2 + y, q])

            @pl.when(z > 0)
            def _():
                send_down(z + t, q)

            over_y(z + t, q)

        @pl.when(t == 1)
        def _():
            arrived(block(z, 1 - y, q), s.msg_rs.at[z * 2 + 1 - y, q])

            @pl.when(inner == 0)
            def _():
                send_zx(q)

        @pl.when((t == 3) & (inner == 1) & (q >= NQ // 2))
        def _():
            send_zx(q)

        @pl.when(i < steps)
        def _():
            piece(built + i)

        @pl.when(i == 0)
        def _():
            prepare2()

        @pl.when((i > 0) & (i < 1 + n_second2))
        def _():
            loop(2, lambda n: piece2(2 * (i - 1) + n))

        @pl.when(i == steps)
        def _():
            agg[...] = jnp.zeros_like(agg)
            lend(0).wait_recv()
            lend(1).wait_recv()

        @pl.when(i >= n_second - NP)
        def _():
            u_from_h(i - (n_second - NP))

        @pl.when((i >= n_second - 5) & (i < n_second))
        def _():
            n = i - (n_second - 5)
            zb = z + jnp.where(n == 0, 0, jnp.where(n == 1, -1, jnp.where(n == 2, 1, jnp.where(n == 3, -2, 2))))

            @pl.when(at_z(zb))
            def _():
                add(zb * 2 + y, 0, NQ)

    loop(n_second, second_phase)

    add(z * 2 + 1 - y, 0, NQ)

    @pl.when(inner == 0)
    def _():
        add((3 - z) * 2 + y, 0, NQ)

    def add_arriving(zb, first, n):
        b = zb * 2 + 1 - y
        loop(n, lambda q: arrived(message.at[b, first + q], s.msg_rs.at[b, first + q]))
        add(b, first, n)

    add_arriving(zx, 0, NQ // 2)
    add_arriving(2 - upper, 0, NQ)
    for q in range(NQ):
        blocks = [3 * (1 - upper) * 2 + 1 - y] + ([zx * 2 + 1 - y] if q >= NQ // 2 else [])
        for b in blocks:
            arrived(message.at[b, q], s.msg_rs.at[b, q])
        for i in range(parts):
            lines = slice(i * chunk, (i + 1) * chunk)
            acc = agg[lines]
            for b in blocks:
                acc = acc + dot(table[b * NQ + q, lines], message[b, q])
            if q < NQ - 1:
                agg[lines] = acc
            else:
                own_h[4 + c, lines] = acc.astype(BF)

    gu, gv, gb, gu2 = s.gu, s.gv, s.gb, s.gu2
    stat, stat_ss, stat_rs = s.stat, s.stat_ss, s.stat_rs
    ga_ss, ga_rs = s.ga_ss, s.ga_rs
    other_x = (1 - x) * 2 + k

    def agg_ref(col, lines):
        return own_h.at[4 + col, lines]

    def agg_start(i):
        a, b = agg_ref(c, theirs(i)), agg_ref(c, mine(i))
        rdma(a, a, ga_ss.at[1, i], ga_rs.at[1, i], xp).start()
        rdma(b, b, ga_ss.at[0, i], ga_rs.at[0, i], core).start()

    def agg_forward(i):
        got = agg_ref(other_x, mine(i))
        arrived(got, ga_rs.at[1, i])
        rdma(got, got, ga_ss.at[2, i], ga_rs.at[2, i], core).start()

    def agg_finish(i):
        arrived(agg_ref(x * 2 + 1 - k, mine(i)), ga_rs.at[0, i])
        arrived(agg_ref((1 - x) * 2 + 1 - k, mine(i)), ga_rs.at[2, i])

    def rest_start():
        a, b = agg_ref(c, own_half), agg_ref(c, their_half)
        rdma(a, a, ga_ss.at[1, NP], ga_rs.at[1, NP], xp).start()
        rdma(b, b, ga_ss.at[0, NP], ga_rs.at[0, NP], core).start()

    def rest_forward():
        got = agg_ref(other_x, their_half)
        arrived(got, ga_rs.at[1, NP])
        rdma(got, got, ga_ss.at[2, NP], ga_rs.at[2, NP], core).start()

    def rest_finish():
        arrived(agg_ref(x * 2 + 1 - k, their_half), ga_rs.at[0, NP])
        arrived(agg_ref((1 - x) * 2 + 1 - k, their_half), ga_rs.at[2, NP])

    loop(NP, agg_start)
    lend(2).wait_recv()
    lend(3).wait_recv()

    def gradients(i):
        return s.cotangent[mine(i)].astype(F32), s.cotangent2[part_of(i)].astype(F32)

    def make_u(i):
        us = [u_pre[n, part_of(i)] for n in range(2)]
        for m in range(4):
            a = own_h[4 + m, mine(i)]
            us = [u + dot(a, w[(4 + m) * width : (5 + m) * width]) for u, w in zip(us, (s.w_w, s.w2))]
        squares, inners = 0.0, 0.0
        for n, (u, g) in enumerate(zip(us, gradients(i))):
            u_pre[n, part_of(i)] = u
            zz = u * jax.nn.sigmoid(u)
            squares = squares + zz * zz
            inners = inners + g * zz
        pad = jnp.zeros((8 - 2 * sub // 128, 128), F32)
        stat[0, i] = jnp.concatenate([row_sums(squares), row_sums(inners), pad], axis=0)
        rdma(stat.at[0, i], stat.at[1, i], stat_ss.at[i], stat_rs.at[i], core).start()

    def make_gu(i):
        arrived(stat.at[1, i], stat_rs.at[i])
        total = stat[0, i] + stat[1, i]
        n_rows = sub // 128
        rr = lax.rsqrt(total[:n_rows] + 1e-6)
        scale = down_rows(rr)
        pull = down_rows(rr * rr * rr * total[n_rows : 2 * n_rows])
        for n, (g, emb, grad) in enumerate(
            zip(gradients(i), (s.embeddings, s.emb2), (gu, gu2))
        ):
            u = u_pre[n, part_of(i)]
            sig = jax.nn.sigmoid(u)
            zz = u * sig
            lines = mine(i) if n == 0 else part_of(i)
            emb[lines] = (zz * scale).astype(BF)
            grad[lines] = ((g * scale - zz * pull) * (sig * (1.0 + u * (1.0 - sig)))).astype(BF)

    def agg_part(col, i):
        lines = pl.ds(pl.multiple_of((4 + col) * width, width), width)
        return dot_nt(gu[mine(i)], s.w_w[lines, :]) + dot_nt(gu2[part_of(i)], s.w2[lines, :])

    grad_agg, grad_agg2 = s.grad_agg, s.grad_agg2
    sa_send, sa_recv, sa_x, sa_ss, sa_rs = s.sa_send, s.sa_recv, s.sa_x, s.sa_ss, s.sa_rs

    def agg_first(i):
        for n, xs in ((0, 1 - x), (1, x)):
            sa_send[n, i] = agg_part(xs * 2 + 1 - k, i).astype(BF)
            rdma(sa_send.at[n, i], sa_recv.at[n, i], sa_ss.at[n, i], sa_rs.at[n, i], core).start()

    def agg_second(i):
        own = agg_part(other_x, i)
        arrived(sa_recv.at[0, i], sa_rs.at[0, i])
        sa_x[i] = (own + sa_recv[0, i].astype(F32)).T.astype(BF)
        if i == NP - 1:
            to, there = grad_agg2.at[x * NP + i], (1 - x) * NP + i
            rdma(sa_x.at[i], to, s.gy_ss.at[there], s.gy_rs.at[x * NP + i], diagonal).start()
        rdma(sa_x.at[i], grad_agg.at[x * NP + i], sa_ss.at[2, i], sa_rs.at[2, i], xp).start()

    def agg_third(i):
        own = agg_part(c, i)
        arrived(sa_recv.at[1, i], sa_rs.at[1, i])
        grad_agg[x * NP + i] = (own + sa_recv[1, i].astype(F32)).T.astype(BF)
        agg_over_y(x * NP + i)

    def agg_over_y(i):
        rdma(grad_agg.at[i], grad_agg2.at[i], s.gy_ss.at[i], s.gy_rs.at[i], yp).start()

    def room(at_block, n):
        return [lambda d, b=b, n=n: message.at[b, d, pl.ds(0, n)] for b in (at_block, at_block + 1)]

    def room_narrow(at_block, n):
        return [lambda d, i=i: message.at[at_block, d, pl.ds(i * n, n)] for i in range(2)]

    sum_w = WeightSum(lambda d, yy, first=False: dot_tn(own_h[d * 2 + yy], gu[...]), "ww", s.grad_w, *room(4, width))

    def half_phases():
        for i in range(NP):
            agg_forward(i)
            if i > 0:
                make_gu(i - 1)
                agg_first(i - 1)
            agg_finish(i)
            make_u(i)
            if i > 0:
                agg_second(i - 1)
                agg_third(i - 1)
        make_gu(NP - 1)
        agg_first(NP - 1)
        agg_second(NP - 1)
        agg_third(NP - 1)

    half_phases()

    def give(n):
        src, dst = ((gu2, gu.at[own_half]), (s.emb2, s.embeddings.at[own_half]))[n]
        return rdma(src, dst, s.give_ss.at[n], s.give_rs.at[n], xp)

    def give_back(n):
        ref = (gu, s.embeddings)[n].at[their_half]
        return rdma(ref, ref, s.give_ss.at[n], s.give_rs.at[n], xp)

    give(0).start()
    rest_start()
    give(1).start()
    def pass_on(i):
        arrived(grad_agg.at[(1 - x) * NP + i], sa_rs.at[2, i])
        if i < NP - 1:
            agg_over_y((1 - x) * NP + i)

    for i in range(NP):
        pass_on(i)
    loop(2 * NP, lambda i: arrived(grad_agg2.at[i], s.gy_rs.at[i]))

    def sent_messages(q):
        @pl.when(z < 3)
        def _():
            sent(block(z, y, q), s.up_ss.at[z, q])

        @pl.when(z > 0)
        def _():
            sent(block(z, y, q), s.down_ss.at[z, q])

        for t in range(1, 4):
            @pl.when((z - t >= 0) & (z < 3))
            def _():
                sent(block(z, y, q), s.up_ss.at[z - t, q])

            @pl.when((z + t <= 3) & (z > 0))
            def _():
                sent(block(z, y, q), s.down_ss.at[z + t, q])

        for zb in range(4):
            @pl.when((zb != zx) | ((inner == 0) & (q < NQ // 2)))
            def _():
                sent(block(z, y, q), s.y_ss.at[zb, q])

        @pl.when((inner == 0) | (q >= NQ // 2))
        def _():
            sent(block(z, y, q), s.zx_ss.at[q])

    loop(NQ, sent_messages)

    zsend, zrecv = message, s.zrecv
    m_zs, m_zr = s.m_zs, s.m_zr
    adjust = (0, 0, -1, 1)

    def dest(j):
        base = 3 - j + inner * adjust[j]
        return base + upper * (3 - 2 * base)

    each = 2 * NP // NQ

    def sum_of(terms):
        total = None
        for term in terms:
            total = term if total is None else total + term
        return total

    def spread(d, q):
        own, other = (d * 2 + y) * NQ + q, d * NQ + q

        def grads(ref, i):
            return jnp.concatenate([ref[m] for m in range(i * each, (i + 1) * each)], axis=1)

        return sum_of(
            dot(grads(ref, i), tab[b, at(i)])
            for ref, tab, b in ((grad_agg, table, own), (grad_agg2, table2, other))
            for i in range(NQ)
        )

    def along(j, q):
        d = dest(j)
        step = 1 - 2 * upper
        if j == 2:
            step = step * (1 - 2 * inner)
        is_dest = (0, inner, 1)[j]
        slot = d + is_dest * ((1 - step) // 2) * (4 - d)
        own = spread(d, q)

        @pl.when(inner == 0)
        def _():
            zsend[d, q] = own.astype(BF)

        @pl.when(inner == 1)
        def _():
            arrived(zrecv.at[d, q], m_zr.at[d, q])
            zsend[d, q] = (own + zrecv[d, q].astype(F32)).astype(BF)

        rdma(
            zsend.at[d, q], zrecv.at[slot, q], m_zs.at[d, q], m_zr.at[slot, q], ((z + step) * 2 + y, c)
        ).start()

    loop(NQ, lambda q: along(0, q))

    @pl.when(inner == 0)
    def _():
        for j in (1, 2):
            loop(NQ, lambda q, j=j: along(j, q))

    give_back(0).wait_recv()
    rest_forward()
    rest_finish()
    sum_w.first()

    @pl.when(inner == 1)
    def _():
        def both_ways(q):
            along(2, q)
            along(1, q)

        loop(NQ, both_ways)

    give_back(1).wait_recv()
    store(0, 0, s.embeddings, s.embeddings_out).start()

    total_t = s.total_t

    def make_gv(q):
        total_t[...] = spread(z, q)

        @pl.when(z > 0)
        def _():
            arrived(zrecv.at[z, q], m_zr.at[z, q])
            total_t[...] += zrecv[z, q].astype(F32)

        @pl.when(z < 3)
        def _():
            arrived(zrecv.at[4, q], m_zr.at[4, q])
            total_t[...] += zrecv[4, q].astype(F32)

        v = v_pre[at(q)]
        sig = jax.nn.sigmoid(v)
        gv[at(q)] = (total_t[...].T * (sig * (1.0 + v * (1.0 - sig)))).astype(BF)

    def h_part(col, q):
        lines = pl.ds(pl.multiple_of(col * width, width), width)
        return dot_nt(gu[at(q)], s.w_w[lines, :]) + dot_nt(gv[at(q)], s.q_w[lines, :])

    def b_part(col, q):
        lines = pl.ds(pl.multiple_of(col * bwidth, bwidth), bwidth)
        return dot_nt(gb[at(q)], s.proj_w[lines, :])

    scatter_h, scatter_b = Scatter(h_part, "sh"), Scatter(b_part, "sb")


    def q_part(d, yy, first=False):
        n = width // 2
        keep = u_pre.at[0, pl.ds(d * n, n)]
        if not first:
            return keep[...]
        both = dot_tn(own_h[d], gv[...])
        keep[...] = jnp.where(y == 0, both[:n], both[n:])
        return jnp.where(y == 0, both[n:], both[:n])

    sum_q = WeightSum(q_part, "wq", s.grad_q, *room_narrow(6, width // 2))
    sum_p = DirectSum(s.grad_p)
    small, small_ss, small_rs = s.small, s.small_ss, s.small_rs

    def column_sums(i, ref):
        small[r, i : i + 1] = jnp.sum(ref[...].astype(F32), axis=0, keepdims=True)

    def send_small():
        column_sums(0, gb)
        for d in range(1, 8):
            rdma(
                small.at[r], small.at[r], small_ss.at[d - 1], small_rs.at[r], ((r + d) % 8, c)
            ).start()

    def finish_board(q):
        s.grad_board[at(q)] = scatter_b.third(q)
        store(2, q, s.grad_board.at[at(q)], s.grad_board_out.at[at(q)]).start()

    def fourth_phase(t):
        @pl.when(t < NQ)
        def _():
            make_gv(t)
            scatter_h.first(t)

        @pl.when((t >= 3) & (t < NQ + 2))
        def _():
            scatter_b.second(t - 3)

        @pl.when(t == NQ - 1)
        def _():
            scatter_h.second(t)
            sum_q.first()

        @pl.when((t >= 2) & (t < NQ + 2))
        def _():
            q = t - 2
            g = scatter_h.third(q)
            m = mask_of(q)
            gb[at(q)] = jnp.where(m, g, 0.0).astype(BF)
            s.grad_pin[at(q)] = jnp.where(m, 0.0, g)

            @pl.when(t == NQ + 1)
            def _():
                sum_p.first(lambda d: dot_tn(boards[d], gb[...]))

            scatter_b.first(q)
            store(1, q, s.grad_pin.at[at(q)], s.grad_pin_out.at[at(q)]).start()

        @pl.when(t < NQ - 1)
        def _():
            scatter_h.second(t)

        @pl.when(t == 1)
        def _():
            sum_w.second()

        @pl.when(t == NQ)
        def _():
            column_sums(1, gv)
            column_sums(2, gu)

    loop(NQ + 2, fourth_phase)
    scatter_b.second(NQ - 1)
    send_small()
    sum_q.second()
    for q in range(NQ - 1):
        finish_board(q)
    sum_w.third()
    store(0, 1, s.grad_w, s.grad_w_out).start()
    finish_board(NQ - 1)
    sum_q.third()
    store(0, 2, s.grad_q, s.grad_q_out).start()
    for d in range(1, 8):
        other = (r + d) % 8
        arrived(small.at[other], small_rs.at[other])
    total = small[0]
    for i in range(1, 8):
        total = total + small[i]
    nodes = rows * 8
    per = jnp.concatenate(
        [jnp.full((1, 128), 1.0 / nodes, F32), jnp.full((1, 128), 1.0 / (nodes * SLOTS), F32)], axis=1
    )
    s.sums[...] = total
    s.sums[3:4] = total[3:4] * per
    store(0, 3, s.sums, s.sums_out).start()
    sum_p.second()
    store(3, 0, s.grad_p, s.grad_p_out).start()

    def drain(q):
        gather_b.drain(q)
        gather_h.drain(q)
        scatter_h.drain(q)
        scatter_b.drain(q)
        store(1, q, s.grad_pin.at[at(q)], s.grad_pin_out.at[at(q)]).wait()
        store(2, q, s.grad_board.at[at(q)], s.grad_board_out.at[at(q)]).wait()
        for d in range(4):
            @pl.when(d != z)
            def _():
                sent(zsend.at[d, q], m_zs.at[d, q])

    loop(NQ, drain)

    def drain_half(i):
        for n in range(3):
            sent(agg_ref(c, mine(i)), ga_ss.at[n, i])
        for n in range(2):
            sent(sa_send.at[n, i], sa_ss.at[n, i])
        sent(sa_x.at[i], sa_ss.at[2, i])
        sent(stat.at[0, i], stat_ss.at[i])

    loop(NP, drain_half)
    for n in range(3):
        sent(agg_ref(c, own_half), ga_ss.at[n, NP])
    for n in range(4):
        lend(n).wait_send()
    for n in range(2):
        lend_list(n).wait_send()
    loop(2 * NP, lambda i: sent(grad_agg.at[i], s.gy_ss.at[i]))
    for n in range(2):
        give(n).wait_send()
    sum_w.drain()
    sum_q.drain()
    sum_p.drain()
    for d in range(7):
        sent(small.at[r], small_ss.at[d])
    for i, (n, name) in enumerate(
        ((0, "embeddings"), (0, "grad_w"), (0, "grad_q"), (0, "sums"), (3, "grad_p"))
    ):
        store(n, i % 4, getattr(s, name), getattr(s, name + "_out")).wait()


def finish_kernel(*refs):
    ins, sums, outs, small, held, sem = refs[:6], refs[6], refs[7:13], refs[13:18], refs[18:24], refs[24]
    first = [pltpu.make_async_copy(a, b, sem.at[0, i]) for i, (a, b) in enumerate(zip(ins, held))]
    second = [pltpu.make_async_copy(a, b, sem.at[1, i]) for i, (a, b) in enumerate(zip(held, outs))]
    for copy in first:
        copy.start()
    for i in range(3):
        small[i][...] = sums[i : i + 1]
    small[3][...] = sums[3:4, 0:1]
    small[4][...] = sums[3:4, 128:129]
    for a, b in zip(first, second):
        a.wait()
        b.start()
    for copy in second:
        copy.wait()


def fused_device(
    pin, board, is_board, neighbours, present, importance, proj_w, proj_b, q_w, q_b, w_w, w_b, cotangent
):
    rows, width = pin.shape
    bwidth = board.shape[1]
    chunk = rows // NQ
    nodes = rows * 8
    inputs = dict(
        board=board,
        is_board=is_board.reshape(rows // 128, 128),
        proj_w=proj_w,
        proj_b=proj_b.reshape(1, width),
        pin=pin,
        neighbours=neighbours.T,
        present=present.T,
        importance=importance.T,
        q_w=q_w,
        q_b=q_b.reshape(1, width),
        w_w=w_w,
        w_b=w_b.reshape(1, width),
        cotangent=cotangent,
    )
    shape = jax.ShapeDtypeStruct
    outs = dict(
        embeddings=shape((rows, width), BF),
        grad_pin=shape((rows, width), F32),
        grad_board=shape((rows, bwidth), F32),
        grad_p=shape((bwidth * 4 // 8, width), F32),
        grad_q=shape((width * 4 // 8, width), F32),
        grad_w=shape((2 * width * 4 // 8, width), F32),
        sums=shape((8, width), F32),
    )
    vmem, dma = pltpu.VMEM, pltpu.SemaphoreType.DMA
    scratch = dict(
        in_sem=dma((len(inputs),)),
        out_sem=dma((4, NQ)),
        flags=vmem((rows // 128, 128), jnp.int32),
        numbers=vmem((SLOTS, rows), jnp.int32),
        numbers2=vmem((SLOTS, rows), jnp.int32),
        alpha=vmem((64, rows), BF),
        alpha2=vmem((64, rows), BF),
        padded=vmem((64, rows), F32),
        table2=vmem((nodes // 2 // chunk, rows, chunk), BF),
        high2=vmem((2, rows // 4, 128), F32),
        low2=vmem((2, rows // 4, 128), F32),
        weight2=vmem((2, rows // 4, 128), F32),
        grad_agg2=vmem((2 * NP, width, rows // 2 // NP), BF),
        table=vmem((nodes // chunk, rows, chunk), BF),
        stage=vmem((64 * (PIECE + 8), 128), F32),
        high=vmem((2, rows // 4, 128), F32),
        low=vmem((2, rows // 4, 128), F32),
        weight=vmem((2, rows // 4, 128), F32),
        mask=vmem((rows, 128), F32),
        boards=vmem((4, rows, bwidth), BF),
        ha=vmem((8, rows, width), BF),
        message=vmem((8, NQ, chunk, width), BF),
        v_pre=vmem((rows, width), F32),
        u_pre=vmem((2, rows // 2, width), F32),
        w2=vmem(w_w.shape, BF),
        w_b2=vmem((1, width), F32),
        cotangent2=vmem((rows // 2, width), BF),
        gu2=vmem((rows // 2, width), BF),
        emb2=vmem((rows // 2, width), BF),
        sa_send=vmem((2, NP, rows // 2 // NP, width), BF),
        sa_recv=vmem((2, NP, rows // 2 // NP, width), BF),
        sa_x=vmem((NP, width, rows // 2 // NP), BF),
        sa_ss=dma((3, NP)),
        sa_rs=dma((3, NP)),
        ga_ss=dma((3, NP + 1)),
        ga_rs=dma((3, NP + 1)),
        lend_ss=dma((4,)),
        lend_rs=dma((4,)),
        give_ss=dma((2,)),
        give_rs=dma((2,)),
        gu=vmem((rows, width), BF),
        gv=vmem((rows, width), BF),
        gb=vmem((rows, width), BF),
        grad_agg=vmem((2 * NP, width, rows // 2 // NP), BF),
        stat=vmem((2, NP, 8, 128), F32),
        small=vmem((8, 8, width), F32),
        zrecv=vmem((5, NQ, width, chunk), BF),
        total_t=vmem((width, chunk), F32),
        stat_ss=dma((NP,)),
        stat_rs=dma((NP,)),
        msg_rs=dma((8, NQ)),
        up_ss=dma((4, NQ)),
        down_ss=dma((4, NQ)),
        y_ss=dma((4, NQ)),
        zx_ss=dma((NQ,)),
        m_zs=dma((4, NQ)),
        m_zr=dma((5, NQ)),
        list_ss=dma((2,)),
        list_rs=dma((2,)),
        gy_ss=dma((2 * NP,)),
        gy_rs=dma((2 * NP,)),
        small_ss=dma((7,)),
        small_rs=dma((8,)),
    )
    for name in ("present", "importance", "proj_w", "proj_b", "pin", "q_w", "q_b", "w_w", "w_b", "cotangent"):
        scratch[name] = vmem(inputs[name].shape, inputs[name].dtype)
    for name, out in outs.items():
        scratch[name] = vmem(out.shape, out.dtype)
    for name in ("gb", "gh"):
        scratch[name + "_ss"] = dma((3, NQ))
        scratch[name + "_rs"] = dma((3, NQ))
    for name, w in (("sh", width), ("sb", bwidth)):
        scratch[name + "_send1"] = vmem((2, NQ, chunk, w), BF)
        scratch[name + "_recv1"] = vmem((2, NQ, chunk, w), BF)
        scratch[name + "_sendx"] = vmem((NQ, chunk, w), BF)
        scratch[name + "_recvx"] = vmem((NQ, chunk, w), BF)
        scratch[name + "_ss"] = dma((3, NQ))
        scratch[name + "_rs"] = dma((3, NQ))
    for name, n in (("ww", width), ("wq", width // 2)):
        for part in ("_yrecv", "_zrecv"):
            scratch[name + part] = vmem((4, n, width), BF)
        scratch[name + "_ss"] = dma((2, 4))
        scratch[name + "_rs"] = dma((2, 4))
    for name in ("wp_send", "wp_recv"):
        scratch[name] = vmem((8, bwidth // 2, width), BF)
    for name in ("wp_ss", "wp_rs"):
        scratch[name] = dma((8,))
    place = pl.BlockSpec(memory_space=pl.ANY)
    whole = pl.BlockSpec(memory_space=pltpu.VMEM)
    names = [n + "_in" for n in inputs] + [n + "_out" for n in outs] + list(scratch)
    got = pl.pallas_call(
        functools.partial(fused_kernel, names=tuple(names)),
        out_shape=list(outs.values()),
        in_specs=[place] * len(inputs),
        out_specs=[place] * len(outs),
        scratch_shapes=list(scratch.values()),
        compiler_params=pltpu.CompilerParams(
            collective_id=1, has_side_effects=True, vmem_limit_bytes=63 << 20
        ),
        cost_estimate=pl.CostEstimate(flops=14 << 30, bytes_accessed=8 << 20, transcendentals=0),
    )(*inputs.values())
    row, one = shape((1, width), F32), shape((1, 1), F32)
    emb, g_pin, g_board, g_proj, g_q, g_w, p_b, q_bias, w_bias, count, weight = pl.pallas_call(
        finish_kernel,
        out_shape=list(outs.values())[:6] + [row, row, row, one, one],
        in_specs=[place] * 6 + [whole],
        out_specs=[place] * 6 + [whole] * 5,
        scratch_shapes=[vmem(out.shape, out.dtype) for out in list(outs.values())[:6]] + [dma((2, 6))],
        cost_estimate=pl.CostEstimate(flops=0, bytes_accessed=5 << 20, transcendentals=0),
    )(*got)
    return (
        emb,
        g_pin,
        g_board,
        g_proj,
        p_b.reshape(width),
        g_q,
        q_bias.reshape(width),
        g_w,
        w_bias.reshape(width),
        count.reshape(()),
        weight.reshape(()),
    )


def silu_slope(value):
    sig = jax.nn.sigmoid(value)
    return sig * (1.0 + value * (1.0 - sig))


def slot_table(nbr_block, alpha_block, start, width):
    offsets = nbr_block - start
    places = lax.broadcasted_iota(jnp.int32, (1, 1, width), 2)
    return jnp.sum(jnp.where(offsets[:, :, None] == places, alpha_block[:, :, None], 0.0), axis=1)


def split_pair(table):
    upper = table.astype(jnp.bfloat16)
    lower = (table - upper.astype(jnp.float32)).astype(jnp.bfloat16)
    return (upper, lower)


def collect_rows(nbrs, alphas, table_all):
    total, columns = table_all.shape
    col_tile = math.gcd(total, 2048)
    count_tiles = total // col_tile
    tiles = table_all.reshape(count_tiles, col_tile, columns)
    rows = nbrs.shape[0]
    row_block = math.gcd(rows, 512)
    count_rows = rows // row_block

    def one_rows(pair):
        nbr_block, alpha_block = pair

        def step(acc, index):
            upper, lower = split_pair(
                slot_table(nbr_block, alpha_block, index * col_tile, col_tile)
            )
            piece = tiles[index]
            acc = acc + jnp.dot(upper, piece, preferred_element_type=jnp.float32)
            return (acc + jnp.dot(lower, piece, preferred_element_type=jnp.float32), None)

        acc, unused = lax.scan(
            step, jnp.zeros((row_block, columns), jnp.float32), jnp.arange(count_tiles)
        )
        return acc

    out = lax.map(
        one_rows,
        (nbrs.reshape(count_rows, row_block, -1), alphas.reshape(count_rows, row_block, -1)),
    )
    return out.reshape(rows, columns)


def spread_rows(grads, nbrs, alphas, base, width):
    rows, columns = grads.shape
    row_block = math.gcd(rows, 512)
    count_rows = rows // row_block
    col_tile = math.gcd(width, 2048)
    count_tiles = width // col_tile
    stacked = (
        grads.reshape(count_rows, row_block, columns),
        nbrs.reshape(count_rows, row_block, -1),
        alphas.reshape(count_rows, row_block, -1),
    )
    tdot = (((0,), (0,)), ((), ()))

    def one_tile(index):

        def step(acc, triple):
            grad_block, nbr_block, alpha_block = triple
            upper, lower = split_pair(
                slot_table(nbr_block, alpha_block, base + index * col_tile, col_tile)
            )
            acc = acc + lax.dot_general(upper, grad_block, tdot, preferred_element_type=jnp.float32)
            return (
                acc + lax.dot_general(lower, grad_block, tdot, preferred_element_type=jnp.float32),
                None,
            )

        acc, unused = lax.scan(step, jnp.zeros((col_tile, columns), jnp.float32), stacked)
        return acc

    out = lax.map(one_tile, jnp.arange(count_tiles))
    return out.reshape(width, columns)


def per_device(
    pin_features,
    board_features,
    is_board,
    neighbours,
    present,
    importance,
    proj_weight,
    proj_bias,
    q_weight,
    q_bias,
    w_weight,
    w_bias,
    cotangent,
):
    local_rows = pin_features.shape[0]
    width = q_weight.shape[0]
    filled = present.astype(jnp.float32) * importance
    alpha = filled / jnp.sum(filled, axis=1, keepdims=True)
    board_mask = (is_board == 1)[:, None]
    stat_terms = (jnp.sum(present.astype(jnp.float32)), jnp.sum(filled))
    stat_totals = lax.psum((stat_terms[0], stat_terms[1]), "rows")
    board_full = lax.all_gather(board_features, "cols", axis=1, tiled=True)
    board_proj = jnp.dot(board_full, proj_weight, preferred_element_type=jnp.float32) + proj_bias
    h_local = jnp.where(board_mask, board_proj, pin_features.astype(jnp.float32)).astype(
        jnp.bfloat16
    )
    h_full = lax.all_gather(h_local, "cols", axis=1, tiled=True)
    v_pre = jnp.dot(h_full, q_weight, preferred_element_type=jnp.float32) + q_bias
    message = jax.nn.silu(v_pre).astype(jnp.bfloat16)
    message_all = lax.all_gather(message, "rows", axis=0, tiled=True)
    agg_local = collect_rows(neighbours, alpha, message_all).astype(jnp.bfloat16)
    agg_full = lax.all_gather(agg_local, "cols", axis=1, tiled=True)
    w_self = w_weight[:width]
    w_agg = w_weight[width:]
    u_pre = (
        jnp.dot(h_full, w_self, preferred_element_type=jnp.float32)
        + jnp.dot(agg_full, w_agg, preferred_element_type=jnp.float32)
        + w_bias
    )
    z_act = jax.nn.silu(u_pre)
    squares = lax.psum(jnp.sum(z_act * z_act, axis=1), "cols")
    scale = lax.rsqrt(squares + 1e-06)[:, None]
    embeddings = (z_act * scale).astype(jnp.bfloat16)
    grad_out = cotangent.astype(jnp.float32)
    inner = lax.psum(jnp.sum(grad_out * z_act, axis=1), "cols")[:, None]
    grad_z = grad_out * scale - z_act * scale * scale * scale * inner
    grad_u = (grad_z * silu_slope(u_pre)).astype(jnp.bfloat16)
    agg_part = lax.dot_general(
        grad_u, w_agg, (((1,), (1,)), ((), ())), preferred_element_type=jnp.float32
    )
    grad_agg = lax.psum_scatter(agg_part, "cols", scatter_dimension=1, tiled=True).astype(
        jnp.bfloat16
    )
    table = spread_rows(grad_agg, neighbours, alpha, 0, message_all.shape[0])
    grad_message = lax.psum_scatter(
        table.astype(jnp.bfloat16), "rows", scatter_dimension=0, tiled=True
    ).astype(jnp.float32)
    grad_v = (grad_message * silu_slope(v_pre)).astype(jnp.bfloat16)
    h_part = lax.dot_general(
        grad_u, w_self, (((1,), (1,)), ((), ())), preferred_element_type=jnp.float32
    )
    h_part = h_part + lax.dot_general(
        grad_v, q_weight, (((1,), (1,)), ((), ())), preferred_element_type=jnp.float32
    )
    grad_h = lax.psum_scatter(
        h_part.astype(jnp.bfloat16), "cols", scatter_dimension=1, tiled=True
    ).astype(jnp.float32)
    grad_pin = jnp.where(board_mask, 0.0, grad_h)
    grad_hb = jnp.where(board_mask, grad_h, 0.0).astype(jnp.bfloat16)
    board_part = lax.dot_general(
        grad_hb, proj_weight, (((1,), (1,)), ((), ())), preferred_element_type=jnp.float32
    )
    grad_board = lax.psum_scatter(
        board_part.astype(jnp.bfloat16), "cols", scatter_dimension=1, tiled=True
    ).astype(jnp.float32)
    tdot = (((0,), (0,)), ((), ()))
    grad_w_local = jnp.concatenate(
        [
            lax.dot_general(h_full, grad_u, tdot, preferred_element_type=jnp.float32),
            lax.dot_general(agg_full, grad_u, tdot, preferred_element_type=jnp.float32),
        ],
        axis=0,
    )
    grad_q_local = lax.dot_general(h_full, grad_v, tdot, preferred_element_type=jnp.float32)
    grad_p_local = lax.dot_general(board_full, grad_hb, tdot, preferred_element_type=jnp.float32)
    grad_w, grad_q, grad_proj = (
        lax.psum_scatter(
            grad_w_local.astype(jnp.bfloat16), "rows", scatter_dimension=0, tiled=True
        ).astype(jnp.float32),
        lax.psum_scatter(
            grad_q_local.astype(jnp.bfloat16), "rows", scatter_dimension=0, tiled=True
        ).astype(jnp.float32),
        lax.psum_scatter(
            grad_p_local.astype(jnp.bfloat16), "rows", scatter_dimension=0, tiled=True
        ).astype(jnp.float32),
    )
    bias_terms = (
        jnp.sum(grad_hb.astype(jnp.float32), axis=0),
        jnp.sum(grad_v.astype(jnp.float32), axis=0),
        jnp.sum(grad_u.astype(jnp.float32), axis=0),
    )
    grad_pb, grad_qb, grad_wb = lax.psum((bias_terms[0], bias_terms[1], bias_terms[2]), "rows")
    all_nodes = local_rows * lax.axis_size("rows")
    mean_count = stat_totals[0] / all_nodes
    mean_weight = stat_totals[1] / (all_nodes * SLOTS)
    return (
        embeddings,
        grad_pin,
        grad_board,
        grad_proj,
        grad_pb,
        grad_q,
        grad_qb,
        grad_w,
        grad_wb,
        mean_count,
        mean_weight,
    )


def solution(mesh):
    in_specs = (
        P("rows", "cols"),
        P("rows", "cols"),
        P("rows"),
        P("rows", None),
        P("rows", None),
        P("rows", None),
        P(None, "cols"),
        P("cols"),
        P(None, "cols"),
        P("cols"),
        P(None, "cols"),
        P("cols"),
        P("rows", "cols"),
    )
    out_specs = (
        P("rows", "cols"),
        P("rows", "cols"),
        P("rows", "cols"),
        P("rows", "cols"),
        P("cols"),
        P("rows", "cols"),
        P("cols"),
        P("rows", "cols"),
        P("cols"),
        P(),
        P(),
    )
    fused = mesh.shape["rows"] == 8 and mesh.shape["cols"] == 4
    return jax.shard_map(
        fused_device if fused else per_device, mesh=mesh, in_specs=in_specs, out_specs=out_specs, check_vma=False
    )
```

```python
import functools
import math
import types

import jax
import jax.numpy as jnp
from jax import lax
from jax.experimental import pallas as pl
from jax.experimental.pallas import tpu as pltpu
from jax.sharding import PartitionSpec as P

SLOTS = 50
MESH = pl.DeviceIdType.MESH
BF = jnp.bfloat16
F32 = jnp.float32
NQ = 4
NP = 2
LO_BITS = 7
LO = 1 << LO_BITS
PIECE = 64
NT = (((1,), (1,)), ((), ()))
TN = (((0,), (0,)), ((), ()))


def dot(a, b):
    return jnp.dot(a, b, preferred_element_type=F32)


def dot_nt(a, b):
    return lax.dot_general(a, b, NT, preferred_element_type=F32)


def dot_tn(a, b):
    return lax.dot_general(a, b, TN, preferred_element_type=F32)


def loop(n, body, unroll=1):
    def step(i, carry):
        body(i)
        return carry

    lax.fori_loop(0, n, step, 0, unroll=unroll)


def row_sums(x):
    y = x[:, :128] + x[:, 128:]
    sums = [
        jnp.sum(y[i * 128 : (i + 1) * 128].T, axis=0, keepdims=True) for i in range(x.shape[0] // 128)
    ]
    return sums[0] if len(sums) == 1 else jnp.concatenate(sums, axis=0)


def down(row):
    return jnp.broadcast_to(row, (128, 128)).T


def down_rows(rows):
    cols = [down(rows[i : i + 1]) for i in range(rows.shape[0])]
    col = cols[0] if len(cols) == 1 else jnp.concatenate(cols, axis=0)
    return jnp.concatenate([col, col], axis=1)


def fused_kernel(*refs, names):
    s = types.SimpleNamespace(**dict(zip(names, refs)))
    r = lax.axis_index("rows")
    c = lax.axis_index("cols")
    z, y = r // 2, r % 2
    x, k = c // 2, c % 2
    rows, width = s.pin.shape
    bwidth = s.boards.shape[2]
    chunk = rows // NQ
    zn = 4
    per_block = rows // LO
    core = (r, x * 2 + 1 - k)
    xp = (r, (1 - x) * 2 + k)
    diagonal = (z * 2 + 1 - y, (1 - x) * 2 + k)
    yp = (z * 2 + 1 - y, c)
    upper = z // 2
    inner = (z % 2) + upper * (1 - 2 * (z % 2))
    zx = z + 1 - 2 * (z % 2)
    zxp = (zx * 2 + y, c)

    def at(q):
        return pl.ds(pl.multiple_of(q * chunk, chunk), chunk)

    def rdma(src, dst, send, recv, dev):
        return pltpu.make_async_remote_copy(
            src_ref=src, dst_ref=dst, send_sem=send, recv_sem=recv, device_id=dev, device_id_type=MESH
        )

    def arrived(ref, sem):
        rdma(ref, ref, sem, sem, core).wait_recv()

    def sent(ref, sem):
        rdma(ref, ref, sem, sem, core).wait_send()

    class Gather:
        def __init__(self, buf, base, ss, rs):
            self.buf, self.base, self.ss, self.rs = buf, base, ss, rs

        def ref(self, col, q):
            return self.buf.at[self.base + col, at(q)]

        def start(self, q):
            own = self.ref(c, q)
            rdma(own, own, self.ss.at[1, q], self.rs.at[1, q], xp).start()
            rdma(own, own, self.ss.at[0, q], self.rs.at[0, q], core).start()

        def forward(self, q):
            got = self.ref((1 - x) * 2 + k, q)
            arrived(got, self.rs.at[1, q])
            rdma(got, got, self.ss.at[2, q], self.rs.at[2, q], core).start()

        def finish(self, q):
            arrived(self.ref(x * 2 + 1 - k, q), self.rs.at[0, q])
            arrived(self.ref((1 - x) * 2 + 1 - k, q), self.rs.at[2, q])

        def drain(self, q):
            for i in range(3):
                sent(self.ref(c, q), self.ss.at[i, q])

    class Scatter:
        def __init__(self, part, name):
            self.part = part
            self.send1, self.recv1 = getattr(s, name + "_send1"), getattr(s, name + "_recv1")
            self.sendx, self.recvx = getattr(s, name + "_sendx"), getattr(s, name + "_recvx")
            self.ss, self.rs = getattr(s, name + "_ss"), getattr(s, name + "_rs")

        def first(self, q):
            for i, xs in ((0, 1 - x), (1, x)):
                self.send1[i, q] = self.part(xs * 2 + 1 - k, q).astype(BF)
                rdma(
                    self.send1.at[i, q], self.recv1.at[i, q], self.ss.at[i, q], self.rs.at[i, q], core
                ).start()

        def second(self, q):
            own = self.part((1 - x) * 2 + k, q)
            arrived(self.recv1.at[0, q], self.rs.at[0, q])
            self.sendx[q] = (own + self.recv1[0, q].astype(F32)).astype(BF)
            rdma(self.sendx.at[q], self.recvx.at[q], self.ss.at[2, q], self.rs.at[2, q], xp).start()

        def third(self, q):
            own = self.part(c, q)
            arrived(self.recv1.at[1, q], self.rs.at[1, q])
            own = own + self.recv1[1, q].astype(F32)
            arrived(self.recvx.at[q], self.rs.at[2, q])
            return own + self.recvx[q].astype(F32)

        def drain(self, q):
            for i in range(2):
                sent(self.send1.at[i, q], self.ss.at[i, q])
            sent(self.sendx.at[q], self.ss.at[2, q])

    class WeightSum:
        def __init__(self, part, name, out, ysend, zsend):
            self.part, self.out = part, out
            self.ysend, self.zsend = ysend, zsend
            self.yrecv, self.zrecv = getattr(s, name + "_yrecv"), getattr(s, name + "_zrecv")
            self.ss, self.rs = getattr(s, name + "_ss"), getattr(s, name + "_rs")

        def first(self, at0=0, n=4):
            def step(i):
                d = at0 + i
                ref = self.ysend(d)
                ref[...] = self.part(d, 1 - y, True).astype(BF)
                rdma(ref, self.yrecv.at[d], self.ss.at[0, d], self.rs.at[0, d], yp).start()

            loop(n, step, unroll=n)

        def second(self, at0=0, n=4):
            def step(i):
                d = at0 + i
                own = self.part(d, y)
                arrived(self.yrecv.at[d], self.rs.at[0, d])
                own = own + self.yrecv[d].astype(F32)

                @pl.when(d == z)
                def _():
                    self.out[...] = own

                @pl.when(d != z)
                def _():
                    ref = self.zsend(d)
                    ref[...] = own.astype(BF)
                    rdma(
                        ref, self.zrecv.at[z], self.ss.at[1, d], self.rs.at[1, z], (d * 2 + y, c)
                    ).start()

            loop(n, step)

        def third(self):
            def step(d):
                @pl.when(d != z)
                def _():
                    arrived(self.zrecv.at[d], self.rs.at[1, d])
                    self.out[...] += self.zrecv[d].astype(F32)

            loop(zn, step)

        def drain(self):
            def step(d):
                sent(self.ysend(d), self.ss.at[0, d])

                @pl.when(d != z)
                def _():
                    sent(self.zsend(d), self.ss.at[1, d])

            loop(zn, step)

    class PairSum(WeightSum):
        def first(self):
            for d in ((zx + 2) % 4, zx, (z + 2) % 4, z):
                ref = self.ysend(d)
                ref[...] = self.part(d, 1 - y, True).astype(BF)
                rdma(ref, self.yrecv.at[d], self.ss.at[0, d], self.rs.at[0, d], yp).start()

        def total(self, d):
            own = self.part(d, y)
            arrived(self.yrecv.at[d], self.rs.at[0, d])
            return own + self.yrecv[d].astype(F32)

        def second(self):
            for n, d in enumerate(((zx + 2) % 4, zx)):
                ref = self.zsend(n)
                ref[...] = self.total(d).astype(BF)
                rdma(ref, self.zrecv.at[n], self.ss.at[1, n], self.rs.at[1, n], zxp).start()

        def across(self):
            d = (z + 2) % 4
            ref = self.zsend(2)
            own = self.total(d)
            arrived(self.zrecv.at[0], self.rs.at[1, 0])
            ref[...] = (own + self.zrecv[0].astype(F32)).astype(BF)
            rdma(ref, self.zrecv.at[2], self.ss.at[1, 2], self.rs.at[1, 2], (d * 2 + y, c)).start()

        def third(self):
            own = self.total(z)
            for n in (1, 2):
                arrived(self.zrecv.at[n], self.rs.at[1, n])
                own = own + self.zrecv[n].astype(F32)
            self.out[...] = own

        def drain(self):
            for d in range(zn):
                sent(self.ysend(d), self.ss.at[0, d])
            for n in range(3):
                sent(self.zsend(n), self.ss.at[1, n])

    class DirectSum:
        def __init__(self, out):
            self.out, self.send, self.recv = out, s.wp_send, s.wp_recv
            self.ss, self.rs = s.wp_ss, s.wp_rs

        def first(self, part):
            n = self.out.shape[0]

            def step(d):
                both = part(d)
                for yy in range(2):
                    block = both[yy * n : (yy + 1) * n]
                    row = d * 2 + yy

                    @pl.when(row == r)
                    def _():
                        self.out[...] = block

                    @pl.when(row != r)
                    def _():
                        ref = self.send.at[row]
                        ref[...] = block.astype(BF)
                        rdma(ref, self.recv.at[r], self.ss.at[row], self.rs.at[r], (row, c)).start()

            loop(zn, step)

        def second(self):
            def step(row):
                @pl.when(row != r)
                def _():
                    arrived(self.recv.at[row], self.rs.at[row])
                    self.out[...] += self.recv[row].astype(F32)

            loop(2 * zn, step)

        def drain(self):
            def step(row):
                @pl.when(row != r)
                def _():
                    sent(self.send.at[row], self.ss.at[row])

            loop(2 * zn, step)

    barrier = pltpu.get_barrier_semaphore()

    def greet(dev):
        pl.semaphore_signal(barrier, inc=1, device_id=dev, device_id_type=MESH)

    near_by = (xp, yp, diagonal, core)
    for dev in near_by:
        greet(dev)

    @pl.when(z < 3)
    def _():
        greet(((z + 1) * 2 + y, c))

    @pl.when(z > 0)
    def _():
        greet(((z - 1) * 2 + y, c))

    boards, own_h = s.boards, s.ha
    in_sem = s.in_sem
    loads = {}
    order = (
        ("board", boards.at[c]),
        ("is_board", s.flags),
        ("proj_w", s.proj_w),
        ("proj_b", s.proj_b),
        ("pin", s.pin),
        ("neighbours", s.numbers),
        ("present", s.present),
        ("importance", s.importance),
        ("q_w", s.q_w),
        ("q_b", s.q_b),
        ("w_w", s.w_w),
        ("w_b", s.w_b),
        ("cotangent", s.cotangent),
    )
    for i, (name, ref) in enumerate(order):
        loads[name] = pltpu.make_async_copy(getattr(s, name + "_in"), ref, in_sem.at[i])
        loads[name].start()

    out_sem = s.out_sem

    def store(i, q, src, dst):
        return pltpu.make_async_copy(src, dst, out_sem.at[i, q])

    gather_b = Gather(boards, 0, s.gb_ss, s.gb_rs)
    gather_h = Gather(own_h, 0, s.gh_ss, s.gh_rs)
    loads["board"].wait()
    pl.semaphore_wait(barrier, len(near_by) + 1 + inner)
    loop(NQ, gather_b.start)

    mask = s.mask
    loads["is_board"].wait()
    flags = s.flags[...].astype(F32)
    for i in range(rows // 128):
        mask[i * 128 : (i + 1) * 128] = down(flags[i : i + 1])

    half = rows // 2
    padded = s.padded
    list_ss, list_rs = s.list_ss, s.list_rs

    quarter = rows // 4

    def lay(ref):
        for t in range(2):
            for i in range(quarter // 128):
                a, b = 2 * t * quarter + i * 128, (2 * t + 1) * quarter + i * 128
                ref[t, i * 128 : (i + 1) * 128] = jnp.concatenate(
                    [padded[:, a : a + 128], padded[:, b : b + 128]], axis=0
                ).T

    def lend_list(i):
        src, dst = ((s.numbers, s.numbers2), (s.alpha, s.alpha2))[i]
        return rdma(src, dst, list_ss.at[i], list_rs.at[i], yp)

    def prepare():
        for name in ("neighbours", "present", "importance"):
            loads[name].wait()
        lend_list(0).start()
        present = s.present[...].astype(F32)
        filled = present * s.importance[...]
        padded[SLOTS:] = jnp.zeros((padded.shape[0] - SLOTS, rows), F32)
        padded[:SLOTS] = filled / jnp.sum(filled, axis=0, keepdims=True)
        s.alpha[...] = padded[...].astype(BF)
        lend_list(1).start()
        lay(s.weight)
        small = s.small
        small[r] = jnp.zeros(small.shape[1:], F32)
        small[r, 3:4] = jnp.concatenate(
            [
                jnp.broadcast_to(jnp.sum(present).reshape(1, 1), (1, 128)),
                jnp.broadcast_to(jnp.sum(filled).reshape(1, 1), (1, 128)),
            ],
            axis=1,
        )
        numbers = s.numbers[...]
        padded[:SLOTS] = (numbers >> LO_BITS).astype(F32)
        lay(s.high)
        padded[:SLOTS] = (numbers & (LO - 1)).astype(F32)
        lay(s.low)

    def prepare2():
        for i in range(2):
            lend_list(i).wait_recv()
        numbers = s.numbers2[...]
        high = numbers >> LO_BITS
        place = (high // (2 * per_block)) * per_block + high % per_block
        padded[:SLOTS] = jnp.where((high // per_block) % 2 == y, place, -1).astype(F32)
        lay(s.high2)
        padded[:SLOTS] = (numbers & (LO - 1)).astype(F32)
        lay(s.low2)
        padded[...] = s.alpha2[...].astype(F32)
        lay(s.weight2)

    def mask_of(q):
        m = mask[at(q)] > 0.5
        return jnp.concatenate([m, m], axis=1)

    table, stage = s.table, s.stage
    pitch = stage.shape[0] // 64
    piece_rows = PIECE // 4

    def build(i, lists, table):
        n_high = 2 * table.shape[0]
        iota = lax.broadcasted_iota(jnp.int32, (128, 128), 0).astype(F32).astype(BF)
        front = lax.broadcasted_iota(jnp.int32, (16, 128), 1) < 64
        zero, one = jnp.zeros((), BF), jnp.ones((), BF)

        def tiles(v, n):
            return jnp.concatenate([v] * n, axis=0)

        zeros = jnp.zeros((n_high, 128), BF)
        n = n_high // 16

        def four(j):
            p = i * piece_rows + j
            weights, places = [], []
            for t in range(2):

                def row(ref):
                    return jnp.broadcast_to(ref[t, pl.ds(p, 1), :], (16, 128))

                hi, lo, al = row(lists[0]).astype(BF), row(lists[1]).astype(BF), row(lists[2])
                places.append(jnp.where(tiles(lo, 8) == iota, one, zero))
                same = tiles(hi, n) == iota[:n_high]
                for a in (jnp.where(front, al, 0.0), jnp.where(front, 0.0, al)):
                    w = jnp.where(same, tiles(a.astype(BF), n), zero)
                    weights.append(jnp.concatenate([w, zeros] if t == 0 else [zeros, w], axis=1))
            out = dot_nt(jnp.concatenate(weights, axis=0), jnp.concatenate(places, axis=1))
            for g in range(4):
                stage[pl.ds(j + g * piece_rows, n_high, stride=pitch), :] = out[
                    g * n_high : (g + 1) * n_high
                ]

        loop(piece_rows, four, unroll=16)

        def convert(h):
            for f in range(2):
                base = (2 * h + f) * pitch
                for g in range(4):
                    table[
                        h,
                        pl.ds(pl.multiple_of(i * piece_rows + g * quarter, 16), piece_rows),
                        f * 128 : (f + 1) * 128,
                    ] = stage[
                        pl.ds(pl.multiple_of(base + g * piece_rows, 8), piece_rows), :
                    ].astype(BF)

        loop(table.shape[0], convert, unroll=4)

    lists1 = (s.high, s.low, s.weight)
    lists2 = (s.high2, s.low2, s.weight2)
    table2 = s.table2

    def piece(i):
        build(i, lists1, table)

    def piece2(i):
        build(i, lists2, table2)

    n_pieces = rows // PIECE

    message, v_pre = s.message, s.v_pre

    def make_h(q):
        lines = at(q)
        b01 = jnp.concatenate([boards[0, lines], boards[1, lines]], axis=1)
        b23 = jnp.concatenate([boards[2, lines], boards[3, lines]], axis=1)
        proj = dot(b01, s.proj_w[: 2 * bwidth]) + dot(b23, s.proj_w[2 * bwidth :]) + s.proj_b[...]
        own_h[c, lines] = jnp.where(mask_of(q), proj, s.pin[lines].astype(F32)).astype(BF)

    def block(zb, yb, q):
        return message.at[zb * 2 + yb, q]

    def send_up(zb, q):
        ref = block(zb, y, q)
        rdma(ref, ref, s.up_ss.at[zb, q], s.msg_rs.at[zb * 2 + y, q], ((z + 1) * 2 + y, c)).start()

    def send_down(zb, q):
        ref = block(zb, y, q)
        rdma(ref, ref, s.down_ss.at[zb, q], s.msg_rs.at[zb * 2 + y, q], ((z - 1) * 2 + y, c)).start()

    def send_y(zb, q):
        ref = block(zb, y, q)
        rdma(ref, ref, s.y_ss.at[zb, q], s.msg_rs.at[zb * 2 + y, q], yp).start()

    def make_message(q):
        lines = at(q)
        acc = dot(own_h[0, lines], s.q_w[:width])
        for i in range(1, 4):
            acc = acc + dot(own_h[i, lines], s.q_w[i * width : (i + 1) * width])
        v = acc + s.q_b[...]
        v_pre[lines] = v
        message[r, q] = (v * jax.nn.sigmoid(v)).astype(BF)

        @pl.when(z < 3)
        def _():
            send_up(z, q)

        @pl.when(z > 0)
        def _():
            send_down(z, q)

        send_y(z, q)

    prepare()
    for name in ("proj_w", "proj_b", "pin"):
        loads[name].wait()

    def board_phase(q):
        gather_b.forward(q)
        gather_b.finish(q)
        make_h(q)
        gather_h.start(q)

    piece(0)
    loop(NQ, board_phase)
    early = 3
    loop(early - 1, lambda i: piece(1 + i))

    half = rows // 2
    sub = half // NP
    own_half = pl.ds(pl.multiple_of(x * half, half), half)
    their_half = pl.ds(pl.multiple_of((1 - x) * half, half), half)
    lend_ss, lend_rs = s.lend_ss, s.lend_rs
    wide = 4 * width

    def lends():
        return (
            (s.w_w.at[:wide], s.w2.at[:wide]),
            (s.w_b, s.w_b2),
            (s.w_w.at[wide:], s.w2.at[wide:]),
            (s.cotangent.at[their_half], s.cotangent2),
        )

    def lend(i):
        src, dst = lends()[i]
        return rdma(src, dst, lend_ss.at[i], lend_rs.at[i], xp)

    for name in ("w_w", "w_b", "cotangent"):
        loads[name].wait()
    for i in range(4):
        lend(i).start()
    loads["q_w"].wait()
    loads["q_b"].wait()

    def message_phase(q):
        gather_h.forward(q)
        gather_h.finish(q)
        make_message(q)
        piece(early + q)

        @pl.when(q % 2 == 0)
        def _():
            piece(early + NQ + q // 2)

    loop(NQ, message_phase)
    built = early + NQ + NQ // 2

    u_pre = s.u_pre

    def part_of(i):
        return pl.ds(pl.multiple_of(i * sub, sub), sub)

    def mine(i):
        return pl.ds(pl.multiple_of(x * half + i * sub, sub), sub)

    def theirs(i):
        return pl.ds(pl.multiple_of((1 - x) * half + i * sub, sub), sub)

    def u_from_h(i):
        for n, w, b in ((0, s.w_w, s.w_b), (1, s.w2, s.w_b2)):
            acc = dot(own_h[0, mine(i)], w[:width])
            for m in range(1, 4):
                acc = acc + dot(own_h[m, mine(i)], w[m * width : (m + 1) * width])
            u_pre[n, part_of(i)] = acc + b[...]

    agg = s.grad_pin
    parts = rows // chunk

    def add(b, first, n):
        for i in range(parts):
            lines = slice(i * chunk, (i + 1) * chunk)
            acc = agg[lines]
            for q in range(first, first + n):
                acc = acc + dot(table[b * NQ + q, lines], message[b, q])
            agg[lines] = acc

    def over_y(zb, q):
        @pl.when((zb != zx) | ((inner == 0) & (q < NQ // 2)))
        def _():
            send_y(zb, q)

    def send_zx(q):
        ref = block(z, 1 - y, q)
        rdma(ref, ref, s.zx_ss.at[q], s.msg_rs.at[z * 2 + 1 - y, q], zxp).start()

    def at_z(zb):
        return (zb >= 0) & (zb <= 3)

    n_second = 3 * NQ
    n_second2 = n_pieces // 2
    steps = n_pieces - built

    def second_phase(i):
        t, q = 1 + i // NQ, i % NQ

        @pl.when(z - t >= 0)
        def _():
            arrived(block(z - t, y, q), s.msg_rs.at[(z - t) * 2 + y, q])

            @pl.when(z < 3)
            def _():
                send_up(z - t, q)

            over_y(z - t, q)

        @pl.when(z + t <= 3)
        def _():
            arrived(block(z + t, y, q), s.msg_rs.at[(z + t) * 2 + y, q])

            @pl.when(z > 0)
            def _():
                send_down(z + t, q)

            over_y(z + t, q)

        @pl.when(t == 1)
        def _():
            arrived(block(z, 1 - y, q), s.msg_rs.at[z * 2 + 1 - y, q])

            @pl.when(inner == 0)
            def _():
                send_zx(q)

        @pl.when((t == 3) & (inner == 1) & (q >= NQ // 2))
        def _():
            send_zx(q)

        @pl.when(i < steps)
        def _():
            piece(built + i)

        @pl.when(i == 0)
        def _():
            prepare2()

        @pl.when((i > 0) & (i < 1 + n_second2))
        def _():
            loop(2, lambda n: piece2(2 * (i - 1) + n))

        @pl.when(i == steps)
        def _():
            agg[...] = jnp.zeros_like(agg)
            lend(0).wait_recv()
            lend(1).wait_recv()

        @pl.when(i >= n_second - NP)
        def _():
            u_from_h(i - (n_second - NP))

        @pl.when((i >= n_second - 5) & (i < n_second))
        def _():
            n = i - (n_second - 5)
            zb = z + jnp.where(n == 0, 0, jnp.where(n == 1, -1, jnp.where(n == 2, 1, jnp.where(n == 3, -2, 2))))

            @pl.when(at_z(zb))
            def _():
                add(zb * 2 + y, 0, NQ)

    loop(n_second, second_phase)

    add(z * 2 + 1 - y, 0, NQ)

    @pl.when(inner == 0)
    def _():
        add((3 - z) * 2 + y, 0, NQ)

    def add_arriving(zb, first, n):
        b = zb * 2 + 1 - y
        loop(n, lambda q: arrived(message.at[b, first + q], s.msg_rs.at[b, first + q]))
        add(b, first, n)

    add_arriving(zx, 0, NQ // 2)
    add_arriving(2 - upper, 0, NQ)
    for q in range(NQ):
        blocks = [3 * (1 - upper) * 2 + 1 - y] + ([zx * 2 + 1 - y] if q >= NQ // 2 else [])
        for b in blocks:
            arrived(message.at[b, q], s.msg_rs.at[b, q])
        for i in range(parts):
            lines = slice(i * chunk, (i + 1) * chunk)
            acc = agg[lines]
            for b in blocks:
                acc = acc + dot(table[b * NQ + q, lines], message[b, q])
            if q < NQ - 1:
                agg[lines] = acc
            else:
                own_h[4 + c, lines] = acc.astype(BF)

    gu, gv, gb, gu2 = s.gu, s.gv, s.gb, s.gu2
    stat, stat_ss, stat_rs = s.stat, s.stat_ss, s.stat_rs
    ga_ss, ga_rs = s.ga_ss, s.ga_rs
    other_x = (1 - x) * 2 + k

    def agg_ref(col, lines):
        return own_h.at[4 + col, lines]

    def agg_start(i):
        a, b = agg_ref(c, theirs(i)), agg_ref(c, mine(i))
        rdma(a, a, ga_ss.at[1, i], ga_rs.at[1, i], xp).start()
        rdma(b, b, ga_ss.at[0, i], ga_rs.at[0, i], core).start()

    def agg_forward(i):
        got = agg_ref(other_x, mine(i))
        arrived(got, ga_rs.at[1, i])
        rdma(got, got, ga_ss.at[2, i], ga_rs.at[2, i], core).start()

    def agg_finish(i):
        arrived(agg_ref(x * 2 + 1 - k, mine(i)), ga_rs.at[0, i])
        arrived(agg_ref((1 - x) * 2 + 1 - k, mine(i)), ga_rs.at[2, i])

    def rest_start():
        a, b = agg_ref(c, own_half), agg_ref(c, their_half)
        rdma(a, a, ga_ss.at[1, NP], ga_rs.at[1, NP], xp).start()
        rdma(b, b, ga_ss.at[0, NP], ga_rs.at[0, NP], core).start()

    def rest_forward():
        got = agg_ref(other_x, their_half)
        arrived(got, ga_rs.at[1, NP])
        rdma(got, got, ga_ss.at[2, NP], ga_rs.at[2, NP], core).start()

    def rest_finish():
        arrived(agg_ref(x * 2 + 1 - k, their_half), ga_rs.at[0, NP])
        arrived(agg_ref((1 - x) * 2 + 1 - k, their_half), ga_rs.at[2, NP])

    loop(NP, agg_start)
    lend(2).wait_recv()
    lend(3).wait_recv()

    def gradients(i):
        return s.cotangent[mine(i)].astype(F32), s.cotangent2[part_of(i)].astype(F32)

    def make_u(i):
        us = [u_pre[n, part_of(i)] for n in range(2)]
        for m in range(4):
            a = own_h[4 + m, mine(i)]
            us = [u + dot(a, w[(4 + m) * width : (5 + m) * width]) for u, w in zip(us, (s.w_w, s.w2))]
        squares, inners = 0.0, 0.0
        for n, (u, g) in enumerate(zip(us, gradients(i))):
            u_pre[n, part_of(i)] = u
            zz = u * jax.nn.sigmoid(u)
            squares = squares + zz * zz
            inners = inners + g * zz
        pad = jnp.zeros((8 - 2 * sub // 128, 128), F32)
        stat[0, i] = jnp.concatenate([row_sums(squares), row_sums(inners), pad], axis=0)
        rdma(stat.at[0, i], stat.at[1, i], stat_ss.at[i], stat_rs.at[i], core).start()

    def make_gu(i):
        arrived(stat.at[1, i], stat_rs.at[i])
        total = stat[0, i] + stat[1, i]
        n_rows = sub // 128
        rr = lax.rsqrt(total[:n_rows] + 1e-6)
        scale = down_rows(rr)
        pull = down_rows(rr * rr * rr * total[n_rows : 2 * n_rows])
        for n, (g, emb, grad) in enumerate(
            zip(gradients(i), (s.embeddings, s.emb2), (gu, gu2))
        ):
            u = u_pre[n, part_of(i)]
            sig = jax.nn.sigmoid(u)
            zz = u * sig
            lines = mine(i) if n == 0 else part_of(i)
            emb[lines] = (zz * scale).astype(BF)
            grad[lines] = ((g * scale - zz * pull) * (sig * (1.0 + u * (1.0 - sig)))).astype(BF)

    def agg_part(col, i):
        lines = pl.ds(pl.multiple_of((4 + col) * width, width), width)
        return dot_nt(gu[mine(i)], s.w_w[lines, :]) + dot_nt(gu2[part_of(i)], s.w2[lines, :])

    grad_agg, grad_agg2 = s.grad_agg, s.grad_agg2
    sa_send, sa_recv, sa_x, sa_ss, sa_rs = s.sa_send, s.sa_recv, s.sa_x, s.sa_ss, s.sa_rs

    def agg_first(i):
        for n, xs in ((0, 1 - x), (1, x)):
            sa_send[n, i] = agg_part(xs * 2 + 1 - k, i).astype(BF)
            rdma(sa_send.at[n, i], sa_recv.at[n, i], sa_ss.at[n, i], sa_rs.at[n, i], core).start()

    def part_c(h):
        return pl.ds(h * (width // 2), width // 2)

    def agg_second(i):
        own = agg_part(other_x, i)
        arrived(sa_recv.at[0, i], sa_rs.at[0, i])
        sa_x[i] = (own + sa_recv[0, i].astype(F32)).T.astype(BF)
        here, there = x * NP + i, (1 - x) * NP + i
        for h in range(2):
            src = sa_x.at[i, part_c(h)]
            if i == NP - 1:
                to = grad_agg2.at[here, part_c(h)]
                rdma(src, to, s.gy_ss.at[h, there], s.gy_rs.at[h, here], diagonal).start()
            rdma(src, grad_agg.at[here, part_c(h)], sa_ss.at[2 + h, i], sa_rs.at[2 + h, i], xp).start()

    def agg_third(i):
        own = agg_part(c, i)
        arrived(sa_recv.at[1, i], sa_rs.at[1, i])
        grad_agg[x * NP + i] = (own + sa_recv[1, i].astype(F32)).T.astype(BF)
        agg_over_y(x * NP + i)

    def agg_over_y(i, halves=(0, 1)):
        for h in halves:
            rdma(
                grad_agg.at[i, part_c(h)],
                grad_agg2.at[i, part_c(h)],
                s.gy_ss.at[h, i],
                s.gy_rs.at[h, i],
                yp,
            ).start()

    def room(at_block, n):
        return [lambda d, b=b, n=n: message.at[b, d, pl.ds(0, n)] for b in (at_block, at_block + 1)]

    def room_narrow(at_block, n):
        return [lambda d, i=i: message.at[at_block, d, pl.ds(i * n, n)] for i in range(2)]

    sum_w = WeightSum(lambda d, yy, first=False: dot_tn(own_h[d * 2 + yy], gu[...]), "ww", s.grad_w, *room(4, width))

    def half_phases():
        for i in range(NP):
            agg_forward(i)
            if i > 0:
                make_gu(i - 1)
                agg_first(i - 1)
            agg_finish(i)
            make_u(i)
            if i > 0:
                agg_second(i - 1)
                agg_third(i - 1)
        make_gu(NP - 1)
        agg_first(NP - 1)
        agg_second(NP - 1)
        agg_third(NP - 1)

    half_phases()

    def give(n):
        src, dst = ((gu2, gu.at[own_half]), (s.emb2, s.embeddings.at[own_half]))[n]
        return rdma(src, dst, s.give_ss.at[n], s.give_rs.at[n], xp)

    def give_back(n):
        ref = (gu, s.embeddings)[n].at[their_half]
        return rdma(ref, ref, s.give_ss.at[n], s.give_rs.at[n], xp)

    give(0).start()
    rest_start()
    give(1).start()
    def arrived_x(i, h):
        arrived(grad_agg.at[(1 - x) * NP + i, part_c(h)], sa_rs.at[2 + h, i])

    for i in range(NP - 1):
        for h in range(2):
            arrived_x(i, h)
            agg_over_y((1 - x) * NP + i, (h,))

    def gradients_here(h):
        arrived_x(NP - 1, h)
        for i in range(2 * NP):
            arrived(grad_agg2.at[i, part_c(h)], s.gy_rs.at[h, i])

    def sent_messages(q):
        @pl.when(z < 3)
        def _():
            sent(block(z, y, q), s.up_ss.at[z, q])

        @pl.when(z > 0)
        def _():
            sent(block(z, y, q), s.down_ss.at[z, q])

        for t in range(1, 4):
            @pl.when((z - t >= 0) & (z < 3))
            def _():
                sent(block(z, y, q), s.up_ss.at[z - t, q])

            @pl.when((z + t <= 3) & (z > 0))
            def _():
                sent(block(z, y, q), s.down_ss.at[z + t, q])

        for zb in range(4):
            @pl.when((zb != zx) | ((inner == 0) & (q < NQ // 2)))
            def _():
                sent(block(z, y, q), s.y_ss.at[zb, q])

        @pl.when((inner == 0) | (q >= NQ // 2))
        def _():
            sent(block(z, y, q), s.zx_ss.at[q])

    loop(NQ, sent_messages)

    zsend, zrecv = message, s.zrecv
    m_zs, m_zr = s.m_zs, s.m_zr
    adjust = (0, 0, -1, 1)

    def dest(j):
        base = 3 - j + inner * adjust[j]
        return base + upper * (3 - 2 * base)

    each = 2 * NP // NQ

    def sum_of(terms):
        total = None
        for term in terms:
            total = term if total is None else total + term
        return total

    def spread(d, q, c0=0, nc=width):
        own, other = (d * 2 + y) * NQ + q, d * NQ + q
        n = sub
        return sum_of(
            dot(ref[m, c0 : c0 + nc], tab[b, m * n : (m + 1) * n])
            for ref, tab, b in ((grad_agg, table, own), (grad_agg2, table2, other))
            for m in range(2 * NP)
        )

    small = s.small

    def column_sums(i, ref):
        small[r, i : i + 1] = dot(jnp.ones((16, rows), BF), ref[...])[0:1]

    m_hs, m_hr = s.m_hs, s.m_hr

    def target(j):
        d = dest(j)
        step = 1 - 2 * upper
        if j == 2:
            step = step * (1 - 2 * inner)
        is_dest = (0, inner, 1)[j]
        slot = d + is_dest * ((1 - step) // 2) * (4 - d)
        return d, slot, ((z + step) * 2 + y, c)

    def along_half(q, h):
        d, slot, dev = target(0)
        lines = part_c(h)
        own = spread(d, q, h * (width // 2), width // 2)

        @pl.when(inner == 0)
        def _():
            zsend[d, q, lines] = own.astype(BF)

        @pl.when(inner == 1)
        def _():
            arrived(zrecv.at[d, q, lines], m_hr.at[d, h, q])
            zsend[d, q, lines] = (own + zrecv[d, q, lines].astype(F32)).astype(BF)

        rdma(
            zsend.at[d, q, lines], zrecv.at[slot, q, lines], m_hs.at[h, q], m_hr.at[slot, h, q], dev
        ).start()

    def along(j, q):
        d, slot, dev = target(j)
        own = spread(d, q)

        @pl.when(inner == 0)
        def _():
            zsend[d, q] = own.astype(BF)

        @pl.when(inner == 1)
        def _():
            if j == 1:
                arrived(zrecv.at[d, q], m_zr.at[d, q])
            else:
                for h in range(2):
                    arrived(zrecv.at[d, q, part_c(h)], m_hr.at[d, h, q])
            zsend[d, q] = (own + zrecv[d, q].astype(F32)).astype(BF)

        rdma(zsend.at[d, q], zrecv.at[slot, q], m_zs.at[d, q], m_zr.at[slot, q], dev).start()

    for h in range(2):
        gradients_here(h)
        loop(NQ, lambda q, h=h: along_half(q, h))
        if h == 0:

            @pl.when(inner == 1)
            def _():
                give_back(0).wait_recv()
                sum_w.first(0, 2)

    @pl.when(inner == 0)
    def _():
        for j in (1, 2):
            loop(NQ, lambda q, j=j: along(j, q))
        give_back(0).wait_recv()
        sum_w.first(0, 2)

    rest_forward()
    rest_finish()
    sum_w.first(2, 2)
    column_sums(2, gu)

    @pl.when(inner == 1)
    def _():
        def both_ways(q):
            along(2, q)
            along(1, q)

        loop(NQ, both_ways)

    give_back(1).wait_recv()
    store(0, 0, s.embeddings, s.embeddings_out).start()

    total_t = s.total_t

    def make_gv(q):
        total_t[...] = spread(z, q)

        @pl.when(z > 0)
        def _():
            arrived(zrecv.at[z, q], m_zr.at[z, q])
            total_t[...] += zrecv[z, q].astype(F32)

        @pl.when(z < 3)
        def _():
            arrived(zrecv.at[4, q], m_zr.at[4, q])
            total_t[...] += zrecv[4, q].astype(F32)

        v = v_pre[at(q)]
        sig = jax.nn.sigmoid(v)
        gv[at(q)] = (total_t[...].T * (sig * (1.0 + v * (1.0 - sig)))).astype(BF)

    def h_part(col, q):
        lines = pl.ds(pl.multiple_of(col * width, width), width)
        return dot_nt(gu[at(q)], s.w_w[lines, :]) + dot_nt(gv[at(q)], s.q_w[lines, :])

    def b_part(col, q):
        lines = pl.ds(pl.multiple_of(col * bwidth, bwidth), bwidth)
        return dot_nt(gb[at(q)], s.proj_w[lines, :])

    scatter_h, scatter_b = Scatter(h_part, "sh"), Scatter(b_part, "sb")


    def q_part(d, yy, first=False):
        n = width // 2
        keep = u_pre.at[0, pl.ds(d * n, n)]
        if not first:
            return keep[...]
        both = dot_tn(own_h[d], gv[...])
        keep[...] = jnp.where(y == 0, both[:n], both[n:])
        return jnp.where(y == 0, both[n:], both[:n])

    sum_q = PairSum(q_part, "wq", s.grad_q, *room_narrow(6, width // 2))
    sum_p = DirectSum(s.grad_p)
    small_ss, small_rs = s.small_ss, s.small_rs

    def so_far(d):
        return u_pre.at[1, pl.ds(d * bwidth, bwidth)]

    def add_proj(q):
        for d in range(4):
            got = dot_tn(boards[d, at(q)], gb[at(q)])

            @pl.when(q == 0)
            def _():
                so_far(d)[...] = got

            @pl.when(q > 0)
            def _():
                so_far(d)[...] += got

    def proj_part(d):
        last = slice((NQ - 1) * chunk, NQ * chunk)
        return so_far(d)[...] + dot_tn(boards[d, last], gb[last])

    def send_small():
        column_sums(0, gb)
        for d in range(1, 8):
            rdma(
                small.at[r], small.at[r], small_ss.at[d - 1], small_rs.at[r], ((r + d) % 8, c)
            ).start()

    def finish_board(q):
        s.grad_board[at(q)] = scatter_b.third(q)
        store(2, q, s.grad_board.at[at(q)], s.grad_board_out.at[at(q)]).start()

    def fourth_phase(t):
        @pl.when(t < NQ)
        def _():
            make_gv(t)
            scatter_h.first(t)

        @pl.when((t >= 3) & (t < NQ + 2))
        def _():
            scatter_b.second(t - 3)

        @pl.when(t == NQ - 1)
        def _():
            scatter_h.second(t)
            sum_q.first()

        @pl.when((t >= 2) & (t < NQ + 2))
        def _():
            q = t - 2
            g = scatter_h.third(q)
            m = mask_of(q)
            gb[at(q)] = jnp.where(m, g, 0.0).astype(BF)
            s.grad_pin[at(q)] = jnp.where(m, 0.0, g)

            @pl.when(t == NQ + 1)
            def _():
                sum_p.first(proj_part)

            scatter_b.first(q)
            store(1, q, s.grad_pin.at[at(q)], s.grad_pin_out.at[at(q)]).start()

        @pl.when(t < NQ - 1)
        def _():
            scatter_h.second(t)


        @pl.when((t >= 2) & (t <= NQ))
        def _():
            add_proj(t - 2)

    sum_w.second()
    loop(NQ + 2, fourth_phase)
    sum_q.second()
    scatter_b.second(NQ - 1)
    column_sums(1, gv)
    send_small()
    for q in range(NQ - 1):
        finish_board(q)
    sum_q.across()
    sum_w.third()
    store(0, 1, s.grad_w, s.grad_w_out).start()
    finish_board(NQ - 1)
    sum_q.third()
    store(0, 2, s.grad_q, s.grad_q_out).start()
    for d in range(1, 8):
        other = (r + d) % 8
        arrived(small.at[other], small_rs.at[other])
    total = small[0]
    for i in range(1, 8):
        total = total + small[i]
    nodes = rows * 8
    per = jnp.concatenate(
        [jnp.full((1, 128), 1.0 / nodes, F32), jnp.full((1, 128), 1.0 / (nodes * SLOTS), F32)], axis=1
    )
    s.sums[...] = total
    s.sums[3:4] = total[3:4] * per
    store(0, 3, s.sums, s.sums_out).start()
    sum_p.second()
    store(3, 0, s.grad_p, s.grad_p_out).start()

    def drain(q):
        gather_b.drain(q)
        gather_h.drain(q)
        scatter_h.drain(q)
        scatter_b.drain(q)
        store(1, q, s.grad_pin.at[at(q)], s.grad_pin_out.at[at(q)]).wait()
        store(2, q, s.grad_board.at[at(q)], s.grad_board_out.at[at(q)]).wait()
        for d in range(4):
            @pl.when((d != z) & (d != dest(0)))
            def _():
                sent(zsend.at[d, q], m_zs.at[d, q])

    loop(NQ, drain)

    def drain_half(i):
        for n in range(3):
            sent(agg_ref(c, mine(i)), ga_ss.at[n, i])
        for n in range(2):
            sent(sa_send.at[n, i], sa_ss.at[n, i])
        for h in range(2):
            sent(sa_x.at[i, part_c(h)], sa_ss.at[2 + h, i])
        sent(stat.at[0, i], stat_ss.at[i])

    loop(NP, drain_half)
    for n in range(3):
        sent(agg_ref(c, own_half), ga_ss.at[n, NP])
    for n in range(4):
        lend(n).wait_send()
    for n in range(2):
        lend_list(n).wait_send()
    for h in range(2):
        loop(2 * NP, lambda i, h=h: sent(grad_agg.at[i, part_c(h)], s.gy_ss.at[h, i]))
        loop(NQ, lambda q, h=h: sent(zsend.at[dest(0), q, part_c(h)], m_hs.at[h, q]))
    for n in range(2):
        give(n).wait_send()
    sum_w.drain()
    sum_q.drain()
    sum_p.drain()
    for d in range(7):
        sent(small.at[r], small_ss.at[d])
    for i, (n, name) in enumerate(
        ((0, "embeddings"), (0, "grad_w"), (0, "grad_q"), (0, "sums"), (3, "grad_p"))
    ):
        store(n, i % 4, getattr(s, name), getattr(s, name + "_out")).wait()


def finish_kernel(*refs):
    ins, sums, outs, small, held, sem = refs[:6], refs[6], refs[7:13], refs[13:18], refs[18:24], refs[24]
    first = [pltpu.make_async_copy(a, b, sem.at[0, i]) for i, (a, b) in enumerate(zip(ins, held))]
    second = [pltpu.make_async_copy(a, b, sem.at[1, i]) for i, (a, b) in enumerate(zip(held, outs))]
    for copy in first:
        copy.start()
    for i in range(3):
        small[i][...] = sums[i : i + 1]
    small[3][...] = sums[3:4, 0:1]
    small[4][...] = sums[3:4, 128:129]
    for a, b in zip(first, second):
        a.wait()
        b.start()
    for copy in second:
        copy.wait()


def fused_device(
    pin, board, is_board, neighbours, present, importance, proj_w, proj_b, q_w, q_b, w_w, w_b, cotangent
):
    rows, width = pin.shape
    bwidth = board.shape[1]
    chunk = rows // NQ
    nodes = rows * 8
    inputs = dict(
        board=board,
        is_board=is_board.reshape(rows // 128, 128),
        proj_w=proj_w,
        proj_b=proj_b.reshape(1, width),
        pin=pin,
        neighbours=neighbours.T,
        present=present.T,
        importance=importance.T,
        q_w=q_w,
        q_b=q_b.reshape(1, width),
        w_w=w_w,
        w_b=w_b.reshape(1, width),
        cotangent=cotangent,
    )
    shape = jax.ShapeDtypeStruct
    outs = dict(
        embeddings=shape((rows, width), BF),
        grad_pin=shape((rows, width), F32),
        grad_board=shape((rows, bwidth), F32),
        grad_p=shape((bwidth * 4 // 8, width), F32),
        grad_q=shape((width * 4 // 8, width), F32),
        grad_w=shape((2 * width * 4 // 8, width), F32),
        sums=shape((8, width), F32),
    )
    vmem, dma = pltpu.VMEM, pltpu.SemaphoreType.DMA
    scratch = dict(
        in_sem=dma((len(inputs),)),
        out_sem=dma((4, NQ)),
        flags=vmem((rows // 128, 128), jnp.int32),
        numbers=vmem((SLOTS, rows), jnp.int32),
        numbers2=vmem((SLOTS, rows), jnp.int32),
        alpha=vmem((64, rows), BF),
        alpha2=vmem((64, rows), BF),
        padded=vmem((64, rows), F32),
        table2=vmem((nodes // 2 // chunk, rows, chunk), BF),
        high2=vmem((2, rows // 4, 128), F32),
        low2=vmem((2, rows // 4, 128), F32),
        weight2=vmem((2, rows // 4, 128), F32),
        grad_agg2=vmem((2 * NP, width, rows // 2 // NP), BF),
        table=vmem((nodes // chunk, rows, chunk), BF),
        stage=vmem((64 * (PIECE + 8), 128), F32),
        high=vmem((2, rows // 4, 128), F32),
        low=vmem((2, rows // 4, 128), F32),
        weight=vmem((2, rows // 4, 128), F32),
        mask=vmem((rows, 128), F32),
        boards=vmem((4, rows, bwidth), BF),
        ha=vmem((8, rows, width), BF),
        message=vmem((8, NQ, chunk, width), BF),
        v_pre=vmem((rows, width), F32),
        u_pre=vmem((2, rows // 2, width), F32),
        w2=vmem(w_w.shape, BF),
        w_b2=vmem((1, width), F32),
        cotangent2=vmem((rows // 2, width), BF),
        gu2=vmem((rows // 2, width), BF),
        emb2=vmem((rows // 2, width), BF),
        sa_send=vmem((2, NP, rows // 2 // NP, width), BF),
        sa_recv=vmem((2, NP, rows // 2 // NP, width), BF),
        sa_x=vmem((NP, width, rows // 2 // NP), BF),
        sa_ss=dma((4, NP)),
        sa_rs=dma((4, NP)),
        ga_ss=dma((3, NP + 1)),
        ga_rs=dma((3, NP + 1)),
        lend_ss=dma((4,)),
        lend_rs=dma((4,)),
        give_ss=dma((2,)),
        give_rs=dma((2,)),
        gu=vmem((rows, width), BF),
        gv=vmem((rows, width), BF),
        gb=vmem((rows, width), BF),
        grad_agg=vmem((2 * NP, width, rows // 2 // NP), BF),
        stat=vmem((2, NP, 8, 128), F32),
        small=vmem((8, 8, width), F32),
        zrecv=vmem((5, NQ, width, chunk), BF),
        total_t=vmem((width, chunk), F32),
        stat_ss=dma((NP,)),
        stat_rs=dma((NP,)),
        msg_rs=dma((8, NQ)),
        up_ss=dma((4, NQ)),
        down_ss=dma((4, NQ)),
        y_ss=dma((4, NQ)),
        zx_ss=dma((NQ,)),
        m_zs=dma((4, NQ)),
        m_zr=dma((5, NQ)),
        list_ss=dma((2,)),
        list_rs=dma((2,)),
        gy_ss=dma((2, 2 * NP)),
        gy_rs=dma((2, 2 * NP)),
        m_hs=dma((2, NQ)),
        m_hr=dma((4, 2, NQ)),
        small_ss=dma((7,)),
        small_rs=dma((8,)),
    )
    for name in ("present", "importance", "proj_w", "proj_b", "pin", "q_w", "q_b", "w_w", "w_b", "cotangent"):
        scratch[name] = vmem(inputs[name].shape, inputs[name].dtype)
    for name, out in outs.items():
        scratch[name] = vmem(out.shape, out.dtype)
    for name in ("gb", "gh"):
        scratch[name + "_ss"] = dma((3, NQ))
        scratch[name + "_rs"] = dma((3, NQ))
    for name, w in (("sh", width), ("sb", bwidth)):
        scratch[name + "_send1"] = vmem((2, NQ, chunk, w), BF)
        scratch[name + "_recv1"] = vmem((2, NQ, chunk, w), BF)
        scratch[name + "_sendx"] = vmem((NQ, chunk, w), BF)
        scratch[name + "_recvx"] = vmem((NQ, chunk, w), BF)
        scratch[name + "_ss"] = dma((3, NQ))
        scratch[name + "_rs"] = dma((3, NQ))
    for name, n in (("ww", width), ("wq", width // 2)):
        for part in ("_yrecv", "_zrecv"):
            scratch[name + part] = vmem((4, n, width), BF)
        scratch[name + "_ss"] = dma((2, 4))
        scratch[name + "_rs"] = dma((2, 4))
    for name in ("wp_send", "wp_recv"):
        scratch[name] = vmem((8, bwidth // 2, width), BF)
    for name in ("wp_ss", "wp_rs"):
        scratch[name] = dma((8,))
    place = pl.BlockSpec(memory_space=pl.ANY)
    whole = pl.BlockSpec(memory_space=pltpu.VMEM)
    names = [n + "_in" for n in inputs] + [n + "_out" for n in outs] + list(scratch)
    got = pl.pallas_call(
        functools.partial(fused_kernel, names=tuple(names)),
        out_shape=list(outs.values()),
        in_specs=[place] * len(inputs),
        out_specs=[place] * len(outs),
        scratch_shapes=list(scratch.values()),
        compiler_params=pltpu.CompilerParams(
            collective_id=1, has_side_effects=True, vmem_limit_bytes=63 << 20
        ),
        cost_estimate=pl.CostEstimate(flops=14 << 30, bytes_accessed=8 << 20, transcendentals=0),
    )(*inputs.values())
    row, one = shape((1, width), F32), shape((1, 1), F32)
    emb, g_pin, g_board, g_proj, g_q, g_w, p_b, q_bias, w_bias, count, weight = pl.pallas_call(
        finish_kernel,
        out_shape=list(outs.values())[:6] + [row, row, row, one, one],
        in_specs=[place] * 6 + [whole],
        out_specs=[place] * 6 + [whole] * 5,
        scratch_shapes=[vmem(out.shape, out.dtype) for out in list(outs.values())[:6]] + [dma((2, 6))],
        cost_estimate=pl.CostEstimate(flops=0, bytes_accessed=5 << 20, transcendentals=0),
    )(*got)
    return (
        emb,
        g_pin,
        g_board,
        g_proj,
        p_b.reshape(width),
        g_q,
        q_bias.reshape(width),
        g_w,
        w_bias.reshape(width),
        count.reshape(()),
        weight.reshape(()),
    )


def silu_slope(value):
    sig = jax.nn.sigmoid(value)
    return sig * (1.0 + value * (1.0 - sig))


def slot_table(nbr_block, alpha_block, start, width):
    offsets = nbr_block - start
    places = lax.broadcasted_iota(jnp.int32, (1, 1, width), 2)
    return jnp.sum(jnp.where(offsets[:, :, None] == places, alpha_block[:, :, None], 0.0), axis=1)


def split_pair(table):
    upper = table.astype(jnp.bfloat16)
    lower = (table - upper.astype(jnp.float32)).astype(jnp.bfloat16)
    return (upper, lower)


def collect_rows(nbrs, alphas, table_all):
    total, columns = table_all.shape
    col_tile = math.gcd(total, 2048)
    count_tiles = total // col_tile
    tiles = table_all.reshape(count_tiles, col_tile, columns)
    rows = nbrs.shape[0]
    row_block = math.gcd(rows, 512)
    count_rows = rows // row_block

    def one_rows(pair):
        nbr_block, alpha_block = pair

        def step(acc, index):
            upper, lower = split_pair(
                slot_table(nbr_block, alpha_block, index * col_tile, col_tile)
            )
            piece = tiles[index]
            acc = acc + jnp.dot(upper, piece, preferred_element_type=jnp.float32)
            return (acc + jnp.dot(lower, piece, preferred_element_type=jnp.float32), None)

        acc, unused = lax.scan(
            step, jnp.zeros((row_block, columns), jnp.float32), jnp.arange(count_tiles)
        )
        return acc

    out = lax.map(
        one_rows,
        (nbrs.reshape(count_rows, row_block, -1), alphas.reshape(count_rows, row_block, -1)),
    )
    return out.reshape(rows, columns)


def spread_rows(grads, nbrs, alphas, base, width):
    rows, columns = grads.shape
    row_block = math.gcd(rows, 512)
    count_rows = rows // row_block
    col_tile = math.gcd(width, 2048)
    count_tiles = width // col_tile
    stacked = (
        grads.reshape(count_rows, row_block, columns),
        nbrs.reshape(count_rows, row_block, -1),
        alphas.reshape(count_rows, row_block, -1),
    )
    tdot = (((0,), (0,)), ((), ()))

    def one_tile(index):

        def step(acc, triple):
            grad_block, nbr_block, alpha_block = triple
            upper, lower = split_pair(
                slot_table(nbr_block, alpha_block, base + index * col_tile, col_tile)
            )
            acc = acc + lax.dot_general(upper, grad_block, tdot, preferred_element_type=jnp.float32)
            return (
                acc + lax.dot_general(lower, grad_block, tdot, preferred_element_type=jnp.float32),
                None,
            )

        acc, unused = lax.scan(step, jnp.zeros((col_tile, columns), jnp.float32), stacked)
        return acc

    out = lax.map(one_tile, jnp.arange(count_tiles))
    return out.reshape(width, columns)


def per_device(
    pin_features,
    board_features,
    is_board,
    neighbours,
    present,
    importance,
    proj_weight,
    proj_bias,
    q_weight,
    q_bias,
    w_weight,
    w_bias,
    cotangent,
):
    local_rows = pin_features.shape[0]
    width = q_weight.shape[0]
    filled = present.astype(jnp.float32) * importance
    alpha = filled / jnp.sum(filled, axis=1, keepdims=True)
    board_mask = (is_board == 1)[:, None]
    stat_terms = (jnp.sum(present.astype(jnp.float32)), jnp.sum(filled))
    stat_totals = lax.psum((stat_terms[0], stat_terms[1]), "rows")
    board_full = lax.all_gather(board_features, "cols", axis=1, tiled=True)
    board_proj = jnp.dot(board_full, proj_weight, preferred_element_type=jnp.float32) + proj_bias
    h_local = jnp.where(board_mask, board_proj, pin_features.astype(jnp.float32)).astype(
        jnp.bfloat16
    )
    h_full = lax.all_gather(h_local, "cols", axis=1, tiled=True)
    v_pre = jnp.dot(h_full, q_weight, preferred_element_type=jnp.float32) + q_bias
    message = jax.nn.silu(v_pre).astype(jnp.bfloat16)
    message_all = lax.all_gather(message, "rows", axis=0, tiled=True)
    agg_local = collect_rows(neighbours, alpha, message_all).astype(jnp.bfloat16)
    agg_full = lax.all_gather(agg_local, "cols", axis=1, tiled=True)
    w_self = w_weight[:width]
    w_agg = w_weight[width:]
    u_pre = (
        jnp.dot(h_full, w_self, preferred_element_type=jnp.float32)
        + jnp.dot(agg_full, w_agg, preferred_element_type=jnp.float32)
        + w_bias
    )
    z_act = jax.nn.silu(u_pre)
    squares = lax.psum(jnp.sum(z_act * z_act, axis=1), "cols")
    scale = lax.rsqrt(squares + 1e-06)[:, None]
    embeddings = (z_act * scale).astype(jnp.bfloat16)
    grad_out = cotangent.astype(jnp.float32)
    inner = lax.psum(jnp.sum(grad_out * z_act, axis=1), "cols")[:, None]
    grad_z = grad_out * scale - z_act * scale * scale * scale * inner
    grad_u = (grad_z * silu_slope(u_pre)).astype(jnp.bfloat16)
    agg_part = lax.dot_general(
        grad_u, w_agg, (((1,), (1,)), ((), ())), preferred_element_type=jnp.float32
    )
    grad_agg = lax.psum_scatter(agg_part, "cols", scatter_dimension=1, tiled=True).astype(
        jnp.bfloat16
    )
    table = spread_rows(grad_agg, neighbours, alpha, 0, message_all.shape[0])
    grad_message = lax.psum_scatter(
        table.astype(jnp.bfloat16), "rows", scatter_dimension=0, tiled=True
    ).astype(jnp.float32)
    grad_v = (grad_message * silu_slope(v_pre)).astype(jnp.bfloat16)
    h_part = lax.dot_general(
        grad_u, w_self, (((1,), (1,)), ((), ())), preferred_element_type=jnp.float32
    )
    h_part = h_part + lax.dot_general(
        grad_v, q_weight, (((1,), (1,)), ((), ())), preferred_element_type=jnp.float32
    )
    grad_h = lax.psum_scatter(
        h_part.astype(jnp.bfloat16), "cols", scatter_dimension=1, tiled=True
    ).astype(jnp.float32)
    grad_pin = jnp.where(board_mask, 0.0, grad_h)
    grad_hb = jnp.where(board_mask, grad_h, 0.0).astype(jnp.bfloat16)
    board_part = lax.dot_general(
        grad_hb, proj_weight, (((1,), (1,)), ((), ())), preferred_element_type=jnp.float32
    )
    grad_board = lax.psum_scatter(
        board_part.astype(jnp.bfloat16), "cols", scatter_dimension=1, tiled=True
    ).astype(jnp.float32)
    tdot = (((0,), (0,)), ((), ()))
    grad_w_local = jnp.concatenate(
        [
            lax.dot_general(h_full, grad_u, tdot, preferred_element_type=jnp.float32),
            lax.dot_general(agg_full, grad_u, tdot, preferred_element_type=jnp.float32),
        ],
        axis=0,
    )
    grad_q_local = lax.dot_general(h_full, grad_v, tdot, preferred_element_type=jnp.float32)
    grad_p_local = lax.dot_general(board_full, grad_hb, tdot, preferred_element_type=jnp.float32)
    grad_w, grad_q, grad_proj = (
        lax.psum_scatter(
            grad_w_local.astype(jnp.bfloat16), "rows", scatter_dimension=0, tiled=True
        ).astype(jnp.float32),
        lax.psum_scatter(
            grad_q_local.astype(jnp.bfloat16), "rows", scatter_dimension=0, tiled=True
        ).astype(jnp.float32),
        lax.psum_scatter(
            grad_p_local.astype(jnp.bfloat16), "rows", scatter_dimension=0, tiled=True
        ).astype(jnp.float32),
    )
    bias_terms = (
        jnp.sum(grad_hb.astype(jnp.float32), axis=0),
        jnp.sum(grad_v.astype(jnp.float32), axis=0),
        jnp.sum(grad_u.astype(jnp.float32), axis=0),
    )
    grad_pb, grad_qb, grad_wb = lax.psum((bias_terms[0], bias_terms[1], bias_terms[2]), "rows")
    all_nodes = local_rows * lax.axis_size("rows")
    mean_count = stat_totals[0] / all_nodes
    mean_weight = stat_totals[1] / (all_nodes * SLOTS)
    return (
        embeddings,
        grad_pin,
        grad_board,
        grad_proj,
        grad_pb,
        grad_q,
        grad_qb,
        grad_w,
        grad_wb,
        mean_count,
        mean_weight,
    )


def solution(mesh):
    in_specs = (
        P("rows", "cols"),
        P("rows", "cols"),
        P("rows"),
        P("rows", None),
        P("rows", None),
        P("rows", None),
        P(None, "cols"),
        P("cols"),
        P(None, "cols"),
        P("cols"),
        P(None, "cols"),
        P("cols"),
        P("rows", "cols"),
    )
    out_specs = (
        P("rows", "cols"),
        P("rows", "cols"),
        P("rows", "cols"),
        P("rows", "cols"),
        P("cols"),
        P("rows", "cols"),
        P("cols"),
        P("rows", "cols"),
        P("cols"),
        P(),
        P(),
    )
    fused = mesh.shape["rows"] == 8 and mesh.shape["cols"] == 4
    return jax.shard_map(
        fused_device if fused else per_device, mesh=mesh, in_specs=in_specs, out_specs=out_specs, check_vma=False
    )
```

```python
import functools
import math
import types

import jax
import jax.numpy as jnp
from jax import lax
from jax.experimental import pallas as pl
from jax.experimental.pallas import tpu as pltpu
from jax.sharding import PartitionSpec as P

SLOTS = 50
MESH = pl.DeviceIdType.MESH
BF = jnp.bfloat16
F32 = jnp.float32
NQ = 4
NP = 2
LO_BITS = 7
LO = 1 << LO_BITS
PIECE = 64
NT = (((1,), (1,)), ((), ()))
TN = (((0,), (0,)), ((), ()))


def dot(a, b):
    return jnp.dot(a, b, preferred_element_type=F32)


def dot_nt(a, b):
    return lax.dot_general(a, b, NT, preferred_element_type=F32)


def dot_tn(a, b):
    return lax.dot_general(a, b, TN, preferred_element_type=F32)


def loop(n, body, unroll=1):
    def step(i, carry):
        body(i)
        return carry

    lax.fori_loop(0, n, step, 0, unroll=unroll)


def row_sums(x):
    y = x[:, :128] + x[:, 128:]
    sums = [
        jnp.sum(y[i * 128 : (i + 1) * 128].T, axis=0, keepdims=True) for i in range(x.shape[0] // 128)
    ]
    return sums[0] if len(sums) == 1 else jnp.concatenate(sums, axis=0)


def down(row):
    return jnp.broadcast_to(row, (128, 128)).T


def down_rows(rows):
    cols = [down(rows[i : i + 1]) for i in range(rows.shape[0])]
    col = cols[0] if len(cols) == 1 else jnp.concatenate(cols, axis=0)
    return jnp.concatenate([col, col], axis=1)


def fused_kernel(*refs, names):
    s = types.SimpleNamespace(**dict(zip(names, refs)))
    r = lax.axis_index("rows")
    c = lax.axis_index("cols")
    z, y = r // 2, r % 2
    x, k = c // 2, c % 2
    rows, width = s.pin.shape
    bwidth = s.boards.shape[2]
    chunk = rows // NQ
    zn = 4
    per_block = rows // LO
    core = (r, x * 2 + 1 - k)
    xp = (r, (1 - x) * 2 + k)
    diagonal = (z * 2 + 1 - y, (1 - x) * 2 + k)
    yp = (z * 2 + 1 - y, c)
    upper = z // 2
    inner = (z % 2) + upper * (1 - 2 * (z % 2))
    zx = z + 1 - 2 * (z % 2)
    zxp = (zx * 2 + y, c)

    def at(q):
        return pl.ds(pl.multiple_of(q * chunk, chunk), chunk)

    def rdma(src, dst, send, recv, dev):
        return pltpu.make_async_remote_copy(
            src_ref=src, dst_ref=dst, send_sem=send, recv_sem=recv, device_id=dev, device_id_type=MESH
        )

    def arrived(ref, sem):
        rdma(ref, ref, sem, sem, core).wait_recv()

    def sent(ref, sem):
        rdma(ref, ref, sem, sem, core).wait_send()

    class Gather:
        def __init__(self, buf, base, ss, rs):
            self.buf, self.base, self.ss, self.rs = buf, base, ss, rs

        def ref(self, col, q):
            return self.buf.at[self.base + col, at(q)]

        def start(self, q):
            own = self.ref(c, q)
            rdma(own, own, self.ss.at[1, q], self.rs.at[1, q], xp).start()
            rdma(own, own, self.ss.at[0, q], self.rs.at[0, q], core).start()

        def forward(self, q):
            got = self.ref((1 - x) * 2 + k, q)
            arrived(got, self.rs.at[1, q])
            rdma(got, got, self.ss.at[2, q], self.rs.at[2, q], core).start()

        def finish(self, q):
            arrived(self.ref(x * 2 + 1 - k, q), self.rs.at[0, q])
            arrived(self.ref((1 - x) * 2 + 1 - k, q), self.rs.at[2, q])

        def drain(self, q):
            for i in range(3):
                sent(self.ref(c, q), self.ss.at[i, q])

    class Scatter:
        def __init__(self, part, name):
            self.part = part
            self.send1, self.recv1 = getattr(s, name + "_send1"), getattr(s, name + "_recv1")
            self.sendx, self.recvx = getattr(s, name + "_sendx"), getattr(s, name + "_recvx")
            self.ss, self.rs = getattr(s, name + "_ss"), getattr(s, name + "_rs")

        def first(self, q):
            for i, xs in ((0, 1 - x), (1, x)):
                self.send1[i, q] = self.part(xs * 2 + 1 - k, q).astype(BF)
                rdma(
                    self.send1.at[i, q], self.recv1.at[i, q], self.ss.at[i, q], self.rs.at[i, q], core
                ).start()

        def second(self, q):
            own = self.part((1 - x) * 2 + k, q)
            arrived(self.recv1.at[0, q], self.rs.at[0, q])
            self.sendx[q] = (own + self.recv1[0, q].astype(F32)).astype(BF)
            rdma(self.sendx.at[q], self.recvx.at[q], self.ss.at[2, q], self.rs.at[2, q], xp).start()

        def third(self, q):
            own = self.part(c, q)
            arrived(self.recv1.at[1, q], self.rs.at[1, q])
            own = own + self.recv1[1, q].astype(F32)
            arrived(self.recvx.at[q], self.rs.at[2, q])
            return own + self.recvx[q].astype(F32)

        def drain(self, q):
            for i in range(2):
                sent(self.send1.at[i, q], self.ss.at[i, q])
            sent(self.sendx.at[q], self.ss.at[2, q])

    class WeightSum:
        def __init__(self, part, name, out, ysend, zsend):
            self.part, self.out = part, out
            self.ysend, self.zsend = ysend, zsend
            self.yrecv, self.zrecv = getattr(s, name + "_yrecv"), getattr(s, name + "_zrecv")
            self.ss, self.rs = getattr(s, name + "_ss"), getattr(s, name + "_rs")

        def first(self, at0=0, n=4):
            def step(i):
                d = at0 + i
                ref = self.ysend(d)
                ref[...] = self.part(d, 1 - y, True).astype(BF)
                rdma(ref, self.yrecv.at[d], self.ss.at[0, d], self.rs.at[0, d], yp).start()

            loop(n, step, unroll=n)

        def second(self, at0=0, n=4):
            def step(i):
                d = at0 + i
                own = self.part(d, y)
                arrived(self.yrecv.at[d], self.rs.at[0, d])
                own = own + self.yrecv[d].astype(F32)

                @pl.when(d == z)
                def _():
                    self.out[...] = own

                @pl.when(d != z)
                def _():
                    ref = self.zsend(d)
                    ref[...] = own.astype(BF)
                    rdma(
                        ref, self.zrecv.at[z], self.ss.at[1, d], self.rs.at[1, z], (d * 2 + y, c)
                    ).start()

            loop(n, step)

        def third(self):
            def step(d):
                @pl.when(d != z)
                def _():
                    arrived(self.zrecv.at[d], self.rs.at[1, d])
                    self.out[...] += self.zrecv[d].astype(F32)

            loop(zn, step)

        def drain(self):
            def step(d):
                sent(self.ysend(d), self.ss.at[0, d])

                @pl.when(d != z)
                def _():
                    sent(self.zsend(d), self.ss.at[1, d])

            loop(zn, step)

    class PairSum(WeightSum):
        def first(self):
            for d in ((zx + 2) % 4, zx, (z + 2) % 4, z):
                ref = self.ysend(d)
                ref[...] = self.part(d, 1 - y, True).astype(BF)
                rdma(ref, self.yrecv.at[d], self.ss.at[0, d], self.rs.at[0, d], yp).start()

        def total(self, d):
            own = self.part(d, y)
            arrived(self.yrecv.at[d], self.rs.at[0, d])
            return own + self.yrecv[d].astype(F32)

        def second(self):
            for n, d in enumerate(((zx + 2) % 4, zx)):
                ref = self.zsend(n)
                ref[...] = self.total(d).astype(BF)
                rdma(ref, self.zrecv.at[n], self.ss.at[1, n], self.rs.at[1, n], zxp).start()

        def across(self):
            d = (z + 2) % 4
            ref = self.zsend(2)
            own = self.total(d)
            arrived(self.zrecv.at[0], self.rs.at[1, 0])
            ref[...] = (own + self.zrecv[0].astype(F32)).astype(BF)
            rdma(ref, self.zrecv.at[2], self.ss.at[1, 2], self.rs.at[1, 2], (d * 2 + y, c)).start()

        def third(self):
            own = self.total(z)
            for n in (1, 2):
                arrived(self.zrecv.at[n], self.rs.at[1, n])
                own = own + self.zrecv[n].astype(F32)
            self.out[...] = own

        def drain(self):
            for d in range(zn):
                sent(self.ysend(d), self.ss.at[0, d])
            for n in range(3):
                sent(self.zsend(n), self.ss.at[1, n])

    barrier = pltpu.get_barrier_semaphore()

    def greet(dev):
        pl.semaphore_signal(barrier, inc=1, device_id=dev, device_id_type=MESH)

    near_by = (xp, yp, diagonal, core)
    for dev in near_by:
        greet(dev)

    @pl.when(z < 3)
    def _():
        greet(((z + 1) * 2 + y, c))

    @pl.when(z > 0)
    def _():
        greet(((z - 1) * 2 + y, c))

    boards, own_h = s.boards, s.ha
    in_sem = s.in_sem
    loads = {}
    order = (
        ("board", boards.at[c]),
        ("is_board", s.flags),
        ("proj_w", s.proj_w),
        ("proj_b", s.proj_b),
        ("pin", s.pin),
        ("neighbours", s.numbers),
        ("present", s.present),
        ("importance", s.importance),
        ("q_w", s.q_w),
        ("q_b", s.q_b),
        ("w_w", s.w_w),
        ("w_b", s.w_b),
        ("cotangent", s.cotangent),
    )
    for i, (name, ref) in enumerate(order):
        loads[name] = pltpu.make_async_copy(getattr(s, name + "_in"), ref, in_sem.at[i])
        loads[name].start()

    out_sem = s.out_sem

    def store(i, q, src, dst):
        return pltpu.make_async_copy(src, dst, out_sem.at[i, q])

    gather_b = Gather(boards, 0, s.gb_ss, s.gb_rs)
    gather_h = Gather(own_h, 0, s.gh_ss, s.gh_rs)
    loads["board"].wait()
    pl.semaphore_wait(barrier, len(near_by) + 1 + inner)
    loop(NQ, gather_b.start)

    mask = s.mask
    loads["is_board"].wait()
    flags = s.flags[...].astype(F32)
    for i in range(rows // 128):
        mask[i * 128 : (i + 1) * 128] = down(flags[i : i + 1])

    half = rows // 2
    padded = s.padded
    list_ss, list_rs = s.list_ss, s.list_rs

    quarter = rows // 4

    def lay(ref):
        for t in range(2):
            for i in range(quarter // 128):
                a, b = 2 * t * quarter + i * 128, (2 * t + 1) * quarter + i * 128
                ref[t, i * 128 : (i + 1) * 128] = jnp.concatenate(
                    [padded[:, a : a + 128], padded[:, b : b + 128]], axis=0
                ).T

    def lend_list(i):
        src, dst = ((s.numbers, s.numbers2), (s.alpha, s.alpha2))[i]
        return rdma(src, dst, list_ss.at[i], list_rs.at[i], yp)

    def prepare():
        for name in ("neighbours", "present", "importance"):
            loads[name].wait()
        lend_list(0).start()
        present = s.present[...].astype(F32)
        filled = present * s.importance[...]
        padded[SLOTS:] = jnp.zeros((padded.shape[0] - SLOTS, rows), F32)
        padded[:SLOTS] = filled / jnp.sum(filled, axis=0, keepdims=True)
        s.alpha[...] = padded[...].astype(BF)
        lend_list(1).start()
        lay(s.weight)
        small = s.small
        small[r] = jnp.zeros(small.shape[1:], F32)
        small[r, 3:4] = jnp.concatenate(
            [
                jnp.broadcast_to(jnp.sum(present).reshape(1, 1), (1, 128)),
                jnp.broadcast_to(jnp.sum(filled).reshape(1, 1), (1, 128)),
            ],
            axis=1,
        )
        numbers = s.numbers[...]
        padded[:SLOTS] = (numbers >> LO_BITS).astype(F32)
        lay(s.high)
        padded[:SLOTS] = (numbers & (LO - 1)).astype(F32)
        lay(s.low)

    def prepare2():
        for i in range(2):
            lend_list(i).wait_recv()
        numbers = s.numbers2[...]
        high = numbers >> LO_BITS
        place = (high // (2 * per_block)) * per_block + high % per_block
        padded[:SLOTS] = jnp.where((high // per_block) % 2 == y, place, -1).astype(F32)
        lay(s.high2)
        padded[:SLOTS] = (numbers & (LO - 1)).astype(F32)
        lay(s.low2)
        padded[...] = s.alpha2[...].astype(F32)
        lay(s.weight2)

    def mask_of(q):
        m = mask[at(q)] > 0.5
        return jnp.concatenate([m, m], axis=1)

    table, stage = s.table, s.stage
    pitch = stage.shape[0] // 64
    piece_rows = PIECE // 4

    def build(i, lists, table):
        n_high = 2 * table.shape[0]
        iota = lax.broadcasted_iota(jnp.int32, (128, 128), 0).astype(F32).astype(BF)
        front = lax.broadcasted_iota(jnp.int32, (16, 128), 1) < 64
        zero, one = jnp.zeros((), BF), jnp.ones((), BF)

        def tiles(v, n):
            return jnp.concatenate([v] * n, axis=0)

        zeros = jnp.zeros((n_high, 128), BF)
        n = n_high // 16

        def four(j):
            p = i * piece_rows + j
            weights, places = [], []
            for t in range(2):

                def row(ref):
                    return jnp.broadcast_to(ref[t, pl.ds(p, 1), :], (16, 128))

                hi, lo, al = row(lists[0]).astype(BF), row(lists[1]).astype(BF), row(lists[2])
                places.append(jnp.where(tiles(lo, 8) == iota, one, zero))
                same = tiles(hi, n) == iota[:n_high]
                for a in (jnp.where(front, al, 0.0), jnp.where(front, 0.0, al)):
                    w = jnp.where(same, tiles(a.astype(BF), n), zero)
                    weights.append(jnp.concatenate([w, zeros] if t == 0 else [zeros, w], axis=1))
            out = dot_nt(jnp.concatenate(weights, axis=0), jnp.concatenate(places, axis=1))
            for g in range(4):
                stage[pl.ds(j + g * piece_rows, n_high, stride=pitch), :] = out[
                    g * n_high : (g + 1) * n_high
                ]

        loop(piece_rows, four, unroll=16)

        def convert(h):
            for f in range(2):
                base = (2 * h + f) * pitch
                for g in range(4):
                    table[
                        h,
                        pl.ds(pl.multiple_of(i * piece_rows + g * quarter, 16), piece_rows),
                        f * 128 : (f + 1) * 128,
                    ] = stage[
                        pl.ds(pl.multiple_of(base + g * piece_rows, 8), piece_rows), :
                    ].astype(BF)

        loop(table.shape[0], convert, unroll=4)

    lists1 = (s.high, s.low, s.weight)
    lists2 = (s.high2, s.low2, s.weight2)
    table2 = s.table2

    def piece(i):
        build(i, lists1, table)

    def piece2(i):
        build(i, lists2, table2)

    n_pieces = rows // PIECE

    message, v_pre = s.message, s.v_pre

    def make_h(q):
        lines = at(q)
        b01 = jnp.concatenate([boards[0, lines], boards[1, lines]], axis=1)
        b23 = jnp.concatenate([boards[2, lines], boards[3, lines]], axis=1)
        proj = dot(b01, s.proj_w[: 2 * bwidth]) + dot(b23, s.proj_w[2 * bwidth :]) + s.proj_b[...]
        own_h[c, lines] = jnp.where(mask_of(q), proj, s.pin[lines].astype(F32)).astype(BF)

    def block(zb, yb, q):
        return message.at[zb * 2 + yb, q]

    def send_up(zb, q):
        ref = block(zb, y, q)
        rdma(ref, ref, s.up_ss.at[zb, q], s.msg_rs.at[zb * 2 + y, q], ((z + 1) * 2 + y, c)).start()

    def send_down(zb, q):
        ref = block(zb, y, q)
        rdma(ref, ref, s.down_ss.at[zb, q], s.msg_rs.at[zb * 2 + y, q], ((z - 1) * 2 + y, c)).start()

    def send_y(zb, q):
        ref = block(zb, y, q)
        rdma(ref, ref, s.y_ss.at[zb, q], s.msg_rs.at[zb * 2 + y, q], yp).start()

    def make_message(q):
        lines = at(q)
        acc = dot(own_h[0, lines], s.q_w[:width])
        for i in range(1, 4):
            acc = acc + dot(own_h[i, lines], s.q_w[i * width : (i + 1) * width])
        v = acc + s.q_b[...]
        v_pre[lines] = v
        message[r, q] = (v * jax.nn.sigmoid(v)).astype(BF)

        @pl.when(z < 3)
        def _():
            send_up(z, q)

        @pl.when(z > 0)
        def _():
            send_down(z, q)

        send_y(z, q)

    prepare()
    for name in ("proj_w", "proj_b", "pin"):
        loads[name].wait()

    def board_phase(q):
        gather_b.forward(q)
        gather_b.finish(q)
        make_h(q)
        gather_h.start(q)

    piece(0)
    loop(NQ, board_phase)
    early = 3
    loop(early - 1, lambda i: piece(1 + i))

    half = rows // 2
    sub = half // NP
    own_half = pl.ds(pl.multiple_of(x * half, half), half)
    their_half = pl.ds(pl.multiple_of((1 - x) * half, half), half)
    lend_ss, lend_rs = s.lend_ss, s.lend_rs
    wide = 4 * width

    def lends():
        return (
            (s.w_w.at[:wide], s.w2.at[:wide]),
            (s.w_b, s.w_b2),
            (s.w_w.at[wide:], s.w2.at[wide:]),
            (s.cotangent.at[their_half], s.cotangent2),
        )

    def lend(i):
        src, dst = lends()[i]
        return rdma(src, dst, lend_ss.at[i], lend_rs.at[i], xp)

    for name in ("w_w", "w_b", "cotangent"):
        loads[name].wait()
    for i in range(4):
        lend(i).start()
    loads["q_w"].wait()
    loads["q_b"].wait()

    def message_phase(q):
        gather_h.forward(q)
        gather_h.finish(q)
        make_message(q)
        piece(early + q)

        @pl.when(q % 2 == 0)
        def _():
            piece(early + NQ + q // 2)

    loop(NQ, message_phase)
    built = early + NQ + NQ // 2

    u_pre = s.u_pre

    def part_of(i):
        return pl.ds(pl.multiple_of(i * sub, sub), sub)

    def mine(i):
        return pl.ds(pl.multiple_of(x * half + i * sub, sub), sub)

    def theirs(i):
        return pl.ds(pl.multiple_of((1 - x) * half + i * sub, sub), sub)

    def u_from_h(i):
        for n, w, b in ((0, s.w_w, s.w_b), (1, s.w2, s.w_b2)):
            acc = dot(own_h[0, mine(i)], w[:width])
            for m in range(1, 4):
                acc = acc + dot(own_h[m, mine(i)], w[m * width : (m + 1) * width])
            u_pre[n, part_of(i)] = acc + b[...]

    agg = s.grad_pin
    parts = rows // chunk

    def add(b, first, n):
        for i in range(parts):
            lines = slice(i * chunk, (i + 1) * chunk)
            acc = agg[lines]
            for q in range(first, first + n):
                acc = acc + dot(table[b * NQ + q, lines], message[b, q])
            agg[lines] = acc

    def over_y(zb, q):
        @pl.when((zb != zx) | ((inner == 0) & (q < NQ // 2)))
        def _():
            send_y(zb, q)

    def send_zx(q):
        ref = block(z, 1 - y, q)
        rdma(ref, ref, s.zx_ss.at[q], s.msg_rs.at[z * 2 + 1 - y, q], zxp).start()

    def at_z(zb):
        return (zb >= 0) & (zb <= 3)

    n_second = 3 * NQ
    n_second2 = n_pieces // 2
    steps = n_pieces - built

    def second_phase(i):
        t, q = 1 + i // NQ, i % NQ

        @pl.when(z - t >= 0)
        def _():
            arrived(block(z - t, y, q), s.msg_rs.at[(z - t) * 2 + y, q])

            @pl.when(z < 3)
            def _():
                send_up(z - t, q)

            over_y(z - t, q)

        @pl.when(z + t <= 3)
        def _():
            arrived(block(z + t, y, q), s.msg_rs.at[(z + t) * 2 + y, q])

            @pl.when(z > 0)
            def _():
                send_down(z + t, q)

            over_y(z + t, q)

        @pl.when(t == 1)
        def _():
            arrived(block(z, 1 - y, q), s.msg_rs.at[z * 2 + 1 - y, q])

            @pl.when(inner == 0)
            def _():
                send_zx(q)

        @pl.when((t == 3) & (inner == 1) & (q >= NQ // 2))
        def _():
            send_zx(q)

        @pl.when(i < steps)
        def _():
            piece(built + i)

        @pl.when(i == 0)
        def _():
            prepare2()

        @pl.when((i > 0) & (i < 1 + n_second2))
        def _():
            loop(2, lambda n: piece2(2 * (i - 1) + n))

        @pl.when(i == steps)
        def _():
            agg[...] = jnp.zeros_like(agg)
            lend(0).wait_recv()
            lend(1).wait_recv()

        @pl.when(i >= n_second - NP)
        def _():
            u_from_h(i - (n_second - NP))

        @pl.when((i >= n_second - 5) & (i < n_second))
        def _():
            n = i - (n_second - 5)
            zb = z + jnp.where(n == 0, 0, jnp.where(n == 1, -1, jnp.where(n == 2, 1, jnp.where(n == 3, -2, 2))))

            @pl.when(at_z(zb))
            def _():
                add(zb * 2 + y, 0, NQ)

    loop(n_second, second_phase)

    add(z * 2 + 1 - y, 0, NQ)

    @pl.when(inner == 0)
    def _():
        add((3 - z) * 2 + y, 0, NQ)

    def add_arriving(zb, first, n):
        b = zb * 2 + 1 - y
        loop(n, lambda q: arrived(message.at[b, first + q], s.msg_rs.at[b, first + q]))
        add(b, first, n)

    add_arriving(zx, 0, NQ // 2)
    add_arriving(2 - upper, 0, NQ)
    for q in range(NQ):
        blocks = [3 * (1 - upper) * 2 + 1 - y] + ([zx * 2 + 1 - y] if q >= NQ // 2 else [])
        for b in blocks:
            arrived(message.at[b, q], s.msg_rs.at[b, q])
        for i in range(parts):
            lines = slice(i * chunk, (i + 1) * chunk)
            acc = agg[lines]
            for b in blocks:
                acc = acc + dot(table[b * NQ + q, lines], message[b, q])
            if q < NQ - 1:
                agg[lines] = acc
            else:
                own_h[4 + c, lines] = acc.astype(BF)

    gu, gv, gb, gu2 = s.gu, s.gv, s.gb, s.gu2
    stat, stat_ss, stat_rs = s.stat, s.stat_ss, s.stat_rs
    ga_ss, ga_rs = s.ga_ss, s.ga_rs
    other_x = (1 - x) * 2 + k

    def agg_ref(col, lines):
        return own_h.at[4 + col, lines]

    def agg_start(i):
        a, b = agg_ref(c, theirs(i)), agg_ref(c, mine(i))
        rdma(a, a, ga_ss.at[1, i], ga_rs.at[1, i], xp).start()
        rdma(b, b, ga_ss.at[0, i], ga_rs.at[0, i], core).start()

    def agg_forward(i):
        got = agg_ref(other_x, mine(i))
        arrived(got, ga_rs.at[1, i])
        rdma(got, got, ga_ss.at[2, i], ga_rs.at[2, i], core).start()

    def agg_finish(i):
        arrived(agg_ref(x * 2 + 1 - k, mine(i)), ga_rs.at[0, i])
        arrived(agg_ref((1 - x) * 2 + 1 - k, mine(i)), ga_rs.at[2, i])

    def rest_start():
        a, b = agg_ref(c, own_half), agg_ref(c, their_half)
        rdma(a, a, ga_ss.at[1, NP], ga_rs.at[1, NP], xp).start()
        rdma(b, b, ga_ss.at[0, NP], ga_rs.at[0, NP], core).start()

    def rest_forward():
        got = agg_ref(other_x, their_half)
        arrived(got, ga_rs.at[1, NP])
        rdma(got, got, ga_ss.at[2, NP], ga_rs.at[2, NP], core).start()

    def rest_finish():
        arrived(agg_ref(x * 2 + 1 - k, their_half), ga_rs.at[0, NP])
        arrived(agg_ref((1 - x) * 2 + 1 - k, their_half), ga_rs.at[2, NP])

    loop(NP, agg_start)
    lend(2).wait_recv()
    lend(3).wait_recv()

    def gradients(i):
        return s.cotangent[mine(i)].astype(F32), s.cotangent2[part_of(i)].astype(F32)

    def make_u(i):
        us = [u_pre[n, part_of(i)] for n in range(2)]
        for m in range(4):
            a = own_h[4 + m, mine(i)]
            us = [u + dot(a, w[(4 + m) * width : (5 + m) * width]) for u, w in zip(us, (s.w_w, s.w2))]
        squares, inners = 0.0, 0.0
        for n, (u, g) in enumerate(zip(us, gradients(i))):
            u_pre[n, part_of(i)] = u
            zz = u * jax.nn.sigmoid(u)
            squares = squares + zz * zz
            inners = inners + g * zz
        pad = jnp.zeros((8 - 2 * sub // 128, 128), F32)
        stat[0, i] = jnp.concatenate([row_sums(squares), row_sums(inners), pad], axis=0)
        rdma(stat.at[0, i], stat.at[1, i], stat_ss.at[i], stat_rs.at[i], core).start()

    def make_gu(i):
        arrived(stat.at[1, i], stat_rs.at[i])
        total = stat[0, i] + stat[1, i]
        n_rows = sub // 128
        rr = lax.rsqrt(total[:n_rows] + 1e-6)
        scale = down_rows(rr)
        pull = down_rows(rr * rr * rr * total[n_rows : 2 * n_rows])
        for n, (g, emb, grad) in enumerate(
            zip(gradients(i), (s.embeddings, s.emb2), (gu, gu2))
        ):
            u = u_pre[n, part_of(i)]
            sig = jax.nn.sigmoid(u)
            zz = u * sig
            lines = mine(i) if n == 0 else part_of(i)
            emb[lines] = (zz * scale).astype(BF)
            grad[lines] = ((g * scale - zz * pull) * (sig * (1.0 + u * (1.0 - sig)))).astype(BF)

    def agg_part(col, i):
        lines = pl.ds(pl.multiple_of((4 + col) * width, width), width)
        return dot_nt(gu[mine(i)], s.w_w[lines, :]) + dot_nt(gu2[part_of(i)], s.w2[lines, :])

    grad_agg, grad_agg2 = s.grad_agg, s.grad_agg2
    sa_send, sa_recv, sa_x, sa_ss, sa_rs = s.sa_send, s.sa_recv, s.sa_x, s.sa_ss, s.sa_rs

    def agg_first(i):
        for n, xs in ((0, 1 - x), (1, x)):
            sa_send[n, i] = agg_part(xs * 2 + 1 - k, i).astype(BF)
            rdma(sa_send.at[n, i], sa_recv.at[n, i], sa_ss.at[n, i], sa_rs.at[n, i], core).start()

    def part_c(h):
        return pl.ds(h * (width // 2), width // 2)

    def agg_second(i):
        own = agg_part(other_x, i)
        arrived(sa_recv.at[0, i], sa_rs.at[0, i])
        sa_x[i] = (own + sa_recv[0, i].astype(F32)).T.astype(BF)
        here, there = x * NP + i, (1 - x) * NP + i
        for h in range(2):
            src = sa_x.at[i, part_c(h)]
            if i == NP - 1:
                to = grad_agg2.at[here, part_c(h)]
                rdma(src, to, s.gy_ss.at[h, there], s.gy_rs.at[h, here], diagonal).start()
            rdma(src, grad_agg.at[here, part_c(h)], sa_ss.at[2 + h, i], sa_rs.at[2 + h, i], xp).start()

    def agg_third(i):
        own = agg_part(c, i)
        arrived(sa_recv.at[1, i], sa_rs.at[1, i])
        grad_agg[x * NP + i] = (own + sa_recv[1, i].astype(F32)).T.astype(BF)
        agg_over_y(x * NP + i)

    def agg_over_y(i, halves=(0, 1)):
        for h in halves:
            rdma(
                grad_agg.at[i, part_c(h)],
                grad_agg2.at[i, part_c(h)],
                s.gy_ss.at[h, i],
                s.gy_rs.at[h, i],
                yp,
            ).start()

    def room(at_block, n):
        return [lambda d, b=b, n=n: message.at[b, d, pl.ds(0, n)] for b in (at_block, at_block + 1)]

    def room_narrow(at_block, n):
        return [lambda d, i=i: message.at[at_block, d, pl.ds(i * n, n)] for i in range(2)]

    sum_w = WeightSum(lambda d, yy, first=False: dot_tn(own_h[d * 2 + yy], gu[...]), "ww", s.grad_w, *room(4, width))

    def half_phases():
        for i in range(NP):
            agg_forward(i)
            if i > 0:
                make_gu(i - 1)
                agg_first(i - 1)
            agg_finish(i)
            make_u(i)
            if i > 0:
                agg_second(i - 1)
                agg_third(i - 1)
        make_gu(NP - 1)
        agg_first(NP - 1)
        agg_second(NP - 1)
        agg_third(NP - 1)

    half_phases()

    def give(n):
        src, dst = ((gu2, gu.at[own_half]), (s.emb2, s.embeddings.at[own_half]))[n]
        return rdma(src, dst, s.give_ss.at[n], s.give_rs.at[n], xp)

    def give_back(n):
        ref = (gu, s.embeddings)[n].at[their_half]
        return rdma(ref, ref, s.give_ss.at[n], s.give_rs.at[n], xp)

    give(0).start()
    rest_start()
    give(1).start()
    def arrived_x(i, h):
        arrived(grad_agg.at[(1 - x) * NP + i, part_c(h)], sa_rs.at[2 + h, i])

    for i in range(NP - 1):
        for h in range(2):
            arrived_x(i, h)
            agg_over_y((1 - x) * NP + i, (h,))

    def gradients_here(h):
        arrived_x(NP - 1, h)
        for i in range(2 * NP):
            arrived(grad_agg2.at[i, part_c(h)], s.gy_rs.at[h, i])

    def sent_messages(q):
        @pl.when(z < 3)
        def _():
            sent(block(z, y, q), s.up_ss.at[z, q])

        @pl.when(z > 0)
        def _():
            sent(block(z, y, q), s.down_ss.at[z, q])

        for t in range(1, 4):
            @pl.when((z - t >= 0) & (z < 3))
            def _():
                sent(block(z, y, q), s.up_ss.at[z - t, q])

            @pl.when((z + t <= 3) & (z > 0))
            def _():
                sent(block(z, y, q), s.down_ss.at[z + t, q])

        for zb in range(4):
            @pl.when((zb != zx) | ((inner == 0) & (q < NQ // 2)))
            def _():
                sent(block(z, y, q), s.y_ss.at[zb, q])

        @pl.when((inner == 0) | (q >= NQ // 2))
        def _():
            sent(block(z, y, q), s.zx_ss.at[q])

    loop(NQ, sent_messages)

    zsend, zrecv = message, s.zrecv
    m_zs, m_zr = s.m_zs, s.m_zr
    adjust = (0, 0, -1, 1)

    def dest(j):
        base = 3 - j + inner * adjust[j]
        return base + upper * (3 - 2 * base)

    each = 2 * NP // NQ

    def sum_of(terms):
        total = None
        for term in terms:
            total = term if total is None else total + term
        return total

    def spread(d, q, c0=0, nc=width):
        own, other = (d * 2 + y) * NQ + q, d * NQ + q
        n = sub
        return sum_of(
            dot(ref[m, c0 : c0 + nc], tab[b, m * n : (m + 1) * n])
            for ref, tab, b in ((grad_agg, table, own), (grad_agg2, table2, other))
            for m in range(2 * NP)
        )

    small = s.small

    def column_sums(i, ref):
        small[r, i : i + 1] = dot(jnp.ones((16, rows), BF), ref[...])[0:1]

    m_hs, m_hr = s.m_hs, s.m_hr

    def target(j):
        d = dest(j)
        step = 1 - 2 * upper
        if j == 2:
            step = step * (1 - 2 * inner)
        is_dest = (0, inner, 1)[j]
        slot = d + is_dest * ((1 - step) // 2) * (4 - d)
        return d, slot, ((z + step) * 2 + y, c)

    def along_half(q, h):
        d, slot, dev = target(0)
        lines = part_c(h)
        own = spread(d, q, h * (width // 2), width // 2)

        @pl.when(inner == 0)
        def _():
            zsend[d, q, lines] = own.astype(BF)

        @pl.when(inner == 1)
        def _():
            arrived(zrecv.at[d, q, lines], m_hr.at[d, h, q])
            zsend[d, q, lines] = (own + zrecv[d, q, lines].astype(F32)).astype(BF)

        rdma(
            zsend.at[d, q, lines], zrecv.at[slot, q, lines], m_hs.at[h, q], m_hr.at[slot, h, q], dev
        ).start()

    def along(j, q):
        d, slot, dev = target(j)
        own = spread(d, q)

        @pl.when(inner == 0)
        def _():
            zsend[d, q] = own.astype(BF)

        @pl.when(inner == 1)
        def _():
            if j == 1:
                arrived(zrecv.at[d, q], m_zr.at[d, q])
            else:
                for h in range(2):
                    arrived(zrecv.at[d, q, part_c(h)], m_hr.at[d, h, q])
            zsend[d, q] = (own + zrecv[d, q].astype(F32)).astype(BF)

        rdma(zsend.at[d, q], zrecv.at[slot, q], m_zs.at[d, q], m_zr.at[slot, q], dev).start()

    for h in range(2):
        gradients_here(h)
        loop(NQ, lambda q, h=h: along_half(q, h))
        if h == 0:

            @pl.when(inner == 1)
            def _():
                give_back(0).wait_recv()
                sum_w.first(0, 2)

    @pl.when(inner == 0)
    def _():
        for j in (1, 2):
            loop(NQ, lambda q, j=j: along(j, q))
        give_back(0).wait_recv()
        sum_w.first(0, 2)

    rest_forward()
    rest_finish()
    sum_w.first(2, 2)
    column_sums(2, gu)

    @pl.when(inner == 1)
    def _():
        def both_ways(q):
            along(2, q)
            along(1, q)

        loop(NQ, both_ways)

    give_back(1).wait_recv()
    store(0, 0, s.embeddings, s.embeddings_out).start()

    total_t = s.total_t

    def make_gv(q):
        total_t[...] = spread(z, q)

        @pl.when(z > 0)
        def _():
            arrived(zrecv.at[z, q], m_zr.at[z, q])
            total_t[...] += zrecv[z, q].astype(F32)

        @pl.when(z < 3)
        def _():
            arrived(zrecv.at[4, q], m_zr.at[4, q])
            total_t[...] += zrecv[4, q].astype(F32)

        v = v_pre[at(q)]
        sig = jax.nn.sigmoid(v)
        gv[at(q)] = (total_t[...].T * (sig * (1.0 + v * (1.0 - sig)))).astype(BF)

    def h_part(col, q):
        lines = pl.ds(pl.multiple_of(col * width, width), width)
        return dot_nt(gu[at(q)], s.w_w[lines, :]) + dot_nt(gv[at(q)], s.q_w[lines, :])

    def b_part(col, q):
        lines = pl.ds(pl.multiple_of(col * bwidth, bwidth), bwidth)
        return dot_nt(gb[at(q)], s.proj_w[lines, :])

    scatter_h, scatter_b = Scatter(h_part, "sh"), Scatter(b_part, "sb")


    def q_part(d, yy, first=False):
        n = width // 2
        keep = u_pre.at[0, pl.ds(d * n, n)]
        if not first:
            return keep[...]
        both = dot_tn(own_h[d], gv[...])
        keep[...] = jnp.where(y == 0, both[:n], both[n:])
        return jnp.where(y == 0, both[n:], both[:n])

    sum_q = PairSum(q_part, "wq", s.grad_q, *room_narrow(6, width // 2))
    small_ss, small_rs = s.small_ss, s.small_rs

    def so_far(d):
        return u_pre.at[1, pl.ds(d * bwidth, bwidth)]

    def add_proj(q):
        for d in range(4):
            got = dot_tn(boards[d, at(q)], gb[at(q)])

            @pl.when(q == 0)
            def _():
                so_far(d)[...] = got

            @pl.when(q > 0)
            def _():
                so_far(d)[...] += got

    def proj_part(d, yy, first=False):
        last = slice((NQ - 1) * chunk, NQ * chunk)
        n = bwidth // 2
        both = so_far(d)[...]
        if first:
            both = both + dot_tn(boards[d, last], gb[last])
            so_far(d)[...] = both
            return jnp.where(y == 0, both[n:], both[:n])
        return jnp.where(y == 0, both[:n], both[n:])

    sum_p = WeightSum(proj_part, "wp", s.grad_p, *room_narrow(7, bwidth // 2))

    def send_small():
        column_sums(0, gb)
        for d in range(1, 8):
            rdma(
                small.at[r], small.at[r], small_ss.at[d - 1], small_rs.at[r], ((r + d) % 8, c)
            ).start()

    def finish_board(q):
        s.grad_board[at(q)] = scatter_b.third(q)
        store(2, q, s.grad_board.at[at(q)], s.grad_board_out.at[at(q)]).start()

    def fourth_phase(t):
        @pl.when(t < NQ)
        def _():
            make_gv(t)
            scatter_h.first(t)

        @pl.when((t >= 3) & (t < NQ + 2))
        def _():
            scatter_b.second(t - 3)

        @pl.when(t == NQ - 1)
        def _():
            scatter_h.second(t)
            sum_q.first()

        @pl.when((t >= 2) & (t < NQ + 2))
        def _():
            q = t - 2
            g = scatter_h.third(q)
            m = mask_of(q)
            gb[at(q)] = jnp.where(m, g, 0.0).astype(BF)
            s.grad_pin[at(q)] = jnp.where(m, 0.0, g)

            @pl.when(t == NQ + 1)
            def _():
                sum_p.first()
                sum_q.second()

            scatter_b.first(q)
            store(1, q, s.grad_pin.at[at(q)], s.grad_pin_out.at[at(q)]).start()

        @pl.when(t < NQ - 1)
        def _():
            scatter_h.second(t)


        @pl.when((t >= 2) & (t <= NQ))
        def _():
            add_proj(t - 2)

    sum_w.second()
    for t in range(NQ + 2):
        fourth_phase(t)
    scatter_b.second(NQ - 1)
    column_sums(1, gv)
    send_small()
    for q in range(NQ - 1):
        finish_board(q)
    def drain_early(q):
        gather_b.drain(q)
        gather_h.drain(q)
        scatter_h.drain(q)
        for d in range(4):

            @pl.when((d != z) & (d != dest(0)))
            def _():
                sent(zsend.at[d, q], m_zs.at[d, q])

    loop(NQ, drain_early)

    def drain_half(i):
        for n in range(3):
            sent(agg_ref(c, mine(i)), ga_ss.at[n, i])
        for n in range(2):
            sent(sa_send.at[n, i], sa_ss.at[n, i])
        for h in range(2):
            sent(sa_x.at[i, part_c(h)], sa_ss.at[2 + h, i])
        sent(stat.at[0, i], stat_ss.at[i])

    loop(NP, drain_half)
    for n in range(3):
        sent(agg_ref(c, own_half), ga_ss.at[n, NP])
    for n in range(4):
        lend(n).wait_send()
    for n in range(2):
        lend_list(n).wait_send()
    for h in range(2):
        loop(2 * NP, lambda i, h=h: sent(grad_agg.at[i, part_c(h)], s.gy_ss.at[h, i]))
        loop(NQ, lambda q, h=h: sent(zsend.at[dest(0), q, part_c(h)], m_hs.at[h, q]))
    for n in range(2):
        give(n).wait_send()

    sum_p.second()
    sum_q.across()
    sum_w.third()
    sum_w.drain()
    store(0, 1, s.grad_w, s.grad_w_out).start()
    finish_board(NQ - 1)
    sum_q.third()
    store(0, 2, s.grad_q, s.grad_q_out).start()
    for d in range(1, 8):
        other = (r + d) % 8
        arrived(small.at[other], small_rs.at[other])
    total = small[0]
    for i in range(1, 8):
        total = total + small[i]
    nodes = rows * 8
    per = jnp.concatenate(
        [jnp.full((1, 128), 1.0 / nodes, F32), jnp.full((1, 128), 1.0 / (nodes * SLOTS), F32)], axis=1
    )
    s.sums[...] = total
    s.sums[3:4] = total[3:4] * per
    store(0, 3, s.sums, s.sums_out).start()
    sum_p.third()
    store(3, 0, s.grad_p, s.grad_p_out).start()

    def drain(q):
        scatter_b.drain(q)
        store(1, q, s.grad_pin.at[at(q)], s.grad_pin_out.at[at(q)]).wait()
        store(2, q, s.grad_board.at[at(q)], s.grad_board_out.at[at(q)]).wait()

    loop(NQ, drain)
    sum_q.drain()
    sum_p.drain()
    for d in range(7):
        sent(small.at[r], small_ss.at[d])
    for i, (n, name) in enumerate(
        ((0, "embeddings"), (0, "grad_w"), (0, "grad_q"), (0, "sums"), (3, "grad_p"))
    ):
        store(n, i % 4, getattr(s, name), getattr(s, name + "_out")).wait()


def finish_kernel(*refs):
    ins, sums, outs, small, held, sem = refs[:6], refs[6], refs[7:13], refs[13:18], refs[18:24], refs[24]
    first = [pltpu.make_async_copy(a, b, sem.at[0, i]) for i, (a, b) in enumerate(zip(ins, held))]
    second = [pltpu.make_async_copy(a, b, sem.at[1, i]) for i, (a, b) in enumerate(zip(held, outs))]
    for copy in first:
        copy.start()
    for i in range(3):
        small[i][...] = sums[i : i + 1]
    small[3][...] = sums[3:4, 0:1]
    small[4][...] = sums[3:4, 128:129]
    for a, b in zip(first, second):
        a.wait()
        b.start()
    for copy in second:
        copy.wait()


def fused_device(
    pin, board, is_board, neighbours, present, importance, proj_w, proj_b, q_w, q_b, w_w, w_b, cotangent
):
    rows, width = pin.shape
    bwidth = board.shape[1]
    chunk = rows // NQ
    nodes = rows * 8
    inputs = dict(
        board=board,
        is_board=is_board.reshape(rows // 128, 128),
        proj_w=proj_w,
        proj_b=proj_b.reshape(1, width),
        pin=pin,
        neighbours=neighbours.T,
        present=present.T,
        importance=importance.T,
        q_w=q_w,
        q_b=q_b.reshape(1, width),
        w_w=w_w,
        w_b=w_b.reshape(1, width),
        cotangent=cotangent,
    )
    shape = jax.ShapeDtypeStruct
    outs = dict(
        embeddings=shape((rows, width), BF),
        grad_pin=shape((rows, width), F32),
        grad_board=shape((rows, bwidth), F32),
        grad_p=shape((bwidth * 4 // 8, width), F32),
        grad_q=shape((width * 4 // 8, width), F32),
        grad_w=shape((2 * width * 4 // 8, width), F32),
        sums=shape((8, width), F32),
    )
    vmem, dma = pltpu.VMEM, pltpu.SemaphoreType.DMA
    scratch = dict(
        in_sem=dma((len(inputs),)),
        out_sem=dma((4, NQ)),
        flags=vmem((rows // 128, 128), jnp.int32),
        numbers=vmem((SLOTS, rows), jnp.int32),
        numbers2=vmem((SLOTS, rows), jnp.int32),
        alpha=vmem((64, rows), BF),
        alpha2=vmem((64, rows), BF),
        padded=vmem((64, rows), F32),
        table2=vmem((nodes // 2 // chunk, rows, chunk), BF),
        high2=vmem((2, rows // 4, 128), F32),
        low2=vmem((2, rows // 4, 128), F32),
        weight2=vmem((2, rows // 4, 128), F32),
        grad_agg2=vmem((2 * NP, width, rows // 2 // NP), BF),
        table=vmem((nodes // chunk, rows, chunk), BF),
        stage=vmem((64 * (PIECE + 8), 128), F32),
        high=vmem((2, rows // 4, 128), F32),
        low=vmem((2, rows // 4, 128), F32),
        weight=vmem((2, rows // 4, 128), F32),
        mask=vmem((rows, 128), F32),
        boards=vmem((4, rows, bwidth), BF),
        ha=vmem((8, rows, width), BF),
        message=vmem((8, NQ, chunk, width), BF),
        v_pre=vmem((rows, width), F32),
        u_pre=vmem((2, rows // 2, width), F32),
        w2=vmem(w_w.shape, BF),
        w_b2=vmem((1, width), F32),
        cotangent2=vmem((rows // 2, width), BF),
        gu2=vmem((rows // 2, width), BF),
        emb2=vmem((rows // 2, width), BF),
        sa_send=vmem((2, NP, rows // 2 // NP, width), BF),
        sa_recv=vmem((2, NP, rows // 2 // NP, width), BF),
        sa_x=vmem((NP, width, rows // 2 // NP), BF),
        sa_ss=dma((4, NP)),
        sa_rs=dma((4, NP)),
        ga_ss=dma((3, NP + 1)),
        ga_rs=dma((3, NP + 1)),
        lend_ss=dma((4,)),
        lend_rs=dma((4,)),
        give_ss=dma((2,)),
        give_rs=dma((2,)),
        gu=vmem((rows, width), BF),
        gv=vmem((rows, width), BF),
        gb=vmem((rows, width), BF),
        grad_agg=vmem((2 * NP, width, rows // 2 // NP), BF),
        stat=vmem((2, NP, 8, 128), F32),
        small=vmem((8, 8, width), F32),
        zrecv=vmem((5, NQ, width, chunk), BF),
        total_t=vmem((width, chunk), F32),
        stat_ss=dma((NP,)),
        stat_rs=dma((NP,)),
        msg_rs=dma((8, NQ)),
        up_ss=dma((4, NQ)),
        down_ss=dma((4, NQ)),
        y_ss=dma((4, NQ)),
        zx_ss=dma((NQ,)),
        m_zs=dma((4, NQ)),
        m_zr=dma((5, NQ)),
        list_ss=dma((2,)),
        list_rs=dma((2,)),
        gy_ss=dma((2, 2 * NP)),
        gy_rs=dma((2, 2 * NP)),
        m_hs=dma((2, NQ)),
        m_hr=dma((4, 2, NQ)),
        small_ss=dma((7,)),
        small_rs=dma((8,)),
    )
    for name in ("present", "importance", "proj_w", "proj_b", "pin", "q_w", "q_b", "w_w", "w_b", "cotangent"):
        scratch[name] = vmem(inputs[name].shape, inputs[name].dtype)
    for name, out in outs.items():
        scratch[name] = vmem(out.shape, out.dtype)
    for name in ("gb", "gh"):
        scratch[name + "_ss"] = dma((3, NQ))
        scratch[name + "_rs"] = dma((3, NQ))
    for name, w in (("sh", width), ("sb", bwidth)):
        scratch[name + "_send1"] = vmem((2, NQ, chunk, w), BF)
        scratch[name + "_recv1"] = vmem((2, NQ, chunk, w), BF)
        scratch[name + "_sendx"] = vmem((NQ, chunk, w), BF)
        scratch[name + "_recvx"] = vmem((NQ, chunk, w), BF)
        scratch[name + "_ss"] = dma((3, NQ))
        scratch[name + "_rs"] = dma((3, NQ))
    for name, n in (("ww", width), ("wq", width // 2), ("wp", bwidth // 2)):
        for part in ("_yrecv", "_zrecv"):
            scratch[name + part] = vmem((4, n, width), BF)
        scratch[name + "_ss"] = dma((2, 4))
        scratch[name + "_rs"] = dma((2, 4))
    place = pl.BlockSpec(memory_space=pl.ANY)
    whole = pl.BlockSpec(memory_space=pltpu.VMEM)
    names = [n + "_in" for n in inputs] + [n + "_out" for n in outs] + list(scratch)
    got = pl.pallas_call(
        functools.partial(fused_kernel, names=tuple(names)),
        out_shape=list(outs.values()),
        in_specs=[place] * len(inputs),
        out_specs=[place] * len(outs),
        scratch_shapes=list(scratch.values()),
        compiler_params=pltpu.CompilerParams(
            collective_id=1, has_side_effects=True, vmem_limit_bytes=63 << 20
        ),
        cost_estimate=pl.CostEstimate(flops=14 << 30, bytes_accessed=8 << 20, transcendentals=0),
    )(*inputs.values())
    row, one = shape((1, width), F32), shape((1, 1), F32)
    emb, g_pin, g_board, g_proj, g_q, g_w, p_b, q_bias, w_bias, count, weight = pl.pallas_call(
        finish_kernel,
        out_shape=list(outs.values())[:6] + [row, row, row, one, one],
        in_specs=[place] * 6 + [whole],
        out_specs=[place] * 6 + [whole] * 5,
        scratch_shapes=[vmem(out.shape, out.dtype) for out in list(outs.values())[:6]] + [dma((2, 6))],
        cost_estimate=pl.CostEstimate(flops=0, bytes_accessed=5 << 20, transcendentals=0),
    )(*got)
    return (
        emb,
        g_pin,
        g_board,
        g_proj,
        p_b.reshape(width),
        g_q,
        q_bias.reshape(width),
        g_w,
        w_bias.reshape(width),
        count.reshape(()),
        weight.reshape(()),
    )


def silu_slope(value):
    sig = jax.nn.sigmoid(value)
    return sig * (1.0 + value * (1.0 - sig))


def slot_table(nbr_block, alpha_block, start, width):
    offsets = nbr_block - start
    places = lax.broadcasted_iota(jnp.int32, (1, 1, width), 2)
    return jnp.sum(jnp.where(offsets[:, :, None] == places, alpha_block[:, :, None], 0.0), axis=1)


def split_pair(table):
    upper = table.astype(jnp.bfloat16)
    lower = (table - upper.astype(jnp.float32)).astype(jnp.bfloat16)
    return (upper, lower)


def collect_rows(nbrs, alphas, table_all):
    total, columns = table_all.shape
    col_tile = math.gcd(total, 2048)
    count_tiles = total // col_tile
    tiles = table_all.reshape(count_tiles, col_tile, columns)
    rows = nbrs.shape[0]
    row_block = math.gcd(rows, 512)
    count_rows = rows // row_block

    def one_rows(pair):
        nbr_block, alpha_block = pair

        def step(acc, index):
            upper, lower = split_pair(
                slot_table(nbr_block, alpha_block, index * col_tile, col_tile)
            )
            piece = tiles[index]
            acc = acc + jnp.dot(upper, piece, preferred_element_type=jnp.float32)
            return (acc + jnp.dot(lower, piece, preferred_element_type=jnp.float32), None)

        acc, unused = lax.scan(
            step, jnp.zeros((row_block, columns), jnp.float32), jnp.arange(count_tiles)
        )
        return acc

    out = lax.map(
        one_rows,
        (nbrs.reshape(count_rows, row_block, -1), alphas.reshape(count_rows, row_block, -1)),
    )
    return out.reshape(rows, columns)


def spread_rows(grads, nbrs, alphas, base, width):
    rows, columns = grads.shape
    row_block = math.gcd(rows, 512)
    count_rows = rows // row_block
    col_tile = math.gcd(width, 2048)
    count_tiles = width // col_tile
    stacked = (
        grads.reshape(count_rows, row_block, columns),
        nbrs.reshape(count_rows, row_block, -1),
        alphas.reshape(count_rows, row_block, -1),
    )
    tdot = (((0,), (0,)), ((), ()))

    def one_tile(index):

        def step(acc, triple):
            grad_block, nbr_block, alpha_block = triple
            upper, lower = split_pair(
                slot_table(nbr_block, alpha_block, base + index * col_tile, col_tile)
            )
            acc = acc + lax.dot_general(upper, grad_block, tdot, preferred_element_type=jnp.float32)
            return (
                acc + lax.dot_general(lower, grad_block, tdot, preferred_element_type=jnp.float32),
                None,
            )

        acc, unused = lax.scan(step, jnp.zeros((col_tile, columns), jnp.float32), stacked)
        return acc

    out = lax.map(one_tile, jnp.arange(count_tiles))
    return out.reshape(width, columns)


def per_device(
    pin_features,
    board_features,
    is_board,
    neighbours,
    present,
    importance,
    proj_weight,
    proj_bias,
    q_weight,
    q_bias,
    w_weight,
    w_bias,
    cotangent,
):
    local_rows = pin_features.shape[0]
    width = q_weight.shape[0]
    filled = present.astype(jnp.float32) * importance
    alpha = filled / jnp.sum(filled, axis=1, keepdims=True)
    board_mask = (is_board == 1)[:, None]
    stat_terms = (jnp.sum(present.astype(jnp.float32)), jnp.sum(filled))
    stat_totals = lax.psum((stat_terms[0], stat_terms[1]), "rows")
    board_full = lax.all_gather(board_features, "cols", axis=1, tiled=True)
    board_proj = jnp.dot(board_full, proj_weight, preferred_element_type=jnp.float32) + proj_bias
    h_local = jnp.where(board_mask, board_proj, pin_features.astype(jnp.float32)).astype(
        jnp.bfloat16
    )
    h_full = lax.all_gather(h_local, "cols", axis=1, tiled=True)
    v_pre = jnp.dot(h_full, q_weight, preferred_element_type=jnp.float32) + q_bias
    message = jax.nn.silu(v_pre).astype(jnp.bfloat16)
    message_all = lax.all_gather(message, "rows", axis=0, tiled=True)
    agg_local = collect_rows(neighbours, alpha, message_all).astype(jnp.bfloat16)
    agg_full = lax.all_gather(agg_local, "cols", axis=1, tiled=True)
    w_self = w_weight[:width]
    w_agg = w_weight[width:]
    u_pre = (
        jnp.dot(h_full, w_self, preferred_element_type=jnp.float32)
        + jnp.dot(agg_full, w_agg, preferred_element_type=jnp.float32)
        + w_bias
    )
    z_act = jax.nn.silu(u_pre)
    squares = lax.psum(jnp.sum(z_act * z_act, axis=1), "cols")
    scale = lax.rsqrt(squares + 1e-06)[:, None]
    embeddings = (z_act * scale).astype(jnp.bfloat16)
    grad_out = cotangent.astype(jnp.float32)
    inner = lax.psum(jnp.sum(grad_out * z_act, axis=1), "cols")[:, None]
    grad_z = grad_out * scale - z_act * scale * scale * scale * inner
    grad_u = (grad_z * silu_slope(u_pre)).astype(jnp.bfloat16)
    agg_part = lax.dot_general(
        grad_u, w_agg, (((1,), (1,)), ((), ())), preferred_element_type=jnp.float32
    )
    grad_agg = lax.psum_scatter(agg_part, "cols", scatter_dimension=1, tiled=True).astype(
        jnp.bfloat16
    )
    table = spread_rows(grad_agg, neighbours, alpha, 0, message_all.shape[0])
    grad_message = lax.psum_scatter(
        table.astype(jnp.bfloat16), "rows", scatter_dimension=0, tiled=True
    ).astype(jnp.float32)
    grad_v = (grad_message * silu_slope(v_pre)).astype(jnp.bfloat16)
    h_part = lax.dot_general(
        grad_u, w_self, (((1,), (1,)), ((), ())), preferred_element_type=jnp.float32
    )
    h_part = h_part + lax.dot_general(
        grad_v, q_weight, (((1,), (1,)), ((), ())), preferred_element_type=jnp.float32
    )
    grad_h = lax.psum_scatter(
        h_part.astype(jnp.bfloat16), "cols", scatter_dimension=1, tiled=True
    ).astype(jnp.float32)
    grad_pin = jnp.where(board_mask, 0.0, grad_h)
    grad_hb = jnp.where(board_mask, grad_h, 0.0).astype(jnp.bfloat16)
    board_part = lax.dot_general(
        grad_hb, proj_weight, (((1,), (1,)), ((), ())), preferred_element_type=jnp.float32
    )
    grad_board = lax.psum_scatter(
        board_part.astype(jnp.bfloat16), "cols", scatter_dimension=1, tiled=True
    ).astype(jnp.float32)
    tdot = (((0,), (0,)), ((), ()))
    grad_w_local = jnp.concatenate(
        [
            lax.dot_general(h_full, grad_u, tdot, preferred_element_type=jnp.float32),
            lax.dot_general(agg_full, grad_u, tdot, preferred_element_type=jnp.float32),
        ],
        axis=0,
    )
    grad_q_local = lax.dot_general(h_full, grad_v, tdot, preferred_element_type=jnp.float32)
    grad_p_local = lax.dot_general(board_full, grad_hb, tdot, preferred_element_type=jnp.float32)
    grad_w, grad_q, grad_proj = (
        lax.psum_scatter(
            grad_w_local.astype(jnp.bfloat16), "rows", scatter_dimension=0, tiled=True
        ).astype(jnp.float32),
        lax.psum_scatter(
            grad_q_local.astype(jnp.bfloat16), "rows", scatter_dimension=0, tiled=True
        ).astype(jnp.float32),
        lax.psum_scatter(
            grad_p_local.astype(jnp.bfloat16), "rows", scatter_dimension=0, tiled=True
        ).astype(jnp.float32),
    )
    bias_terms = (
        jnp.sum(grad_hb.astype(jnp.float32), axis=0),
        jnp.sum(grad_v.astype(jnp.float32), axis=0),
        jnp.sum(grad_u.astype(jnp.float32), axis=0),
    )
    grad_pb, grad_qb, grad_wb = lax.psum((bias_terms[0], bias_terms[1], bias_terms[2]), "rows")
    all_nodes = local_rows * lax.axis_size("rows")
    mean_count = stat_totals[0] / all_nodes
    mean_weight = stat_totals[1] / (all_nodes * SLOTS)
    return (
        embeddings,
        grad_pin,
        grad_board,
        grad_proj,
        grad_pb,
        grad_q,
        grad_qb,
        grad_w,
        grad_wb,
        mean_count,
        mean_weight,
    )


def solution(mesh):
    in_specs = (
        P("rows", "cols"),
        P("rows", "cols"),
        P("rows"),
        P("rows", None),
        P("rows", None),
        P("rows", None),
        P(None, "cols"),
        P("cols"),
        P(None, "cols"),
        P("cols"),
        P(None, "cols"),
        P("cols"),
        P("rows", "cols"),
    )
    out_specs = (
        P("rows", "cols"),
        P("rows", "cols"),
        P("rows", "cols"),
        P("rows", "cols"),
        P("cols"),
        P("rows", "cols"),
        P("cols"),
        P("rows", "cols"),
        P("cols"),
        P(),
        P(),
    )
    fused = mesh.shape["rows"] == 8 and mesh.shape["cols"] == 4
    return jax.shard_map(
        fused_device if fused else per_device, mesh=mesh, in_specs=in_specs, out_specs=out_specs, check_vma=False
    )
```

```python
import functools
import math
import types

import jax
import jax.numpy as jnp
from jax import lax
from jax.experimental import pallas as pl
from jax.experimental.pallas import tpu as pltpu
from jax.sharding import PartitionSpec as P

SLOTS = 50
MESH = pl.DeviceIdType.MESH
BF = jnp.bfloat16
F32 = jnp.float32
NQ = 4
NP = 2
LO_BITS = 7
LO = 1 << LO_BITS
PIECE = 64
NT = (((1,), (1,)), ((), ()))
TN = (((0,), (0,)), ((), ()))


def dot(a, b):
    return jnp.dot(a, b, preferred_element_type=F32)


def dot_nt(a, b):
    return lax.dot_general(a, b, NT, preferred_element_type=F32)


def dot_tn(a, b):
    return lax.dot_general(a, b, TN, preferred_element_type=F32)


def loop(n, body, unroll=1):
    def step(i, carry):
        body(i)
        return carry

    lax.fori_loop(0, n, step, 0, unroll=unroll)


def row_sums(x):
    y = x[:, :128] + x[:, 128:]
    sums = [
        jnp.sum(y[i * 128 : (i + 1) * 128].T, axis=0, keepdims=True) for i in range(x.shape[0] // 128)
    ]
    return sums[0] if len(sums) == 1 else jnp.concatenate(sums, axis=0)


def down(row):
    return jnp.broadcast_to(row, (128, 128)).T


def down_rows(rows):
    cols = [down(rows[i : i + 1]) for i in range(rows.shape[0])]
    col = cols[0] if len(cols) == 1 else jnp.concatenate(cols, axis=0)
    return jnp.concatenate([col, col], axis=1)


def fused_kernel(*refs, names):
    s = types.SimpleNamespace(**dict(zip(names, refs)))
    r = lax.axis_index("rows")
    c = lax.axis_index("cols")
    z, y = r // 2, r % 2
    x, k = c // 2, c % 2
    rows, width = s.pin.shape
    bwidth = s.boards.shape[2]
    chunk = rows // NQ
    zn = 4
    per_block = rows // LO
    core = (r, x * 2 + 1 - k)
    xp = (r, (1 - x) * 2 + k)
    diagonal = (z * 2 + 1 - y, (1 - x) * 2 + k)
    yp = (z * 2 + 1 - y, c)
    upper = z // 2
    inner = (z % 2) + upper * (1 - 2 * (z % 2))
    zx = z + 1 - 2 * (z % 2)
    zxp = (zx * 2 + y, c)

    def at(q):
        return pl.ds(pl.multiple_of(q * chunk, chunk), chunk)

    def rdma(src, dst, send, recv, dev):
        return pltpu.make_async_remote_copy(
            src_ref=src, dst_ref=dst, send_sem=send, recv_sem=recv, device_id=dev, device_id_type=MESH
        )

    def arrived(ref, sem):
        rdma(ref, ref, sem, sem, core).wait_recv()

    def sent(ref, sem):
        rdma(ref, ref, sem, sem, core).wait_send()

    class Gather:
        def __init__(self, buf, base, ss, rs):
            self.buf, self.base, self.ss, self.rs = buf, base, ss, rs

        def ref(self, col, q):
            return self.buf.at[self.base + col, at(q)]

        def start(self, q):
            own = self.ref(c, q)
            rdma(own, own, self.ss.at[1, q], self.rs.at[1, q], xp).start()
            rdma(own, own, self.ss.at[0, q], self.rs.at[0, q], core).start()

        def forward(self, q):
            got = self.ref((1 - x) * 2 + k, q)
            arrived(got, self.rs.at[1, q])
            rdma(got, got, self.ss.at[2, q], self.rs.at[2, q], core).start()

        def finish(self, q):
            arrived(self.ref(x * 2 + 1 - k, q), self.rs.at[0, q])
            arrived(self.ref((1 - x) * 2 + 1 - k, q), self.rs.at[2, q])

        def drain(self, q):
            for i in range(3):
                sent(self.ref(c, q), self.ss.at[i, q])

    class Scatter:
        def __init__(self, part, name):
            self.part = part
            self.send1, self.recv1 = getattr(s, name + "_send1"), getattr(s, name + "_recv1")
            self.sendx, self.recvx = getattr(s, name + "_sendx"), getattr(s, name + "_recvx")
            self.ss, self.rs = getattr(s, name + "_ss"), getattr(s, name + "_rs")

        def first(self, q):
            for i, xs in ((0, 1 - x), (1, x)):
                self.send1[i, q] = self.part(xs * 2 + 1 - k, q).astype(BF)
                rdma(
                    self.send1.at[i, q], self.recv1.at[i, q], self.ss.at[i, q], self.rs.at[i, q], core
                ).start()

        def second(self, q):
            own = self.part((1 - x) * 2 + k, q)
            arrived(self.recv1.at[0, q], self.rs.at[0, q])
            self.sendx[q] = (own + self.recv1[0, q].astype(F32)).astype(BF)
            rdma(self.sendx.at[q], self.recvx.at[q], self.ss.at[2, q], self.rs.at[2, q], xp).start()

        def third(self, q):
            own = self.part(c, q)
            arrived(self.recv1.at[1, q], self.rs.at[1, q])
            own = own + self.recv1[1, q].astype(F32)
            arrived(self.recvx.at[q], self.rs.at[2, q])
            return own + self.recvx[q].astype(F32)

        def drain(self, q):
            for i in range(2):
                sent(self.send1.at[i, q], self.ss.at[i, q])
            sent(self.sendx.at[q], self.ss.at[2, q])

    class WeightSum:
        def __init__(self, part, name, out, ysend, zsend):
            self.part, self.out = part, out
            self.ysend, self.zsend = ysend, zsend
            self.yrecv, self.zrecv = getattr(s, name + "_yrecv"), getattr(s, name + "_zrecv")
            self.ss, self.rs = getattr(s, name + "_ss"), getattr(s, name + "_rs")

        def first(self, at0=0, n=4):
            def step(i):
                d = at0 + i
                ref = self.ysend(d)
                ref[...] = self.part(d, 1 - y, True).astype(BF)
                rdma(ref, self.yrecv.at[d], self.ss.at[0, d], self.rs.at[0, d], yp).start()

            loop(n, step, unroll=n)

        def second(self, at0=0, n=4):
            def step(i):
                d = at0 + i
                own = self.part(d, y)
                arrived(self.yrecv.at[d], self.rs.at[0, d])
                own = own + self.yrecv[d].astype(F32)

                @pl.when(d == z)
                def _():
                    self.out[...] = own

                @pl.when(d != z)
                def _():
                    ref = self.zsend(d)
                    ref[...] = own.astype(BF)
                    rdma(
                        ref, self.zrecv.at[z], self.ss.at[1, d], self.rs.at[1, z], (d * 2 + y, c)
                    ).start()

            loop(n, step)

        def third(self):
            def step(d):
                @pl.when(d != z)
                def _():
                    arrived(self.zrecv.at[d], self.rs.at[1, d])
                    self.out[...] += self.zrecv[d].astype(F32)

            loop(zn, step)

        def drain(self):
            def step(d):
                sent(self.ysend(d), self.ss.at[0, d])

                @pl.when(d != z)
                def _():
                    sent(self.zsend(d), self.ss.at[1, d])

            loop(zn, step)

    class PairSum(WeightSum):
        def first(self):
            for d in ((zx + 2) % 4, zx, (z + 2) % 4, z):
                ref = self.ysend(d)
                ref[...] = self.part(d, 1 - y, True).astype(BF)
                rdma(ref, self.yrecv.at[d], self.ss.at[0, d], self.rs.at[0, d], yp).start()

        def total(self, d):
            own = self.part(d, y)
            arrived(self.yrecv.at[d], self.rs.at[0, d])
            return own + self.yrecv[d].astype(F32)

        def second(self):
            for n, d in enumerate(((zx + 2) % 4, zx)):
                ref = self.zsend(n)
                ref[...] = self.total(d).astype(BF)
                rdma(ref, self.zrecv.at[n], self.ss.at[1, n], self.rs.at[1, n], zxp).start()

        def across(self):
            d = (z + 2) % 4
            ref = self.zsend(2)
            own = self.total(d)
            arrived(self.zrecv.at[0], self.rs.at[1, 0])
            ref[...] = (own + self.zrecv[0].astype(F32)).astype(BF)
            rdma(ref, self.zrecv.at[2], self.ss.at[1, 2], self.rs.at[1, 2], (d * 2 + y, c)).start()

        def third(self):
            own = self.total(z)
            for n in (1, 2):
                arrived(self.zrecv.at[n], self.rs.at[1, n])
                own = own + self.zrecv[n].astype(F32)
            self.out[...] = own

        def drain(self):
            for d in range(zn):
                sent(self.ysend(d), self.ss.at[0, d])
            for n in range(3):
                sent(self.zsend(n), self.ss.at[1, n])

    barrier = pltpu.get_barrier_semaphore()

    def greet(dev):
        pl.semaphore_signal(barrier, inc=1, device_id=dev, device_id_type=MESH)

    near_by = (xp, yp, diagonal, core)
    for dev in near_by:
        greet(dev)

    @pl.when(z < 3)
    def _():
        greet(((z + 1) * 2 + y, c))

    @pl.when(z > 0)
    def _():
        greet(((z - 1) * 2 + y, c))

    boards, own_h = s.boards, s.ha
    in_sem = s.in_sem
    loads = {}
    order = (
        ("board", boards.at[c]),
        ("is_board", s.flags),
        ("proj_w", s.proj_w),
        ("proj_b", s.proj_b),
        ("pin", s.pin),
        ("neighbours", s.numbers),
        ("present", s.present),
        ("importance", s.importance),
        ("q_w", s.q_w),
        ("q_b", s.q_b),
        ("w_w", s.w_w),
        ("w_b", s.w_b),
        ("cotangent", s.cotangent),
    )
    for i, (name, ref) in enumerate(order):
        loads[name] = pltpu.make_async_copy(getattr(s, name + "_in"), ref, in_sem.at[i])
        loads[name].start()

    out_sem = s.out_sem

    def store(i, q, src, dst):
        return pltpu.make_async_copy(src, dst, out_sem.at[i, q])

    gather_b = Gather(boards, 0, s.gb_ss, s.gb_rs)
    gather_h = Gather(own_h, 0, s.gh_ss, s.gh_rs)
    loads["board"].wait()
    pl.semaphore_wait(barrier, len(near_by) + 1 + inner)
    loop(NQ, gather_b.start)

    mask = s.mask
    loads["is_board"].wait()
    flags = s.flags[...].astype(F32)
    for i in range(rows // 128):
        mask[i * 128 : (i + 1) * 128] = down(flags[i : i + 1])

    half = rows // 2
    padded = s.padded
    list_ss, list_rs = s.list_ss, s.list_rs

    quarter = rows // 4

    def lay(ref):
        for t in range(2):
            for i in range(quarter // 128):
                a, b = 2 * t * quarter + i * 128, (2 * t + 1) * quarter + i * 128
                ref[t, i * 128 : (i + 1) * 128] = jnp.concatenate(
                    [padded[:, a : a + 128], padded[:, b : b + 128]], axis=0
                ).T

    def lend_list(i):
        src, dst = ((s.numbers, s.numbers2), (s.alpha, s.alpha2))[i]
        return rdma(src, dst, list_ss.at[i], list_rs.at[i], yp)

    def prepare():
        for name in ("neighbours", "present", "importance"):
            loads[name].wait()
        lend_list(0).start()
        present = s.present[...].astype(F32)
        filled = present * s.importance[...]
        padded[SLOTS:] = jnp.zeros((padded.shape[0] - SLOTS, rows), F32)
        padded[:SLOTS] = filled / jnp.sum(filled, axis=0, keepdims=True)
        s.alpha[...] = padded[...].astype(BF)
        lend_list(1).start()
        lay(s.weight)
        small = s.small
        small[r] = jnp.zeros(small.shape[1:], F32)
        small[r, 3:4] = jnp.concatenate(
            [
                jnp.broadcast_to(jnp.sum(present).reshape(1, 1), (1, 128)),
                jnp.broadcast_to(jnp.sum(filled).reshape(1, 1), (1, 128)),
            ],
            axis=1,
        )
        numbers = s.numbers[...]
        padded[:SLOTS] = (numbers >> LO_BITS).astype(F32)
        lay(s.high)
        padded[:SLOTS] = (numbers & (LO - 1)).astype(F32)
        lay(s.low)

    def prepare2():
        for i in range(2):
            lend_list(i).wait_recv()
        numbers = s.numbers2[...]
        high = numbers >> LO_BITS
        place = (high // (2 * per_block)) * per_block + high % per_block
        padded[:SLOTS] = jnp.where((high // per_block) % 2 == y, place, -1).astype(F32)
        lay(s.high2)
        padded[:SLOTS] = (numbers & (LO - 1)).astype(F32)
        lay(s.low2)
        padded[...] = s.alpha2[...].astype(F32)
        lay(s.weight2)

    def mask_of(q):
        m = mask[at(q)] > 0.5
        return jnp.concatenate([m, m], axis=1)

    table, stage = s.table, s.stage
    pitch = stage.shape[0] // 64
    piece_rows = PIECE // 4

    def build(i, lists, table):
        n_high = 2 * table.shape[0]
        iota = lax.broadcasted_iota(jnp.int32, (128, 128), 0).astype(F32).astype(BF)
        front = lax.broadcasted_iota(jnp.int32, (16, 128), 1) < 64
        zero, one = jnp.zeros((), BF), jnp.ones((), BF)

        def tiles(v, n):
            return jnp.concatenate([v] * n, axis=0)

        zeros = jnp.zeros((n_high, 128), BF)
        n = n_high // 16

        def four(j):
            p = i * piece_rows + j
            weights, places = [], []
            for t in range(2):

                def row(ref):
                    return jnp.broadcast_to(ref[t, pl.ds(p, 1), :], (16, 128))

                hi, lo, al = row(lists[0]).astype(BF), row(lists[1]).astype(BF), row(lists[2])
                places.append(jnp.where(tiles(lo, 8) == iota, one, zero))
                same = tiles(hi, n) == iota[:n_high]
                for a in (jnp.where(front, al, 0.0), jnp.where(front, 0.0, al)):
                    w = jnp.where(same, tiles(a.astype(BF), n), zero)
                    weights.append(jnp.concatenate([w, zeros] if t == 0 else [zeros, w], axis=1))
            out = dot_nt(jnp.concatenate(weights, axis=0), jnp.concatenate(places, axis=1))
            for g in range(4):
                stage[pl.ds(j + g * piece_rows, n_high, stride=pitch), :] = out[
                    g * n_high : (g + 1) * n_high
                ]

        loop(piece_rows, four, unroll=16)

        def convert(h):
            for f in range(2):
                base = (2 * h + f) * pitch
                for g in range(4):
                    table[
                        h,
                        pl.ds(pl.multiple_of(i * piece_rows + g * quarter, 16), piece_rows),
                        f * 128 : (f + 1) * 128,
                    ] = stage[
                        pl.ds(pl.multiple_of(base + g * piece_rows, 8), piece_rows), :
                    ].astype(BF)

        loop(table.shape[0], convert, unroll=4)

    lists1 = (s.high, s.low, s.weight)
    lists2 = (s.high2, s.low2, s.weight2)
    table2 = s.table2

    def piece(i):
        build(i, lists1, table)

    def piece2(i):
        build(i, lists2, table2)

    n_pieces = rows // PIECE

    message, v_pre = s.message, s.v_pre

    def make_h(q):
        lines = at(q)
        b01 = jnp.concatenate([boards[0, lines], boards[1, lines]], axis=1)
        b23 = jnp.concatenate([boards[2, lines], boards[3, lines]], axis=1)
        proj = dot(b01, s.proj_w[: 2 * bwidth]) + dot(b23, s.proj_w[2 * bwidth :]) + s.proj_b[...]
        own_h[c, lines] = jnp.where(mask_of(q), proj, s.pin[lines].astype(F32)).astype(BF)

    def block(zb, yb, q):
        return message.at[zb * 2 + yb, q]

    def send_up(zb, q):
        ref = block(zb, y, q)
        rdma(ref, ref, s.up_ss.at[zb, q], s.msg_rs.at[zb * 2 + y, q], ((z + 1) * 2 + y, c)).start()

    def send_down(zb, q):
        ref = block(zb, y, q)
        rdma(ref, ref, s.down_ss.at[zb, q], s.msg_rs.at[zb * 2 + y, q], ((z - 1) * 2 + y, c)).start()

    def send_y(zb, q):
        ref = block(zb, y, q)
        rdma(ref, ref, s.y_ss.at[zb, q], s.msg_rs.at[zb * 2 + y, q], yp).start()

    def make_message(q):
        lines = at(q)
        acc = dot(own_h[0, lines], s.q_w[:width])
        for i in range(1, 4):
            acc = acc + dot(own_h[i, lines], s.q_w[i * width : (i + 1) * width])
        v = acc + s.q_b[...]
        v_pre[lines] = v
        message[r, q] = (v * jax.nn.sigmoid(v)).astype(BF)

        @pl.when(z < 3)
        def _():
            send_up(z, q)

        @pl.when(z > 0)
        def _():
            send_down(z, q)

        send_y(z, q)

    prepare()
    for name in ("proj_w", "proj_b", "pin"):
        loads[name].wait()

    def board_phase(q):
        gather_b.forward(q)
        gather_b.finish(q)
        make_h(q)
        gather_h.start(q)

    piece(0)
    loop(NQ, board_phase)
    early = 3
    loop(early - 1, lambda i: piece(1 + i))

    half = rows // 2
    sub = half // NP
    own_half = pl.ds(pl.multiple_of(x * half, half), half)
    their_half = pl.ds(pl.multiple_of((1 - x) * half, half), half)
    lend_ss, lend_rs = s.lend_ss, s.lend_rs
    wide = 4 * width

    def lends():
        return (
            (s.w_w.at[:wide], s.w2.at[:wide]),
            (s.w_b, s.w_b2),
            (s.w_w.at[wide:], s.w2.at[wide:]),
            (s.cotangent.at[their_half], s.cotangent2),
        )

    def lend(i):
        src, dst = lends()[i]
        return rdma(src, dst, lend_ss.at[i], lend_rs.at[i], xp)

    for name in ("w_w", "w_b", "cotangent"):
        loads[name].wait()
    for i in range(4):
        lend(i).start()
    loads["q_w"].wait()
    loads["q_b"].wait()

    def message_phase(q):
        gather_h.forward(q)
        gather_h.finish(q)
        make_message(q)
        piece(early + q)

        @pl.when(q % 2 == 0)
        def _():
            piece(early + NQ + q // 2)

    loop(NQ, message_phase)
    built = early + NQ + NQ // 2

    u_pre = s.u_pre

    def part_of(i):
        return pl.ds(pl.multiple_of(i * sub, sub), sub)

    def mine(i):
        return pl.ds(pl.multiple_of(x * half + i * sub, sub), sub)

    def theirs(i):
        return pl.ds(pl.multiple_of((1 - x) * half + i * sub, sub), sub)

    def u_from_h(i):
        for n, w, b in ((0, s.w_w, s.w_b), (1, s.w2, s.w_b2)):
            acc = dot(own_h[0, mine(i)], w[:width])
            for m in range(1, 4):
                acc = acc + dot(own_h[m, mine(i)], w[m * width : (m + 1) * width])
            u_pre[n, part_of(i)] = acc + b[...]

    agg = s.grad_pin
    parts = rows // chunk

    def add(b, first, n):
        for i in range(parts):
            lines = slice(i * chunk, (i + 1) * chunk)
            acc = agg[lines]
            for q in range(first, first + n):
                acc = acc + dot(table[b * NQ + q, lines], message[b, q])
            agg[lines] = acc

    def over_y(zb, q):
        @pl.when((zb != zx) | ((inner == 0) & (q < NQ // 2)))
        def _():
            send_y(zb, q)

    def send_zx(q):
        ref = block(z, 1 - y, q)
        rdma(ref, ref, s.zx_ss.at[q], s.msg_rs.at[z * 2 + 1 - y, q], zxp).start()

    def at_z(zb):
        return (zb >= 0) & (zb <= 3)

    n_second = 3 * NQ
    n_second2 = n_pieces // 2
    steps = n_pieces - built

    def second_phase(i):
        t, q = 1 + i // NQ, i % NQ

        @pl.when(z - t >= 0)
        def _():
            arrived(block(z - t, y, q), s.msg_rs.at[(z - t) * 2 + y, q])

            @pl.when(z < 3)
            def _():
                send_up(z - t, q)

            over_y(z - t, q)

        @pl.when(z + t <= 3)
        def _():
            arrived(block(z + t, y, q), s.msg_rs.at[(z + t) * 2 + y, q])

            @pl.when(z > 0)
            def _():
                send_down(z + t, q)

            over_y(z + t, q)

        @pl.when(t == 1)
        def _():
            arrived(block(z, 1 - y, q), s.msg_rs.at[z * 2 + 1 - y, q])

            @pl.when(inner == 0)
            def _():
                send_zx(q)

        @pl.when((t == 3) & (inner == 1) & (q >= NQ // 2))
        def _():
            send_zx(q)

        @pl.when(i < steps)
        def _():
            piece(built + i)

        @pl.when(i == 0)
        def _():
            prepare2()

        @pl.when((i > 0) & (i < 1 + n_second2))
        def _():
            loop(2, lambda n: piece2(2 * (i - 1) + n))

        @pl.when(i == steps)
        def _():
            agg[...] = jnp.zeros_like(agg)
            lend(0).wait_recv()
            lend(1).wait_recv()

        @pl.when(i >= n_second - NP)
        def _():
            u_from_h(i - (n_second - NP))

        @pl.when((i >= n_second - 5) & (i < n_second))
        def _():
            n = i - (n_second - 5)
            zb = z + jnp.where(n == 0, 0, jnp.where(n == 1, -1, jnp.where(n == 2, 1, jnp.where(n == 3, -2, 2))))

            @pl.when(at_z(zb))
            def _():
                add(zb * 2 + y, 0, NQ)

    loop(n_second, second_phase)

    add(z * 2 + 1 - y, 0, NQ)

    @pl.when(inner == 0)
    def _():
        add((3 - z) * 2 + y, 0, NQ)

    def add_arriving(zb, first, n):
        b = zb * 2 + 1 - y
        loop(n, lambda q: arrived(message.at[b, first + q], s.msg_rs.at[b, first + q]))
        add(b, first, n)

    add_arriving(zx, 0, NQ // 2)
    add_arriving(2 - upper, 0, NQ)
    for q in range(NQ):
        blocks = [3 * (1 - upper) * 2 + 1 - y] + ([zx * 2 + 1 - y] if q >= NQ // 2 else [])
        for b in blocks:
            arrived(message.at[b, q], s.msg_rs.at[b, q])
        for i in range(parts):
            lines = slice(i * chunk, (i + 1) * chunk)
            acc = agg[lines]
            for b in blocks:
                acc = acc + dot(table[b * NQ + q, lines], message[b, q])
            if q < NQ - 1:
                agg[lines] = acc
            else:
                own_h[4 + c, lines] = acc.astype(BF)

    gu, gv, gb, gu2 = s.gu, s.gv, s.gb, s.gu2
    stat, stat_ss, stat_rs = s.stat, s.stat_ss, s.stat_rs
    ga_ss, ga_rs = s.ga_ss, s.ga_rs
    other_x = (1 - x) * 2 + k

    def agg_ref(col, lines):
        return own_h.at[4 + col, lines]

    def agg_start(i):
        a, b = agg_ref(c, theirs(i)), agg_ref(c, mine(i))
        rdma(a, a, ga_ss.at[1, i], ga_rs.at[1, i], xp).start()
        rdma(b, b, ga_ss.at[0, i], ga_rs.at[0, i], core).start()

    def agg_forward(i):
        got = agg_ref(other_x, mine(i))
        arrived(got, ga_rs.at[1, i])
        rdma(got, got, ga_ss.at[2, i], ga_rs.at[2, i], core).start()

    def agg_finish(i):
        arrived(agg_ref(x * 2 + 1 - k, mine(i)), ga_rs.at[0, i])
        arrived(agg_ref((1 - x) * 2 + 1 - k, mine(i)), ga_rs.at[2, i])

    def rest_start():
        a, b = agg_ref(c, own_half), agg_ref(c, their_half)
        rdma(a, a, ga_ss.at[1, NP], ga_rs.at[1, NP], xp).start()
        rdma(b, b, ga_ss.at[0, NP], ga_rs.at[0, NP], core).start()

    def rest_forward():
        got = agg_ref(other_x, their_half)
        arrived(got, ga_rs.at[1, NP])
        rdma(got, got, ga_ss.at[2, NP], ga_rs.at[2, NP], core).start()

    def rest_finish():
        arrived(agg_ref(x * 2 + 1 - k, their_half), ga_rs.at[0, NP])
        arrived(agg_ref((1 - x) * 2 + 1 - k, their_half), ga_rs.at[2, NP])

    loop(NP, agg_start)
    lend(2).wait_recv()
    lend(3).wait_recv()

    def gradients(i):
        return s.cotangent[mine(i)].astype(F32), s.cotangent2[part_of(i)].astype(F32)

    def make_u(i):
        us = [u_pre[n, part_of(i)] for n in range(2)]
        for m in range(4):
            a = own_h[4 + m, mine(i)]
            us = [u + dot(a, w[(4 + m) * width : (5 + m) * width]) for u, w in zip(us, (s.w_w, s.w2))]
        squares, inners = 0.0, 0.0
        for n, (u, g) in enumerate(zip(us, gradients(i))):
            u_pre[n, part_of(i)] = u
            zz = u * jax.nn.sigmoid(u)
            squares = squares + zz * zz
            inners = inners + g * zz
        pad = jnp.zeros((8 - 2 * sub // 128, 128), F32)
        stat[0, i] = jnp.concatenate([row_sums(squares), row_sums(inners), pad], axis=0)
        rdma(stat.at[0, i], stat.at[1, i], stat_ss.at[i], stat_rs.at[i], core).start()

    def make_gu(i):
        arrived(stat.at[1, i], stat_rs.at[i])
        total = stat[0, i] + stat[1, i]
        n_rows = sub // 128
        rr = lax.rsqrt(total[:n_rows] + 1e-6)
        scale = down_rows(rr)
        pull = down_rows(rr * rr * rr * total[n_rows : 2 * n_rows])
        for n, (g, emb, grad) in enumerate(
            zip(gradients(i), (s.embeddings, s.emb2), (gu, gu2))
        ):
            u = u_pre[n, part_of(i)]
            sig = jax.nn.sigmoid(u)
            zz = u * sig
            lines = mine(i) if n == 0 else part_of(i)
            emb[lines] = (zz * scale).astype(BF)
            grad[lines] = ((g * scale - zz * pull) * (sig * (1.0 + u * (1.0 - sig)))).astype(BF)

    def agg_part(col, i):
        lines = pl.ds(pl.multiple_of((4 + col) * width, width), width)
        return dot_nt(gu[mine(i)], s.w_w[lines, :]) + dot_nt(gu2[part_of(i)], s.w2[lines, :])

    grad_agg, grad_agg2 = s.grad_agg, s.grad_agg2
    sa_send, sa_recv, sa_x, sa_ss, sa_rs = s.sa_send, s.sa_recv, s.sa_x, s.sa_ss, s.sa_rs

    def agg_first(i):
        for n, xs in ((0, 1 - x), (1, x)):
            sa_send[n, i] = agg_part(xs * 2 + 1 - k, i).astype(BF)
            rdma(sa_send.at[n, i], sa_recv.at[n, i], sa_ss.at[n, i], sa_rs.at[n, i], core).start()

    def part_c(h):
        return pl.ds(h * (width // 2), width // 2)

    def agg_second(i):
        own = agg_part(other_x, i)
        arrived(sa_recv.at[0, i], sa_rs.at[0, i])
        sa_x[i] = (own + sa_recv[0, i].astype(F32)).T.astype(BF)
        here, there = x * NP + i, (1 - x) * NP + i
        for h in range(2):
            src = sa_x.at[i, part_c(h)]
            if i == NP - 1:
                to = grad_agg2.at[here, part_c(h)]
                rdma(src, to, s.gy_ss.at[h, there], s.gy_rs.at[h, here], diagonal).start()
            rdma(src, grad_agg.at[here, part_c(h)], sa_ss.at[2 + h, i], sa_rs.at[2 + h, i], xp).start()

    def agg_third(i):
        own = agg_part(c, i)
        arrived(sa_recv.at[1, i], sa_rs.at[1, i])
        grad_agg[x * NP + i] = (own + sa_recv[1, i].astype(F32)).T.astype(BF)
        agg_over_y(x * NP + i)

    def agg_over_y(i, halves=(0, 1)):
        for h in halves:
            rdma(
                grad_agg.at[i, part_c(h)],
                grad_agg2.at[i, part_c(h)],
                s.gy_ss.at[h, i],
                s.gy_rs.at[h, i],
                yp,
            ).start()

    def room(at_block, n):
        return [lambda d, b=b, n=n: message.at[b, d, pl.ds(0, n)] for b in (at_block, at_block + 1)]

    def room_narrow(at_block, n):
        return [lambda d, i=i: message.at[at_block, d, pl.ds(i * n, n)] for i in range(2)]

    sum_w = WeightSum(lambda d, yy, first=False: dot_tn(own_h[d * 2 + yy], gu[...]), "ww", s.grad_w, *room(4, width))

    def half_phases():
        for i in range(NP):
            agg_forward(i)
            if i > 0:
                make_gu(i - 1)
                agg_first(i - 1)
            agg_finish(i)
            make_u(i)
            if i > 0:
                agg_second(i - 1)
                agg_third(i - 1)
        make_gu(NP - 1)
        agg_first(NP - 1)
        agg_second(NP - 1)
        agg_third(NP - 1)

    half_phases()

    def give(n):
        src, dst = ((gu2, gu.at[own_half]), (s.emb2, s.embeddings.at[own_half]))[n]
        return rdma(src, dst, s.give_ss.at[n], s.give_rs.at[n], xp)

    def give_back(n):
        ref = (gu, s.embeddings)[n].at[their_half]
        return rdma(ref, ref, s.give_ss.at[n], s.give_rs.at[n], xp)

    give(0).start()
    rest_start()
    give(1).start()
    def arrived_x(i, h):
        arrived(grad_agg.at[(1 - x) * NP + i, part_c(h)], sa_rs.at[2 + h, i])

    for i in range(NP - 1):
        for h in range(2):
            arrived_x(i, h)
            agg_over_y((1 - x) * NP + i, (h,))

    def gradients_here(h):
        arrived_x(NP - 1, h)
        for i in range(2 * NP):
            arrived(grad_agg2.at[i, part_c(h)], s.gy_rs.at[h, i])

    def sent_messages(q):
        @pl.when(z < 3)
        def _():
            sent(block(z, y, q), s.up_ss.at[z, q])

        @pl.when(z > 0)
        def _():
            sent(block(z, y, q), s.down_ss.at[z, q])

        for t in range(1, 4):
            @pl.when((z - t >= 0) & (z < 3))
            def _():
                sent(block(z, y, q), s.up_ss.at[z - t, q])

            @pl.when((z + t <= 3) & (z > 0))
            def _():
                sent(block(z, y, q), s.down_ss.at[z + t, q])

        for zb in range(4):
            @pl.when((zb != zx) | ((inner == 0) & (q < NQ // 2)))
            def _():
                sent(block(z, y, q), s.y_ss.at[zb, q])

        @pl.when((inner == 0) | (q >= NQ // 2))
        def _():
            sent(block(z, y, q), s.zx_ss.at[q])

    loop(NQ, sent_messages)

    zsend, zrecv = message, s.zrecv
    m_zs, m_zr = s.m_zs, s.m_zr
    adjust = (0, 0, -1, 1)

    def dest(j):
        base = 3 - j + inner * adjust[j]
        return base + upper * (3 - 2 * base)

    each = 2 * NP // NQ

    def sum_of(terms):
        total = None
        for term in terms:
            total = term if total is None else total + term
        return total

    def spread(d, q, c0=0, nc=width):
        own, other = (d * 2 + y) * NQ + q, d * NQ + q
        n = sub
        return sum_of(
            dot(ref[m, c0 : c0 + nc], tab[b, m * n : (m + 1) * n])
            for ref, tab, b in ((grad_agg, table, own), (grad_agg2, table2, other))
            for m in range(2 * NP)
        )

    small = s.small

    def column_sums(i, ref):
        small[r, i : i + 1] = dot(jnp.ones((16, rows), BF), ref[...])[0:1]

    m_hs, m_hr = s.m_hs, s.m_hr

    def target(j):
        d = dest(j)
        step = 1 - 2 * upper
        if j == 2:
            step = step * (1 - 2 * inner)
        is_dest = (0, inner, 1)[j]
        slot = d + is_dest * ((1 - step) // 2) * (4 - d)
        return d, slot, ((z + step) * 2 + y, c)

    def along_half(q, h):
        d, slot, dev = target(0)
        lines = part_c(h)
        own = spread(d, q, h * (width // 2), width // 2)

        @pl.when(inner == 0)
        def _():
            zsend[d, q, lines] = own.astype(BF)

        @pl.when(inner == 1)
        def _():
            arrived(zrecv.at[d, q, lines], m_hr.at[d, h, q])
            zsend[d, q, lines] = (own + zrecv[d, q, lines].astype(F32)).astype(BF)

        rdma(
            zsend.at[d, q, lines], zrecv.at[slot, q, lines], m_hs.at[h, q], m_hr.at[slot, h, q], dev
        ).start()

    def along(j, q):
        d, slot, dev = target(j)
        own = spread(d, q)

        @pl.when(inner == 0)
        def _():
            zsend[d, q] = own.astype(BF)

        @pl.when(inner == 1)
        def _():
            if j == 1:
                arrived(zrecv.at[d, q], m_zr.at[d, q])
            else:
                for h in range(2):
                    arrived(zrecv.at[d, q, part_c(h)], m_hr.at[d, h, q])
            zsend[d, q] = (own + zrecv[d, q].astype(F32)).astype(BF)

        rdma(zsend.at[d, q], zrecv.at[slot, q], m_zs.at[d, q], m_zr.at[slot, q], dev).start()

    for h in range(2):
        gradients_here(h)
        loop(NQ, lambda q, h=h: along_half(q, h))
        if h == 0:

            @pl.when(inner == 1)
            def _():
                give_back(0).wait_recv()
                sum_w.first(0, 2)

    @pl.when(inner == 0)
    def _():
        for j in (1, 2):
            loop(NQ, lambda q, j=j: along(j, q))
        give_back(0).wait_recv()
        sum_w.first(0, 2)

    rest_forward()
    rest_finish()
    sum_w.first(2, 2)
    column_sums(2, gu)

    @pl.when(inner == 1)
    def _():
        def both_ways(q):
            along(2, q)
            along(1, q)

        loop(NQ, both_ways)

    give_back(1).wait_recv()
    store(0, 0, s.embeddings, s.embeddings_out).start()

    total_t = s.total_t

    def make_gv(q):
        total_t[...] = spread(z, q)

        @pl.when(z > 0)
        def _():
            arrived(zrecv.at[z, q], m_zr.at[z, q])
            total_t[...] += zrecv[z, q].astype(F32)

        @pl.when(z < 3)
        def _():
            arrived(zrecv.at[4, q], m_zr.at[4, q])
            total_t[...] += zrecv[4, q].astype(F32)

        v = v_pre[at(q)]
        sig = jax.nn.sigmoid(v)
        gv[at(q)] = (total_t[...].T * (sig * (1.0 + v * (1.0 - sig)))).astype(BF)

    def h_part(col, q):
        lines = pl.ds(pl.multiple_of(col * width, width), width)
        return dot_nt(gu[at(q)], s.w_w[lines, :]) + dot_nt(gv[at(q)], s.q_w[lines, :])

    def b_part(col, q):
        lines = pl.ds(pl.multiple_of(col * bwidth, bwidth), bwidth)
        return dot_nt(gb[at(q)], s.proj_w[lines, :])

    scatter_h, scatter_b = Scatter(h_part, "sh"), Scatter(b_part, "sb")


    def q_part(d, yy, first=False):
        n = width // 2
        keep = u_pre.at[0, pl.ds(d * n, n)]
        if not first:
            return keep[...]
        both = dot_tn(own_h[d], gv[...])
        keep[...] = jnp.where(y == 0, both[:n], both[n:])
        return jnp.where(y == 0, both[n:], both[:n])

    sum_q = PairSum(q_part, "wq", s.grad_q, *room_narrow(6, width // 2))
    small_ss, small_rs = s.small_ss, s.small_rs

    def so_far(d):
        return u_pre.at[1, pl.ds(d * bwidth, bwidth)]

    def add_proj(q):
        for d in range(4):
            got = dot_tn(boards[d, at(q)], gb[at(q)])

            @pl.when(q == 0)
            def _():
                so_far(d)[...] = got

            @pl.when(q > 0)
            def _():
                so_far(d)[...] += got

    def proj_part(d, yy, first=False):
        last = slice((NQ - 1) * chunk, NQ * chunk)
        n = bwidth // 2
        both = so_far(d)[...]
        if first:
            both = both + dot_tn(boards[d, last], gb[last])
            so_far(d)[...] = both
            return jnp.where(y == 0, both[n:], both[:n])
        return jnp.where(y == 0, both[:n], both[n:])

    sum_p = WeightSum(proj_part, "wp", s.grad_p, *room_narrow(7, bwidth // 2))

    def send_small():
        column_sums(0, gb)
        for d in range(1, 8):
            rdma(
                small.at[r], small.at[r], small_ss.at[d - 1], small_rs.at[r], ((r + d) % 8, c)
            ).start()

    def finish_board(q):
        s.grad_board[at(q)] = scatter_b.third(q)
        store(2, q, s.grad_board.at[at(q)], s.grad_board_out.at[at(q)]).start()

    def fourth_phase(t):
        @pl.when(t < NQ)
        def _():
            make_gv(t)
            scatter_h.first(t)

        @pl.when((t >= 3) & (t < NQ + 2))
        def _():
            scatter_b.second(t - 3)

        @pl.when(t == NQ - 1)
        def _():
            scatter_h.second(t)
            sum_q.first()

        @pl.when((t >= 2) & (t < NQ + 2))
        def _():
            q = t - 2
            g = scatter_h.third(q)
            m = mask_of(q)
            gb[at(q)] = jnp.where(m, g, 0.0).astype(BF)
            s.grad_pin[at(q)] = jnp.where(m, 0.0, g)

            @pl.when(t == NQ + 1)
            def _():
                sum_p.first()
                sum_q.second()

            scatter_b.first(q)
            store(1, q, s.grad_pin.at[at(q)], s.grad_pin_out.at[at(q)]).start()

        @pl.when(t < NQ - 1)
        def _():
            scatter_h.second(t)


        @pl.when((t >= 2) & (t <= NQ))
        def _():
            add_proj(t - 2)

    sum_w.second()
    for t in range(NQ + 2):
        fourth_phase(t)
    scatter_b.second(NQ - 1)
    column_sums(1, gv)
    send_small()
    for q in range(NQ - 1):
        finish_board(q)
    def drain_early(q):
        gather_b.drain(q)
        gather_h.drain(q)
        scatter_h.drain(q)
        for d in range(4):

            @pl.when((d != z) & (d != dest(0)))
            def _():
                sent(zsend.at[d, q], m_zs.at[d, q])

    loop(NQ, drain_early)

    def drain_half(i):
        for n in range(3):
            sent(agg_ref(c, mine(i)), ga_ss.at[n, i])
        for n in range(2):
            sent(sa_send.at[n, i], sa_ss.at[n, i])
        for h in range(2):
            sent(sa_x.at[i, part_c(h)], sa_ss.at[2 + h, i])
        sent(stat.at[0, i], stat_ss.at[i])

    loop(NP, drain_half)
    for n in range(3):
        sent(agg_ref(c, own_half), ga_ss.at[n, NP])
    for n in range(4):
        lend(n).wait_send()
    for n in range(2):
        lend_list(n).wait_send()
    for h in range(2):
        loop(2 * NP, lambda i, h=h: sent(grad_agg.at[i, part_c(h)], s.gy_ss.at[h, i]))
        loop(NQ, lambda q, h=h: sent(zsend.at[dest(0), q, part_c(h)], m_hs.at[h, q]))
    for n in range(2):
        give(n).wait_send()

    sum_w.third()
    sum_w.drain()
    store(0, 1, s.grad_w, s.grad_w_out).start()
    sum_p.second()
    sum_q.across()
    finish_board(NQ - 1)
    sum_q.third()
    store(0, 2, s.grad_q, s.grad_q_out).start()
    for d in range(1, 8):
        other = (r + d) % 8
        arrived(small.at[other], small_rs.at[other])
    total = small[0]
    for i in range(1, 8):
        total = total + small[i]
    nodes = rows * 8
    per = jnp.concatenate(
        [jnp.full((1, 128), 1.0 / nodes, F32), jnp.full((1, 128), 1.0 / (nodes * SLOTS), F32)], axis=1
    )
    s.sums[...] = total
    s.sums[3:4] = total[3:4] * per
    store(0, 3, s.sums, s.sums_out).start()
    sum_p.third()
    store(3, 0, s.grad_p, s.grad_p_out).start()

    def drain(q):
        scatter_b.drain(q)
        store(1, q, s.grad_pin.at[at(q)], s.grad_pin_out.at[at(q)]).wait()
        store(2, q, s.grad_board.at[at(q)], s.grad_board_out.at[at(q)]).wait()

    loop(NQ, drain)
    sum_q.drain()
    sum_p.drain()
    for d in range(7):
        sent(small.at[r], small_ss.at[d])
    for i, (n, name) in enumerate(
        ((0, "embeddings"), (0, "grad_w"), (0, "grad_q"), (0, "sums"), (3, "grad_p"))
    ):
        store(n, i % 4, getattr(s, name), getattr(s, name + "_out")).wait()


def finish_kernel(*refs):
    ins, sums, outs, small, held, sem = refs[:6], refs[6], refs[7:13], refs[13:18], refs[18:24], refs[24]
    first = [pltpu.make_async_copy(a, b, sem.at[0, i]) for i, (a, b) in enumerate(zip(ins, held))]
    second = [pltpu.make_async_copy(a, b, sem.at[1, i]) for i, (a, b) in enumerate(zip(held, outs))]
    for copy in first:
        copy.start()
    for i in range(3):
        small[i][...] = sums[i : i + 1]
    small[3][...] = sums[3:4, 0:1]
    small[4][...] = sums[3:4, 128:129]
    for a, b in zip(first, second):
        a.wait()
        b.start()
    for copy in second:
        copy.wait()


def fused_device(
    pin, board, is_board, neighbours, present, importance, proj_w, proj_b, q_w, q_b, w_w, w_b, cotangent
):
    rows, width = pin.shape
    bwidth = board.shape[1]
    chunk = rows // NQ
    nodes = rows * 8
    inputs = dict(
        board=board,
        is_board=is_board.reshape(rows // 128, 128),
        proj_w=proj_w,
        proj_b=proj_b.reshape(1, width),
        pin=pin,
        neighbours=neighbours.T,
        present=present.T,
        importance=importance.T,
        q_w=q_w,
        q_b=q_b.reshape(1, width),
        w_w=w_w,
        w_b=w_b.reshape(1, width),
        cotangent=cotangent,
    )
    shape = jax.ShapeDtypeStruct
    outs = dict(
        embeddings=shape((rows, width), BF),
        grad_pin=shape((rows, width), F32),
        grad_board=shape((rows, bwidth), F32),
        grad_p=shape((bwidth * 4 // 8, width), F32),
        grad_q=shape((width * 4 // 8, width), F32),
        grad_w=shape((2 * width * 4 // 8, width), F32),
        sums=shape((8, width), F32),
    )
    vmem, dma = pltpu.VMEM, pltpu.SemaphoreType.DMA
    scratch = dict(
        in_sem=dma((len(inputs),)),
        out_sem=dma((4, NQ)),
        flags=vmem((rows // 128, 128), jnp.int32),
        numbers=vmem((SLOTS, rows), jnp.int32),
        numbers2=vmem((SLOTS, rows), jnp.int32),
        alpha=vmem((64, rows), BF),
        alpha2=vmem((64, rows), BF),
        padded=vmem((64, rows), F32),
        table2=vmem((nodes // 2 // chunk, rows, chunk), BF),
        high2=vmem((2, rows // 4, 128), F32),
        low2=vmem((2, rows // 4, 128), F32),
        weight2=vmem((2, rows // 4, 128), F32),
        grad_agg2=vmem((2 * NP, width, rows // 2 // NP), BF),
        table=vmem((nodes // chunk, rows, chunk), BF),
        stage=vmem((64 * (PIECE + 8), 128), F32),
        high=vmem((2, rows // 4, 128), F32),
        low=vmem((2, rows // 4, 128), F32),
        weight=vmem((2, rows // 4, 128), F32),
        mask=vmem((rows, 128), F32),
        boards=vmem((4, rows, bwidth), BF),
        ha=vmem((8, rows, width), BF),
        message=vmem((8, NQ, chunk, width), BF),
        v_pre=vmem((rows, width), F32),
        u_pre=vmem((2, rows // 2, width), F32),
        w2=vmem(w_w.shape, BF),
        w_b2=vmem((1, width), F32),
        cotangent2=vmem((rows // 2, width), BF),
        gu2=vmem((rows // 2, width), BF),
        emb2=vmem((rows // 2, width), BF),
        sa_send=vmem((2, NP, rows // 2 // NP, width), BF),
        sa_recv=vmem((2, NP, rows // 2 // NP, width), BF),
        sa_x=vmem((NP, width, rows // 2 // NP), BF),
        sa_ss=dma((4, NP)),
        sa_rs=dma((4, NP)),
        ga_ss=dma((3, NP + 1)),
        ga_rs=dma((3, NP + 1)),
        lend_ss=dma((4,)),
        lend_rs=dma((4,)),
        give_ss=dma((2,)),
        give_rs=dma((2,)),
        gu=vmem((rows, width), BF),
        gv=vmem((rows, width), BF),
        gb=vmem((rows, width), BF),
        grad_agg=vmem((2 * NP, width, rows // 2 // NP), BF),
        stat=vmem((2, NP, 8, 128), F32),
        small=vmem((8, 8, width), F32),
        zrecv=vmem((5, NQ, width, chunk), BF),
        total_t=vmem((width, chunk), F32),
        stat_ss=dma((NP,)),
        stat_rs=dma((NP,)),
        msg_rs=dma((8, NQ)),
        up_ss=dma((4, NQ)),
        down_ss=dma((4, NQ)),
        y_ss=dma((4, NQ)),
        zx_ss=dma((NQ,)),
        m_zs=dma((4, NQ)),
        m_zr=dma((5, NQ)),
        list_ss=dma((2,)),
        list_rs=dma((2,)),
        gy_ss=dma((2, 2 * NP)),
        gy_rs=dma((2, 2 * NP)),
        m_hs=dma((2, NQ)),
        m_hr=dma((4, 2, NQ)),
        small_ss=dma((7,)),
        small_rs=dma((8,)),
    )
    for name in ("present", "importance", "proj_w", "proj_b", "pin", "q_w", "q_b", "w_w", "w_b", "cotangent"):
        scratch[name] = vmem(inputs[name].shape, inputs[name].dtype)
    for name, out in outs.items():
        scratch[name] = vmem(out.shape, out.dtype)
    for name in ("gb", "gh"):
        scratch[name + "_ss"] = dma((3, NQ))
        scratch[name + "_rs"] = dma((3, NQ))
    for name, w in (("sh", width), ("sb", bwidth)):
        scratch[name + "_send1"] = vmem((2, NQ, chunk, w), BF)
        scratch[name + "_recv1"] = vmem((2, NQ, chunk, w), BF)
        scratch[name + "_sendx"] = vmem((NQ, chunk, w), BF)
        scratch[name + "_recvx"] = vmem((NQ, chunk, w), BF)
        scratch[name + "_ss"] = dma((3, NQ))
        scratch[name + "_rs"] = dma((3, NQ))
    for name, n in (("ww", width), ("wq", width // 2), ("wp", bwidth // 2)):
        for part in ("_yrecv", "_zrecv"):
            scratch[name + part] = vmem((4, n, width), BF)
        scratch[name + "_ss"] = dma((2, 4))
        scratch[name + "_rs"] = dma((2, 4))
    place = pl.BlockSpec(memory_space=pl.ANY)
    whole = pl.BlockSpec(memory_space=pltpu.VMEM)
    names = [n + "_in" for n in inputs] + [n + "_out" for n in outs] + list(scratch)
    got = pl.pallas_call(
        functools.partial(fused_kernel, names=tuple(names)),
        out_shape=list(outs.values()),
        in_specs=[place] * len(inputs),
        out_specs=[place] * len(outs),
        scratch_shapes=list(scratch.values()),
        compiler_params=pltpu.CompilerParams(
            collective_id=1, has_side_effects=True, vmem_limit_bytes=63 << 20
        ),
        cost_estimate=pl.CostEstimate(flops=14 << 30, bytes_accessed=8 << 20, transcendentals=0),
    )(*inputs.values())
    row, one = shape((1, width), F32), shape((1, 1), F32)
    emb, g_pin, g_board, g_proj, g_q, g_w, p_b, q_bias, w_bias, count, weight = pl.pallas_call(
        finish_kernel,
        out_shape=list(outs.values())[:6] + [row, row, row, one, one],
        in_specs=[place] * 6 + [whole],
        out_specs=[place] * 6 + [whole] * 5,
        scratch_shapes=[vmem(out.shape, out.dtype) for out in list(outs.values())[:6]] + [dma((2, 6))],
        cost_estimate=pl.CostEstimate(flops=0, bytes_accessed=5 << 20, transcendentals=0),
    )(*got)
    return (
        emb,
        g_pin,
        g_board,
        g_proj,
        p_b.reshape(width),
        g_q,
        q_bias.reshape(width),
        g_w,
        w_bias.reshape(width),
        count.reshape(()),
        weight.reshape(()),
    )


def silu_slope(value):
    sig = jax.nn.sigmoid(value)
    return sig * (1.0 + value * (1.0 - sig))


def slot_table(nbr_block, alpha_block, start, width):
    offsets = nbr_block - start
    places = lax.broadcasted_iota(jnp.int32, (1, 1, width), 2)
    return jnp.sum(jnp.where(offsets[:, :, None] == places, alpha_block[:, :, None], 0.0), axis=1)


def split_pair(table):
    upper = table.astype(jnp.bfloat16)
    lower = (table - upper.astype(jnp.float32)).astype(jnp.bfloat16)
    return (upper, lower)


def collect_rows(nbrs, alphas, table_all):
    total, columns = table_all.shape
    col_tile = math.gcd(total, 2048)
    count_tiles = total // col_tile
    tiles = table_all.reshape(count_tiles, col_tile, columns)
    rows = nbrs.shape[0]
    row_block = math.gcd(rows, 512)
    count_rows = rows // row_block

    def one_rows(pair):
        nbr_block, alpha_block = pair

        def step(acc, index):
            upper, lower = split_pair(
                slot_table(nbr_block, alpha_block, index * col_tile, col_tile)
            )
            piece = tiles[index]
            acc = acc + jnp.dot(upper, piece, preferred_element_type=jnp.float32)
            return (acc + jnp.dot(lower, piece, preferred_element_type=jnp.float32), None)

        acc, unused = lax.scan(
            step, jnp.zeros((row_block, columns), jnp.float32), jnp.arange(count_tiles)
        )
        return acc

    out = lax.map(
        one_rows,
        (nbrs.reshape(count_rows, row_block, -1), alphas.reshape(count_rows, row_block, -1)),
    )
    return out.reshape(rows, columns)


def spread_rows(grads, nbrs, alphas, base, width):
    rows, columns = grads.shape
    row_block = math.gcd(rows, 512)
    count_rows = rows // row_block
    col_tile = math.gcd(width, 2048)
    count_tiles = width // col_tile
    stacked = (
        grads.reshape(count_rows, row_block, columns),
        nbrs.reshape(count_rows, row_block, -1),
        alphas.reshape(count_rows, row_block, -1),
    )
    tdot = (((0,), (0,)), ((), ()))

    def one_tile(index):

        def step(acc, triple):
            grad_block, nbr_block, alpha_block = triple
            upper, lower = split_pair(
                slot_table(nbr_block, alpha_block, base + index * col_tile, col_tile)
            )
            acc = acc + lax.dot_general(upper, grad_block, tdot, preferred_element_type=jnp.float32)
            return (
                acc + lax.dot_general(lower, grad_block, tdot, preferred_element_type=jnp.float32),
                None,
            )

        acc, unused = lax.scan(step, jnp.zeros((col_tile, columns), jnp.float32), stacked)
        return acc

    out = lax.map(one_tile, jnp.arange(count_tiles))
    return out.reshape(width, columns)


def per_device(
    pin_features,
    board_features,
    is_board,
    neighbours,
    present,
    importance,
    proj_weight,
    proj_bias,
    q_weight,
    q_bias,
    w_weight,
    w_bias,
    cotangent,
):
    local_rows = pin_features.shape[0]
    width = q_weight.shape[0]
    filled = present.astype(jnp.float32) * importance
    alpha = filled / jnp.sum(filled, axis=1, keepdims=True)
    board_mask = (is_board == 1)[:, None]
    stat_terms = (jnp.sum(present.astype(jnp.float32)), jnp.sum(filled))
    stat_totals = lax.psum((stat_terms[0], stat_terms[1]), "rows")
    board_full = lax.all_gather(board_features, "cols", axis=1, tiled=True)
    board_proj = jnp.dot(board_full, proj_weight, preferred_element_type=jnp.float32) + proj_bias
    h_local = jnp.where(board_mask, board_proj, pin_features.astype(jnp.float32)).astype(
        jnp.bfloat16
    )
    h_full = lax.all_gather(h_local, "cols", axis=1, tiled=True)
    v_pre = jnp.dot(h_full, q_weight, preferred_element_type=jnp.float32) + q_bias
    message = jax.nn.silu(v_pre).astype(jnp.bfloat16)
    message_all = lax.all_gather(message, "rows", axis=0, tiled=True)
    agg_local = collect_rows(neighbours, alpha, message_all).astype(jnp.bfloat16)
    agg_full = lax.all_gather(agg_local, "cols", axis=1, tiled=True)
    w_self = w_weight[:width]
    w_agg = w_weight[width:]
    u_pre = (
        jnp.dot(h_full, w_self, preferred_element_type=jnp.float32)
        + jnp.dot(agg_full, w_agg, preferred_element_type=jnp.float32)
        + w_bias
    )
    z_act = jax.nn.silu(u_pre)
    squares = lax.psum(jnp.sum(z_act * z_act, axis=1), "cols")
    scale = lax.rsqrt(squares + 1e-06)[:, None]
    embeddings = (z_act * scale).astype(jnp.bfloat16)
    grad_out = cotangent.astype(jnp.float32)
    inner = lax.psum(jnp.sum(grad_out * z_act, axis=1), "cols")[:, None]
    grad_z = grad_out * scale - z_act * scale * scale * scale * inner
    grad_u = (grad_z * silu_slope(u_pre)).astype(jnp.bfloat16)
    agg_part = lax.dot_general(
        grad_u, w_agg, (((1,), (1,)), ((), ())), preferred_element_type=jnp.float32
    )
    grad_agg = lax.psum_scatter(agg_part, "cols", scatter_dimension=1, tiled=True).astype(
        jnp.bfloat16
    )
    table = spread_rows(grad_agg, neighbours, alpha, 0, message_all.shape[0])
    grad_message = lax.psum_scatter(
        table.astype(jnp.bfloat16), "rows", scatter_dimension=0, tiled=True
    ).astype(jnp.float32)
    grad_v = (grad_message * silu_slope(v_pre)).astype(jnp.bfloat16)
    h_part = lax.dot_general(
        grad_u, w_self, (((1,), (1,)), ((), ())), preferred_element_type=jnp.float32
    )
    h_part = h_part + lax.dot_general(
        grad_v, q_weight, (((1,), (1,)), ((), ())), preferred_element_type=jnp.float32
    )
    grad_h = lax.psum_scatter(
        h_part.astype(jnp.bfloat16), "cols", scatter_dimension=1, tiled=True
    ).astype(jnp.float32)
    grad_pin = jnp.where(board_mask, 0.0, grad_h)
    grad_hb = jnp.where(board_mask, grad_h, 0.0).astype(jnp.bfloat16)
    board_part = lax.dot_general(
        grad_hb, proj_weight, (((1,), (1,)), ((), ())), preferred_element_type=jnp.float32
    )
    grad_board = lax.psum_scatter(
        board_part.astype(jnp.bfloat16), "cols", scatter_dimension=1, tiled=True
    ).astype(jnp.float32)
    tdot = (((0,), (0,)), ((), ()))
    grad_w_local = jnp.concatenate(
        [
            lax.dot_general(h_full, grad_u, tdot, preferred_element_type=jnp.float32),
            lax.dot_general(agg_full, grad_u, tdot, preferred_element_type=jnp.float32),
        ],
        axis=0,
    )
    grad_q_local = lax.dot_general(h_full, grad_v, tdot, preferred_element_type=jnp.float32)
    grad_p_local = lax.dot_general(board_full, grad_hb, tdot, preferred_element_type=jnp.float32)
    grad_w, grad_q, grad_proj = (
        lax.psum_scatter(
            grad_w_local.astype(jnp.bfloat16), "rows", scatter_dimension=0, tiled=True
        ).astype(jnp.float32),
        lax.psum_scatter(
            grad_q_local.astype(jnp.bfloat16), "rows", scatter_dimension=0, tiled=True
        ).astype(jnp.float32),
        lax.psum_scatter(
            grad_p_local.astype(jnp.bfloat16), "rows", scatter_dimension=0, tiled=True
        ).astype(jnp.float32),
    )
    bias_terms = (
        jnp.sum(grad_hb.astype(jnp.float32), axis=0),
        jnp.sum(grad_v.astype(jnp.float32), axis=0),
        jnp.sum(grad_u.astype(jnp.float32), axis=0),
    )
    grad_pb, grad_qb, grad_wb = lax.psum((bias_terms[0], bias_terms[1], bias_terms[2]), "rows")
    all_nodes = local_rows * lax.axis_size("rows")
    mean_count = stat_totals[0] / all_nodes
    mean_weight = stat_totals[1] / (all_nodes * SLOTS)
    return (
        embeddings,
        grad_pin,
        grad_board,
        grad_proj,
        grad_pb,
        grad_q,
        grad_qb,
        grad_w,
        grad_wb,
        mean_count,
        mean_weight,
    )


def solution(mesh):
    in_specs = (
        P("rows", "cols"),
        P("rows", "cols"),
        P("rows"),
        P("rows", None),
        P("rows", None),
        P("rows", None),
        P(None, "cols"),
        P("cols"),
        P(None, "cols"),
        P("cols"),
        P(None, "cols"),
        P("cols"),
        P("rows", "cols"),
    )
    out_specs = (
        P("rows", "cols"),
        P("rows", "cols"),
        P("rows", "cols"),
        P("rows", "cols"),
        P("cols"),
        P("rows", "cols"),
        P("cols"),
        P("rows", "cols"),
        P("cols"),
        P(),
        P(),
    )
    fused = mesh.shape["rows"] == 8 and mesh.shape["cols"] == 4
    return jax.shard_map(
        fused_device if fused else per_device, mesh=mesh, in_specs=in_specs, out_specs=out_specs, check_vma=False
    )
```
